32 devices in a mesh: fsdp: 4 (over z), ctx: 4 (over y, x), tp: 2 (over core).
Axes of the slice: x: 2, y: 2, z: 4, core: 2. Of those that a mesh axis runs over, the one named last changes fastest.
Arguments:
- tokens: bfloat16 [2, 2048, 1792], P(None, ('fsdp', 'ctx')), may hold values from -6 to 6
- cotangent: bfloat16 [2, 2048, 1792], P(None, ('fsdp', 'ctx')), may hold values from -6 to 6
- attn_in: bfloat16 [3, 1792, 1792], P(None, 'fsdp', 'tp'), may hold values from -0.125 to 0.125
- attn_out: bfloat16 [1792, 1792], P('tp', 'fsdp'), may hold values from -1 to 1
- gate_up: bfloat16 [2, 1792, 4864], P(None, 'fsdp', 'tp'), may hold values from -0.125 to 0.125
- down_proj: bfloat16 [4864, 1792], P('tp', 'fsdp'), may hold values from -0.078125 to 0.078125
- conv_weight: bfloat16 [2, 3, 896], P('tp', None, 'fsdp'), may hold values from -3 to 3
- norm_gains: bfloat16 [2, 1792], P(None, 'fsdp'), may hold values from 0.5 to 1.5
- deal_order: int32 [2, 2048], P(None, ('fsdp', 'ctx')), may hold values from 0 to 2047, as said below
- lengths: int32 [2, 4, 3], P(None, 'fsdp'), may hold values from 1 to 416, 512 in all within a row
Outputs:
- activations: bfloat16 [2, 2048, 1792], P(None, ('fsdp', 'ctx'))
- input_grad: bfloat16 [2, 2048, 1792], P(None, ('fsdp', 'ctx'))
- grad_attn_in: float32 [3, 1792, 1792], P(None, 'fsdp', 'tp')
- grad_attn_out: float32 [1792, 1792], P('tp', 'fsdp')
- grad_gate_up: float32 [2, 1792, 4864], P(None, 'fsdp', 'tp')
- grad_down: float32 [4864, 1792], P('tp', 'fsdp')
- grad_conv: float32 [2, 3, 896], P('tp', None, 'fsdp')
- grad_gains: float32 [2, 1792], P(None, 'fsdp')
The draws below stay inside these ranges and needn't reach their ends.
Inputs may be any that keep to these rules, and one draw needn't show every extreme that they name: Each row of deal_order is a permutation of the 2048 tokens; the 128 rows that each device of fsdp and ctx holds in the dealt layout take exactly 8 tokens from each device's block of 128 rows of the given order.
All inputs are finite; a program needn't handle non-finite values.
Results may differ from the reference program's by a relative error of at most 0.014.
Values may be sent and summed in bfloat16 or wider, within the bound.
No kernel may reach another device: no remote copies, remote signals or barrier semaphores. Data moves between devices by JAX's collectives and lax.ppermute only.
A program may use at most 320 MiB of HBM per device.

```python
import math
from functools import partial
import jax
import jax.numpy as jnp
import numpy as np
from jax import lax

D = 1792
HEADS = 28
HEAD = 64
FF = 4864
WINDOW = 64
CONV = 3
TOK_DEV = 128
BATCHES = 2
SEQS = 3
TOKENS = 2048
GROUP = 512
MOST = 416
N_FSDP = 4
N_TP = 2


def shuffle(row_key):
    return jax.random.permutation(row_key, TOK_DEV).astype(jnp.int32)


def one_batch(batch_key):
    workers = TOKENS // TOK_DEV
    slots_each = TOK_DEV // workers
    send_key, take_key = jax.random.split(batch_key)
    sending = jax.vmap(shuffle)(jax.random.split(send_key, workers))
    giver = (jnp.arange(workers, dtype=jnp.int32)[:, None] * TOK_DEV + sending).reshape(workers, workers, slots_each)
    incoming = jnp.transpose(giver, (1, 0, 2)).reshape(workers, TOK_DEV)
    taking = jax.vmap(shuffle)(jax.random.split(take_key, workers))
    back_index = jnp.argsort(taking, axis=1).astype(jnp.int32)
    return jnp.take_along_axis(incoming, back_index, axis=1).reshape(TOKENS)


def draw_deal_order(key, part):
    key = jax.random.fold_in(key, 11)
    return jax.vmap(one_batch)(jax.random.split(key, BATCHES)).astype(jnp.int32)


def level_of(stream_key, shape, cuts, low, high):
    def one(dim, blocks):
        draws = jax.random.uniform(jax.random.fold_in(jax.random.fold_in(stream_key, 6), dim), (blocks,), jnp.float32, low / len(cuts), high / len(cuts))
        return jnp.repeat(jnp.exp(draws), shape[dim] // blocks).reshape((-1,) + (1,) * (len(shape) - dim - 1))

    level = one(*cuts[0])
    for cut in cuts[1:]:
        level = level * one(*cut)
    return level


def length_profile(amount, total, most, slope):
    weights = [(1 << 20) // math.isqrt(standing ** slope) + 1 for standing in range(2, amount + 1)]
    surplus, holding = total - most - (amount - 1), [1] * (amount - 1)
    while surplus > 0:
        candidates = [i for i in range(amount - 1) if holding[i] < most]
        pool, budget = sum([weights[i] for i in candidates]), surplus
        for i in candidates:
            extra = min(most - holding[i], max(1, budget * weights[i] // pool), surplus)
            holding[i] = holding[i] + extra
            surplus = surplus - extra
    return np.array([most] + holding)


def uneven(own_key, number_of, total, bound, lean):
    if number_of == 2:
        one = jax.random.randint(own_key, (), max(1, total - bound), min(bound, total - 1) + 1)
        return jnp.stack([one, total - one])
    sizes = jnp.asarray(length_profile(number_of, total, bound, lean), jnp.int32)
    couples = (number_of - 1) // 2
    giver, sink = sizes[1:1 + 2 * couples:2], sizes[2:2 + 2 * couples:2]
    slack = jnp.minimum(giver - 1, bound - sink)
    passed = jax.random.randint(jax.random.fold_in(own_key, 1), (couples,), 0, 1 << 20) % (slack + 1)
    sizes = sizes.at[1:1 + 2 * couples:2].set(giver - passed).at[2:2 + 2 * couples:2].set(sink + passed)
    return sizes[jax.random.permutation(jax.random.fold_in(own_key, 2), number_of)]


def scatter_about(stream_key, extent, spread, limit, pieces=(), kind=jnp.bfloat16):
    array = spread * jax.random.normal(stream_key, extent, jnp.float32)
    if pieces:
        array = array * level_of(stream_key, extent, pieces, -0.22, 0.18)
    return jnp.clip(array, -limit, limit).astype(kind)


def setup_inputs(seed: int = 0) -> dict:
    arg_keys = jax.random.split(jax.random.key(seed), 11)
    return {
        "tokens": scatter_about(arg_keys[0], (BATCHES, TOKENS, D), 1.0, 6.0, ((1, 16),)),
        "cotangent": scatter_about(arg_keys[1], (BATCHES, TOKENS, D), 1.0, 6.0, ((1, 16),)),
        "attn_in": scatter_about(arg_keys[2], (3, D, D), D ** -0.5, 0.125, ((1, 4), (2, 2))),
        "attn_out": scatter_about(arg_keys[3], (D, D), (D // WINDOW) ** -0.5, 1.0, ((0, 2), (1, 4))),
        "gate_up": scatter_about(arg_keys[4], (2, D, FF), D ** -0.5, 0.125, ((1, 4), (2, 2))),
        "down_proj": scatter_about(arg_keys[5], (FF, D), FF ** -0.5, 0.078125, ((0, 2), (1, 4))),
        "conv_weight": scatter_about(arg_keys[6], (N_TP, CONV, D // N_TP), 0.7, 3.0, ((0, 2), (2, 4))),
        "norm_gains": jnp.clip(1.0 + 0.1 * jax.random.normal(arg_keys[7], (2, D), jnp.float32), 0.5, 1.5).astype(jnp.bfloat16),
        "deal_order": draw_deal_order(jax.random.fold_in(arg_keys[10], 71), 0),
        "lengths": jax.vmap(lambda own: uneven(own, SEQS, GROUP, MOST, 2))(jax.random.split(arg_keys[9], BATCHES * N_FSDP)).reshape((BATCHES, N_FSDP, SEQS)).astype(jnp.int32),
    }


@jax.custom_vjp
def low(v):
    return lax.optimization_barrier(v.astype(jnp.bfloat16)).astype(jnp.float32)

@jax.custom_vjp
def low_back(v):
    return v

def low_keep(v):
    return (low(v), None)

def low_pass(kept, grad):
    return (grad,)

def back_keep(v):
    return (v, None)

def back_low(kept, grad):
    return (low(grad),)
low.defvjp(low_keep, low_pass)
low_back.defvjp(back_keep, back_low)
epsilon = 1e-06
masked_score = -1e+30

def product(left, right):
    return jnp.dot(left, right, precision=lax.Precision.HIGHEST)

def rms_scale(values, gain):
    return values * lax.rsqrt(lax.optimization_barrier(jnp.mean(values * values, axis=-1, keepdims=True)) + epsilon) * gain

def segment_ids(lengths_row):
    seq_ends = jnp.cumsum(lengths_row).astype(jnp.int32)
    places = jnp.arange(GROUP, dtype=jnp.int32)
    return lax.optimization_barrier(jnp.sum((places[:, None] >= seq_ends[None, :]).astype(jnp.int32), axis=1)).astype(jnp.int32)

def window_block(tensors, block_start):
    queries, keys_pad, values_pad, seg_query_all, seg_pad = tensors
    block_rows = GROUP // 2
    key_span = block_rows + WINDOW - 1
    query_part = lax.dynamic_slice_in_dim(queries, block_start, block_rows, 0)
    key_part = lax.dynamic_slice_in_dim(keys_pad, block_start, key_span, 0)
    value_part = lax.dynamic_slice_in_dim(values_pad, block_start, key_span, 0)
    seg_query = lax.dynamic_slice_in_dim(seg_query_all, block_start, block_rows, 0)
    seg_key = lax.dynamic_slice_in_dim(seg_pad, block_start, key_span, 0)
    query_pos = block_start + jnp.arange(block_rows, dtype=jnp.int32)
    key_pos = block_start - (WINDOW - 1) + jnp.arange(key_span, dtype=jnp.int32)
    allowed = (seg_key[None, :] == seg_query[:, None]) & (key_pos[None, :] <= query_pos[:, None]) & (key_pos[None, :] > query_pos[:, None] - WINDOW)
    heads_q = query_part.reshape(block_rows, HEADS, HEAD)
    heads_k = key_part.reshape(key_span, HEADS, HEAD)
    heads_v = value_part.reshape(key_span, HEADS, HEAD)
    scaling = 1.0 / math.sqrt(HEAD)
    scores = low_back(jnp.einsum('qhd,khd->hqk', heads_q, heads_k, precision=lax.Precision.HIGHEST) * scaling)
    scores = jnp.where(allowed[None], scores, masked_score)
    shifted = scores - lax.optimization_barrier(jnp.max(scores, axis=-1, keepdims=True))
    weights = jnp.exp(shifted)
    weights = weights / lax.optimization_barrier(jnp.sum(weights, axis=-1, keepdims=True))
    blended = jnp.einsum('hqk,khd->qhd', low(weights), heads_v, precision=lax.Precision.HIGHEST)
    return blended.reshape(block_rows, HEADS * HEAD)

def group_layer(params, group_pair):
    rows_in, seg_ids = group_pair
    attn_in, attn_out, gate_up, down_proj, conv_full, norm_gains = params
    hidden = low(rms_scale(rows_in, norm_gains[0]))
    queries = low(low_back(product(hidden, attn_in[0])))
    key_rows = low(low_back(product(hidden, attn_in[1])))
    values = low(low_back(product(hidden, attn_in[2])))
    seg_pad = jnp.concatenate([jnp.full((WINDOW - 1,), -1, jnp.int32), seg_ids])
    conv_seg = seg_pad[WINDOW - CONV:]
    value_pad = jnp.concatenate([jnp.zeros((CONV - 1, D), jnp.float32), values])
    conv_mix = jnp.zeros((GROUP, D), jnp.float32)
    for lag_step in range(CONV):
        offset = CONV - 1 - lag_step
        earlier = value_pad[offset:offset + GROUP]
        same_seq = conv_seg[offset:offset + GROUP] == seg_ids
        conv_mix = conv_mix + jnp.where(same_seq[:, None], earlier * conv_full[lag_step], 0.0)
    gated_vals = low(values * jax.nn.silu(conv_mix))
    keys_pad = jnp.concatenate([jnp.zeros((WINDOW - 1, D), jnp.float32), key_rows])
    gated_pad = jnp.concatenate([jnp.zeros((WINDOW - 1, D), jnp.float32), gated_vals])
    tensors = (queries, keys_pad, gated_pad, seg_ids, seg_pad)
    starts = jnp.arange(2, dtype=jnp.int32) * (GROUP // 2)
    blocks = lax.map(partial(jax.checkpoint(window_block), tensors), starts)
    attended = low(low_back(blocks.reshape(GROUP, D)))
    branch = low_back(product(attended, attn_out))
    resid = rows_in + branch
    hidden_two = low(rms_scale(resid, norm_gains[1]))
    gate_act = low_back(product(hidden_two, gate_up[0]))
    upper = low_back(product(hidden_two, gate_up[1]))
    inner_act = low(jax.nn.silu(gate_act) * upper)
    return resid + low_back(product(inner_act, down_proj))

def forward(deal_order, lengths, tokens, attn_in, attn_out, gate_up, down_proj, conv_weight, norm_gains):
    conv_full = jnp.transpose(conv_weight, (1, 0, 2)).reshape(CONV, D)
    params = (attn_in, attn_out, gate_up, down_proj, conv_full, norm_gains)
    group_fn = partial(jax.checkpoint(group_layer), params)
    results = []
    for batch_index in range(BATCHES):
        dealt_rows = tokens[batch_index][deal_order[batch_index]]
        seg_all = jax.vmap(segment_ids)(lengths[batch_index])
        outputs = lax.map(group_fn, (dealt_rows.reshape(N_FSDP, GROUP, D), seg_all))
        placed = jnp.zeros((TOKENS, D), jnp.float32).at[deal_order[batch_index]].set(outputs.reshape(TOKENS, D))
        results.append(placed)
    return jnp.stack(results)

def reference(tokens, cotangent, attn_in, attn_out, gate_up, down_proj, conv_weight, norm_gains, deal_order, lengths):
    floats = tuple((member.astype(jnp.float32) for member in (tokens, attn_in, attn_out, gate_up, down_proj, conv_weight, norm_gains)))
    outputs, pullback = jax.vjp(partial(forward, deal_order, lengths), *floats)
    gradients = pullback(cotangent.astype(jnp.float32))
    return (outputs.astype(jnp.bfloat16), gradients[0].astype(jnp.bfloat16), gradients[1], gradients[2], gradients[3], gradients[4], gradients[5], gradients[6])
```

```python
import math

import jax
import jax.numpy as jnp
from jax import lax
from jax.experimental import pallas as pl
from jax.experimental.pallas import tpu as pltpu
from jax.sharding import PartitionSpec as P

HEAD = 64
WINDOW = 64
CONV = 3
BATCHES = 2
BLOCK = 128
HEADS_EACH = 4

epsilon = 1e-06
masked_score = -1e30
f32 = jnp.float32
bf16 = jnp.bfloat16


def flipped(value, sizes, step):
    n_fsdp, n_ctx, n_tp = sizes
    pairs = []
    for f in range(n_fsdp):
        for c in range(n_ctx):
            for t in range(n_tp):
                if step == 2:
                    other = (c, t ^ 1)
                else:
                    other = (c ^ (1 if t == step else 2), t)
                pairs.append(((f * n_ctx + c) * n_tp + t, (f * n_ctx + other[0]) * n_tp + other[1]))
    return lax.ppermute(value, ("fsdp", "ctx", "tp"), pairs)


def plane_gather(own, sizes):
    one = flipped(own, sizes, 0)
    two = flipped(own, sizes, 1)
    three = flipped(one, sizes, 1)
    mine = [own, one, two, three]
    return jnp.concatenate(mine + [flipped(block, sizes, 2) for block in mine])


def plane_scatter(kept, sent, sizes):
    total = kept + flipped(sent.astype(bf16), sizes, 2).astype(f32)
    for step in (1, 0):
        half = total.shape[0] // 2
        total = total[:half] + flipped(total[half:].astype(bf16), sizes, step).astype(f32)
    return total


def product(left, right, dims, out_type=f32):
    return lax.dot_general(left, right, (dims, ((), ())), preferred_element_type=f32).astype(out_type)


NN = ((1,), (0,))
NT = ((1,), (1,))
TN = ((0,), (0,))


def seg_of(places, ends):
    return (places >= ends[0]).astype(jnp.int32) + (places >= ends[1]).astype(jnp.int32)


def conv_terms(values, conv, ends):
    rows = values.shape[0]
    places = lax.broadcasted_iota(jnp.int32, values.shape, 0)
    own_seg = seg_of(places, ends)
    shifted = [values]
    for lag in range(1, CONV):
        same = (places >= lag) & (seg_of(places - lag, ends) == own_seg)
        shifted.append(jnp.where(same, pltpu.roll(values, lag, 0), 0.0))
    mix = shifted[0] * conv[0:1]
    for lag in range(1, CONV):
        mix = mix + shifted[lag] * conv[lag : lag + 1]
    return shifted, mix


def block_mask(block, first, span, ends):
    query = block * BLOCK + lax.broadcasted_iota(jnp.int32, (BLOCK, span), 0)
    key = first * BLOCK + lax.broadcasted_iota(jnp.int32, (BLOCK, span), 1)
    return (seg_of(query, ends) == seg_of(key, ends)) & (key <= query) & (key > query - WINDOW)


def head_lanes(tile, head):
    lanes = lax.broadcasted_iota(jnp.int32, tile.shape, 1)
    return (lanes >= head * HEAD) & (lanes < (head + 1) * HEAD)


def window_weights(query, keys, allowed):
    scores = product(query, keys, NT) * (1.0 / math.sqrt(HEAD))
    scores = jnp.where(allowed, scores, masked_score)
    weights = jnp.exp(scores - jnp.max(scores, axis=-1, keepdims=True))
    return weights / jnp.sum(weights, axis=-1, keepdims=True)


def ends_of(lengths_ref, batch):
    first = lengths_ref[batch, 0]
    return (first, first + lengths_ref[batch, 1])


def attend_forward_kernel(lengths_ref, qkv_ref, conv_ref, out_ref, gated_ref):
    width = HEADS_EACH * HEAD
    group = qkv_ref.shape[0] // BATCHES
    conv = conv_ref[...]
    for batch in range(BATCHES):
        ends = ends_of(lengths_ref, batch)
        base = batch * group
        values = qkv_ref[base : base + group, 2 * width :].astype(f32)
        _, mix = conv_terms(values, conv, ends)
        gated_ref[...] = (values * (mix * jax.nn.sigmoid(mix))).astype(bf16)
        for block in range(group // BLOCK):
            first = max(block - 1, 0)
            span = (block + 1 - first) * BLOCK
            allowed = block_mask(block, first, span, ends)
            rows = slice(base + block * BLOCK, base + (block + 1) * BLOCK)
            for pair in range(width // 128):
                lanes = slice(pair * 128, (pair + 1) * 128)
                query = qkv_ref[rows, lanes]
                keys = qkv_ref[
                    base + first * BLOCK : base + first * BLOCK + span,
                    width + pair * 128 : width + (pair + 1) * 128,
                ]
                gated = gated_ref[first * BLOCK : first * BLOCK + span, lanes]
                blended = []
                for head in range(2):
                    chosen = jnp.where(head_lanes(query, head), query, jnp.zeros_like(query))
                    weights = window_weights(chosen, keys, allowed).astype(bf16)
                    blended.append(product(weights, gated, NN))
                merged = jnp.where(head_lanes(blended[0], 0), blended[0], blended[1])
                out_ref[rows, lanes] = merged.astype(bf16)


def attend_backward_kernel(
    lengths_ref, qkv_ref, grad_ref, conv_ref, out_ref, grad_conv_ref, gated_ref, keys_sum, gated_sum
):
    width = HEADS_EACH * HEAD
    group = qkv_ref.shape[0] // BATCHES
    conv = conv_ref[...]
    scaling = 1.0 / math.sqrt(HEAD)
    conv_sums = [jnp.zeros((1, width), f32) for _ in range(CONV)]
    for batch in range(BATCHES):
        ends = ends_of(lengths_ref, batch)
        base = batch * group
        values = qkv_ref[base : base + group, 2 * width :].astype(f32)
        shifted, mix = conv_terms(values, conv, ends)
        sigmoid = jax.nn.sigmoid(mix)
        gated_ref[...] = (values * (mix * sigmoid)).astype(bf16)
        keys_sum[...] = jnp.zeros_like(keys_sum)
        gated_sum[...] = jnp.zeros_like(gated_sum)
        for block in range(group // BLOCK):
            first = max(block - 1, 0)
            span = (block + 1 - first) * BLOCK
            allowed = block_mask(block, first, span, ends)
            rows = slice(base + block * BLOCK, base + (block + 1) * BLOCK)
            local = slice(first * BLOCK, first * BLOCK + span)
            for pair in range(width // 128):
                lanes = slice(pair * 128, (pair + 1) * 128)
                query = qkv_ref[rows, lanes]
                grad = grad_ref[rows, lanes]
                keys = qkv_ref[
                    base + first * BLOCK : base + first * BLOCK + span,
                    width + pair * 128 : width + (pair + 1) * 128,
                ]
                gated = gated_ref[local, lanes]
                grad_queries = []
                grad_keys = None
                grad_gated = None
                for head in range(2):
                    mine = head_lanes(query, head)
                    chosen = jnp.where(mine, query, jnp.zeros_like(query))
                    chosen_grad = jnp.where(mine, grad, jnp.zeros_like(grad))
                    weights = window_weights(chosen, keys, allowed)
                    grad_weights = product(chosen_grad, gated, NT)
                    inner = jnp.sum(weights * grad_weights, axis=-1, keepdims=True)
                    grad_scores = (weights * (grad_weights - inner)).astype(bf16)
                    grad_queries.append(product(grad_scores, keys, NN))
                    more_keys = product(grad_scores, chosen, TN)
                    more_gated = product(weights.astype(bf16), chosen_grad, TN)
                    grad_keys = more_keys if grad_keys is None else grad_keys + more_keys
                    grad_gated = more_gated if grad_gated is None else grad_gated + more_gated
                merged = jnp.where(head_lanes(grad_queries[0], 0), grad_queries[0], grad_queries[1])
                out_ref[rows, lanes] = (merged * scaling).astype(bf16)
                keys_sum[local, lanes] += grad_keys
                gated_sum[local, lanes] += grad_gated
        out_ref[base : base + group, width : 2 * width] = (keys_sum[...] * scaling).astype(bf16)
        grad_gated = gated_sum[...]
        grad_mix = grad_gated * values * (sigmoid * (1.0 + mix * (1.0 - sigmoid)))
        grad_values = grad_gated * (mix * sigmoid) + grad_mix * conv[0:1]
        places = lax.broadcasted_iota(jnp.int32, values.shape, 0)
        own_seg = seg_of(places, ends)
        conv_sums[0] = conv_sums[0] + jnp.sum(grad_mix * shifted[0], axis=0, keepdims=True)
        for lag in range(1, CONV):
            same = (places < group - lag) & (seg_of(places + lag, ends) == own_seg)
            later = jnp.where(same, pltpu.roll(grad_mix, group - lag, 0), 0.0)
            grad_values = grad_values + later * conv[lag : lag + 1]
            conv_sums[lag] = conv_sums[lag] + jnp.sum(grad_mix * shifted[lag], axis=0, keepdims=True)
        out_ref[base : base + group, 2 * width :] = grad_values.astype(bf16)
    for lag in range(CONV):
        grad_conv_ref[lag : lag + 1, :] = conv_sums[lag]


VMEM = pl.BlockSpec(memory_space=pltpu.VMEM)
SMEM = pl.BlockSpec(memory_space=pltpu.SMEM)


def attend_forward(lengths, qkv, conv):
    rows, width = qkv.shape[0], HEADS_EACH * HEAD
    return pl.pallas_call(
        attend_forward_kernel,
        out_shape=jax.ShapeDtypeStruct((rows, width), bf16),
        in_specs=[SMEM, VMEM, VMEM],
        out_specs=VMEM,
        scratch_shapes=[pltpu.VMEM((rows // BATCHES, width), bf16)],
        compiler_params=pltpu.CompilerParams(vmem_limit_bytes=32 * 1024 * 1024),
        name="attend_forward",
    )(lengths, qkv, conv)


def attend_backward(lengths, qkv, grad, conv):
    rows, width = qkv.shape[0], HEADS_EACH * HEAD
    group = rows // BATCHES
    return pl.pallas_call(
        attend_backward_kernel,
        out_shape=(
            jax.ShapeDtypeStruct((rows, 3 * width), bf16),
            jax.ShapeDtypeStruct((CONV, width), f32),
        ),
        in_specs=[SMEM, VMEM, VMEM, VMEM],
        out_specs=(VMEM, VMEM),
        scratch_shapes=[
            pltpu.VMEM((group, width), bf16),
            pltpu.VMEM((group, width), f32),
            pltpu.VMEM((group, width), f32),
        ],
        compiler_params=pltpu.CompilerParams(vmem_limit_bytes=32 * 1024 * 1024),
        name="attend_backward",
    )(lengths, qkv, grad, conv)


def part_of(total, each, index):
    start = jnp.minimum(index * each, total - each)
    return start, index * each - start


def joined(parts, total, each, axis):
    pieces = []
    for index, part in enumerate(parts):
        shared = index * each - min(index * each, total - each)
        pieces.append(lax.slice_in_dim(part, shared, each, axis=axis))
    return jnp.concatenate(pieces, axis=axis)


def per_device(
    tokens,
    cotangent,
    attn_in,
    attn_out,
    gate_up,
    down_proj,
    conv_weight,
    norm_gains,
    deal_order,
    lengths,
):
    sizes = tuple(lax.axis_size(axis) for axis in ("fsdp", "ctx", "tp"))
    n_fsdp, n_ctx, n_tp = sizes
    workers = n_fsdp * n_ctx
    f, c, t = (lax.axis_index(axis) for axis in ("fsdp", "ctx", "tp"))
    me = f * n_ctx + c
    tok_rows, d_model = tokens.shape[1:]
    d_own = attn_in.shape[1]
    heads_all = attn_in.shape[2]
    width = HEADS_EACH * HEAD
    ff_all = gate_up.shape[2]
    ff = -(-ff_all // (n_ctx * 128)) * 128
    from_each = tok_rows // n_fsdp
    half = from_each // n_tp
    group = n_ctx * tok_rows
    plane = BATCHES * group

    start, shared = part_of(heads_all, width, c)
    sliced = lax.dynamic_slice_in_dim(attn_in, start, width, 2)
    out_part = lax.dynamic_slice_in_dim(attn_out, start, width, 0)
    out_part = jnp.where(jnp.arange(width)[:, None] >= shared, out_part, jnp.zeros_like(out_part))
    attn_own = jnp.concatenate([sliced[0], sliced[1], sliced[2], out_part.T], axis=1)
    ff_start, ff_shared = part_of(ff_all, ff, c)
    sliced = lax.dynamic_slice_in_dim(gate_up, ff_start, ff, 2)
    down_part = lax.dynamic_slice_in_dim(down_proj, ff_start, ff, 0)
    down_part = jnp.where(jnp.arange(ff)[:, None] >= ff_shared, down_part, jnp.zeros_like(down_part))
    mlp_own = jnp.concatenate([sliced[0], sliced[1], down_part.T], axis=1)
    attn_w = lax.all_gather(attn_own, "fsdp", axis=0, tiled=True)
    mlp_w = lax.all_gather(mlp_own, "fsdp", axis=0, tiled=True)
    qkv_w, out_w = attn_w[:, : 3 * width], attn_w[:, 3 * width :]
    gate_w, down_w = mlp_w[:, : 2 * ff], mlp_w[:, 2 * ff :]

    small = jnp.concatenate(
        [
            deal_order.reshape(-1).astype(f32),
            norm_gains.reshape(-1).astype(f32),
            conv_weight.reshape(-1).astype(f32),
        ]
    )
    small = lax.all_to_all(
        jnp.broadcast_to(small[None], (workers,) + small.shape),
        ("fsdp", "ctx"),
        split_axis=0,
        concat_axis=0,
        tiled=True,
    )
    n_order, n_gain = deal_order.size, norm_gains.size
    orders = small[:, :n_order].astype(jnp.int32).reshape(workers, BATCHES, tok_rows)
    by_fsdp = small.reshape(n_fsdp, n_ctx, -1)[:, 0]
    gains = by_fsdp[:, n_order : n_order + n_gain].reshape(n_fsdp, 2, -1)
    gains = jnp.transpose(gains, (1, 0, 2)).reshape(2, 1, d_model)
    conv = by_fsdp[:, n_order + n_gain :].reshape(n_fsdp, CONV, -1)
    conv = jnp.transpose(conv, (1, 0, 2)).reshape(CONV, heads_all)
    conv = lax.dynamic_slice_in_dim(conv, start, width, 1)

    given = me * tok_rows + jnp.arange(tok_rows, dtype=jnp.int32)
    by_batch = jnp.transpose(orders, (1, 0, 2)).reshape(BATCHES, -1)
    planes = jnp.arange(workers * tok_rows, dtype=jnp.int32) // group
    to_plane = jnp.sum(
        jnp.where(by_batch[:, None, :] == given[None, :, None], planes[None, None, :], 0), axis=2
    )
    earlier = jnp.arange(tok_rows)[None, :] < jnp.arange(tok_rows)[:, None]
    slot = jnp.sum(
        ((to_plane[:, None, :] == to_plane[:, :, None]) & earlier[None]).astype(jnp.int32), axis=2
    )
    place = ((slot // half) * n_fsdp + to_plane) * (BATCHES * half) + slot % half
    place = place + jnp.arange(BATCHES, dtype=jnp.int32)[:, None] * half
    place = place.reshape(-1)
    sent_rows = BATCHES * tok_rows // n_tp
    wire = t * sent_rows + jnp.arange(sent_rows, dtype=jnp.int32)
    choose = (place[None, :] == wire[:, None]).astype(bf16)
    both = jnp.concatenate([wire, (1 - t) * sent_rows + jnp.arange(sent_rows, dtype=jnp.int32)])
    undo = (place[:, None] == both[None, :]).astype(bf16)

    def to_planes(rows):
        picked = product(choose, rows.reshape(-1, d_model), NN, bf16)
        return lax.all_to_all(picked, "fsdp", split_axis=0, concat_axis=0, tiled=True)

    def to_given(rows):
        home = lax.all_to_all(rows, "fsdp", split_axis=0, concat_axis=0, tiled=True)
        pair = jnp.concatenate([home, flipped(home, sizes, 2)])
        return product(undo, pair, NN, bf16).reshape(BATCHES, tok_rows, d_model)

    own_x = to_planes(tokens).astype(f32)
    own_g = to_planes(cotangent)

    dealt = lax.dynamic_slice_in_dim(orders, f * n_ctx, n_ctx, 0)
    dealt = jnp.transpose(dealt, (1, 0, 2)).reshape(BATCHES, group)
    giver = dealt // tok_rows
    rank = jnp.sum(
        (
            (giver[:, None, :] == giver[:, :, None]) & (dealt[:, None, :] < dealt[:, :, None])
        ).astype(jnp.int32),
        axis=2,
    )
    core = rank // half
    away = (giver % n_ctx) ^ c
    swapped = jnp.where(core == 0, away, (away % 2) * 2 + away // 2)
    block = jnp.where(core == t, 0, n_ctx) + swapped
    arrival = block * (plane // (n_ctx * n_tp)) + (giver // n_ctx) * (BATCHES * half)
    arrival = arrival + jnp.arange(BATCHES, dtype=jnp.int32)[:, None] * half + rank % half
    deal = (arrival.reshape(-1)[:, None] == jnp.arange(plane, dtype=jnp.int32)[None, :]).astype(bf16)

    first_scale = lax.rsqrt(jnp.mean(own_x * own_x, axis=-1, keepdims=True) + epsilon)
    hidden = plane_gather((own_x * first_scale * gains[0]).astype(bf16), sizes)
    own_lengths = lengths[:, 0]
    qkv = product(deal, product(hidden, qkv_w, NN, bf16), NN, bf16)
    attended = product(deal, attend_forward(own_lengths, qkv, conv), TN, bf16)
    kept = plane // 2
    branch = plane_scatter(
        product(attended[:kept], out_w, NT), product(attended[kept:], out_w, NT, bf16), sizes
    )
    resid = own_x + branch

    second_scale = lax.rsqrt(jnp.mean(resid * resid, axis=-1, keepdims=True) + epsilon)
    hidden_two = plane_gather((resid * second_scale * gains[1]).astype(bf16), sizes)
    grad_dealt = plane_gather(own_g, sizes)
    grad_inner = product(grad_dealt, down_w, NN)
    gate_up_out = product(hidden_two, gate_w, NN)
    gate_act, upper = gate_up_out[:, :ff], gate_up_out[:, ff:]
    sigmoid = jax.nn.sigmoid(gate_act)
    silu = gate_act * sigmoid
    inner = (silu * upper).astype(bf16)
    grad_gate = grad_inner * upper * (sigmoid * (1.0 + gate_act * (1.0 - sigmoid)))
    grad_pair = jnp.concatenate([grad_gate, grad_inner * silu], axis=1).astype(bf16)
    grad_two = plane_scatter(
        product(grad_pair[:kept], gate_w, NT), product(grad_pair[kept:], gate_w, NT, bf16), sizes
    )
    grad_mlp = jnp.concatenate(
        [product(hidden_two, grad_pair, TN, bf16), product(grad_dealt, inner, TN, bf16)], axis=1
    )
    grad_mlp = lax.psum_scatter(grad_mlp, "fsdp", scatter_dimension=0, tiled=True)
    lifted = plane_scatter(
        product(inner[:kept], down_w, NT), product(inner[kept:], down_w, NT, bf16), sizes
    )
    activations = to_given((resid + lifted).astype(bf16))

    normed = resid * second_scale
    scaled = grad_two * gains[1]
    grad_resid = own_g.astype(f32) + second_scale * (
        scaled - normed * jnp.mean(scaled * normed, axis=-1, keepdims=True)
    )
    grad_gain_two = jnp.sum(grad_two * normed, axis=0)

    grad_branch = plane_gather(grad_resid.astype(bf16), sizes)
    grad_attended = product(deal, product(grad_branch, out_w, NN, bf16), NN, bf16)
    grad_proj, grad_conv = attend_backward(own_lengths, qkv, grad_attended, conv)
    grad_proj = product(deal, grad_proj, TN, bf16)
    grad_hidden = plane_scatter(
        product(grad_proj[:kept], qkv_w, NT), product(grad_proj[kept:], qkv_w, NT, bf16), sizes
    )
    grad_attn = jnp.concatenate(
        [product(hidden, grad_proj, TN, bf16), product(grad_branch, attended, TN, bf16)], axis=1
    )
    grad_attn = lax.psum_scatter(grad_attn, "fsdp", scatter_dimension=0, tiled=True)

    normed = own_x * first_scale
    scaled = grad_hidden * gains[0]
    grad_x = grad_resid + first_scale * (
        scaled - normed * jnp.mean(scaled * normed, axis=-1, keepdims=True)
    )
    grad_gain_one = jnp.sum(grad_hidden * normed, axis=0)
    input_grad = to_given(grad_x.astype(bf16))

    placed = lax.dynamic_update_slice(jnp.zeros((CONV, heads_all), f32), grad_conv, (0, start))
    placed = jnp.where(jnp.arange(heads_all)[None, :] >= start + shared, placed, 0.0)
    sums = jnp.concatenate([placed.reshape(-1), grad_gain_one, grad_gain_two])
    sums = lax.psum(sums, ("fsdp", "ctx"))
    grad_conv = sums[: CONV * heads_all].reshape(CONV, heads_all)
    grad_conv = lax.dynamic_slice_in_dim(grad_conv, f * (heads_all // n_fsdp), heads_all // n_fsdp, 1)
    gain_sums = sums[CONV * heads_all :]
    gain_sums = gain_sums + flipped(gain_sums, sizes, 2)
    grad_gains = lax.dynamic_slice_in_dim(gain_sums.reshape(2, d_model), f * d_own, d_own, 1)

    grad_mlp = lax.all_gather(grad_mlp, "ctx", axis=0).astype(f32)
    grad_attn = lax.all_gather(grad_attn, "ctx", axis=0).astype(f32)
    in_parts = [jnp.stack([grad_attn[k][:, i * width : (i + 1) * width] for i in range(3)]) for k in range(n_ctx)]
    gate_parts = [jnp.stack([grad_mlp[k][:, i * ff : (i + 1) * ff] for i in range(2)]) for k in range(n_ctx)]
    out_parts = [grad_attn[k][:, 3 * width :].T for k in range(n_ctx)]
    down_parts = [grad_mlp[k][:, 2 * ff :].T for k in range(n_ctx)]
    return (
        activations,
        input_grad,
        joined(in_parts, heads_all, width, 2),
        joined(out_parts, heads_all, width, 0),
        joined(gate_parts, ff_all, ff, 2),
        joined(down_parts, ff_all, ff, 0),
        grad_conv[None],
        grad_gains,
    )


def solution(mesh):
    return jax.shard_map(
        per_device,
        mesh=mesh,
        in_specs=(
            P(None, ("fsdp", "ctx"), None),
            P(None, ("fsdp", "ctx"), None),
            P(None, "fsdp", "tp"),
            P("tp", "fsdp"),
            P(None, "fsdp", "tp"),
            P("tp", "fsdp"),
            P("tp", None, "fsdp"),
            P(None, "fsdp"),
            P(None, ("fsdp", "ctx")),
            P(None, "fsdp", None),
        ),
        out_specs=(
            P(None, ("fsdp", "ctx"), None),
            P(None, ("fsdp", "ctx"), None),
            P(None, "fsdp", "tp"),
            P("tp", "fsdp"),
            P(None, "fsdp", "tp"),
            P("tp", "fsdp"),
            P("tp", None, "fsdp"),
            P(None, "fsdp"),
        ),
        check_vma=False,
    )
```

```python
import functools
import math

import jax
import jax.numpy as jnp
from jax import lax
from jax.experimental import pallas as pl
from jax.experimental.pallas import tpu as pltpu
from jax.sharding import PartitionSpec as P

HEAD = 64
WINDOW = 64
CONV = 3
BATCHES = 2
BLOCK = 128
HEADS_EACH = 4

epsilon = 1e-06
masked_score = -1e30
f32 = jnp.float32
bf16 = jnp.bfloat16


def flipped(value, sizes, step):
    n_fsdp, n_ctx, n_tp = sizes
    pairs = []
    for f in range(n_fsdp):
        for c in range(n_ctx):
            for t in range(n_tp):
                if step == 2:
                    other = (c, t ^ 1)
                else:
                    other = (c ^ (1 if t == step else 2), t)
                pairs.append(((f * n_ctx + c) * n_tp + t, (f * n_ctx + other[0]) * n_tp + other[1]))
    return lax.ppermute(value, ("fsdp", "ctx", "tp"), pairs)


def plane_gather(own, sizes):
    one = flipped(own, sizes, 0)
    two = flipped(own, sizes, 1)
    three = flipped(one, sizes, 1)
    mine = [own, one, two, three]
    return jnp.concatenate(mine + [flipped(block, sizes, 2) for block in mine])


def plane_scatter(kept, sent, sizes):
    total = kept + flipped(sent.astype(bf16), sizes, 2).astype(f32)
    for step in (1, 0):
        half = total.shape[0] // 2
        total = total[:half] + flipped(total[half:].astype(bf16), sizes, step).astype(f32)
    return total


def after(value, *others):
    return lax.optimization_barrier((value,) + others)[0]


def z_shifted(value, sizes, steps):
    n = sizes[0]
    return lax.ppermute(value, "fsdp", [(i, (i + steps) % n) for i in range(n)])


def z_exchange(blocks, sizes):
    got = [blocks[0]] + [z_shifted(blocks[k], sizes, k) for k in range(1, sizes[0])]
    return jnp.concatenate(got)


def ctx_shares(own, sizes, core):
    one = flipped(own, sizes, 0)
    two = flipped(own, sizes, 1)
    three = flipped(one, sizes, 1)
    return [own, jnp.where(core == 0, one, two), jnp.where(core == 0, two, one), three]


def product(left, right, dims, out_type=f32):
    return lax.dot_general(left, right, (dims, ((), ())), preferred_element_type=f32).astype(out_type)


NN = ((1,), (0,))
NT = ((1,), (1,))
TN = ((0,), (0,))


def seg_of(places, ends):
    return (places >= ends[0]).astype(jnp.int32) + (places >= ends[1]).astype(jnp.int32)


def conv_terms(values, conv, ends):
    rows = values.shape[0]
    places = lax.broadcasted_iota(jnp.int32, values.shape, 0)
    own_seg = seg_of(places, ends)
    shifted = [values]
    for lag in range(1, CONV):
        same = (places >= lag) & (seg_of(places - lag, ends) == own_seg)
        shifted.append(jnp.where(same, pltpu.roll(values, lag, 0), 0.0))
    mix = shifted[0] * conv[0:1]
    for lag in range(1, CONV):
        mix = mix + shifted[lag] * conv[lag : lag + 1]
    return shifted, mix


def block_mask(block, first, span, ends):
    query = block * BLOCK + lax.broadcasted_iota(jnp.int32, (BLOCK, span), 0)
    key = first * BLOCK + lax.broadcasted_iota(jnp.int32, (BLOCK, span), 1)
    return (seg_of(query, ends) == seg_of(key, ends)) & (key <= query) & (key > query - WINDOW)


def head_lanes(tile, head):
    lanes = lax.broadcasted_iota(jnp.int32, tile.shape, 1)
    return (lanes >= head * HEAD) & (lanes < (head + 1) * HEAD)


def window_weights(query, keys, allowed):
    scores = product(query, keys, NT) * (1.0 / math.sqrt(HEAD))
    scores = jnp.where(allowed, scores, masked_score)
    weights = jnp.exp(scores - jnp.max(scores, axis=-1, keepdims=True))
    return weights / jnp.sum(weights, axis=-1, keepdims=True)


def ends_of(lengths_ref, batch):
    first = lengths_ref[batch, 0]
    return (first, first + lengths_ref[batch, 1])


def attend_forward_kernel(lengths_ref, qkv_ref, conv_ref, out_ref, gated_ref):
    width = HEADS_EACH * HEAD
    group = qkv_ref.shape[0] // BATCHES
    conv = conv_ref[...]
    for batch in range(BATCHES):
        ends = ends_of(lengths_ref, batch)
        base = batch * group
        values = qkv_ref[base : base + group, 2 * width :].astype(f32)
        _, mix = conv_terms(values, conv, ends)
        gated_ref[...] = (values * (mix * jax.nn.sigmoid(mix))).astype(bf16)
        for block in range(group // BLOCK):
            first = max(block - 1, 0)
            span = (block + 1 - first) * BLOCK
            allowed = block_mask(block, first, span, ends)
            rows = slice(base + block * BLOCK, base + (block + 1) * BLOCK)
            for pair in range(width // 128):
                lanes = slice(pair * 128, (pair + 1) * 128)
                query = qkv_ref[rows, lanes]
                keys = qkv_ref[
                    base + first * BLOCK : base + first * BLOCK + span,
                    width + pair * 128 : width + (pair + 1) * 128,
                ]
                gated = gated_ref[first * BLOCK : first * BLOCK + span, lanes]
                blended = []
                for head in range(2):
                    chosen = jnp.where(head_lanes(query, head), query, jnp.zeros_like(query))
                    weights = window_weights(chosen, keys, allowed).astype(bf16)
                    blended.append(product(weights, gated, NN))
                merged = jnp.where(head_lanes(blended[0], 0), blended[0], blended[1])
                out_ref[rows, lanes] = merged.astype(bf16)


def attend_backward_kernel(
    lengths_ref, qkv_ref, grad_ref, conv_ref, out_ref, grad_conv_ref, gated_ref, keys_sum, gated_sum
):
    width = HEADS_EACH * HEAD
    group = qkv_ref.shape[0] // BATCHES
    conv = conv_ref[...]
    scaling = 1.0 / math.sqrt(HEAD)
    conv_sums = [jnp.zeros((1, width), f32) for _ in range(CONV)]
    for batch in range(BATCHES):
        ends = ends_of(lengths_ref, batch)
        base = batch * group
        values = qkv_ref[base : base + group, 2 * width :].astype(f32)
        shifted, mix = conv_terms(values, conv, ends)
        sigmoid = jax.nn.sigmoid(mix)
        gated_ref[...] = (values * (mix * sigmoid)).astype(bf16)
        keys_sum[...] = jnp.zeros_like(keys_sum)
        gated_sum[...] = jnp.zeros_like(gated_sum)
        for block in range(group // BLOCK):
            first = max(block - 1, 0)
            span = (block + 1 - first) * BLOCK
            allowed = block_mask(block, first, span, ends)
            rows = slice(base + block * BLOCK, base + (block + 1) * BLOCK)
            local = slice(first * BLOCK, first * BLOCK + span)
            for pair in range(width // 128):
                lanes = slice(pair * 128, (pair + 1) * 128)
                query = qkv_ref[rows, lanes]
                grad = grad_ref[rows, lanes]
                keys = qkv_ref[
                    base + first * BLOCK : base + first * BLOCK + span,
                    width + pair * 128 : width + (pair + 1) * 128,
                ]
                gated = gated_ref[local, lanes]
                grad_queries = []
                grad_keys = None
                grad_gated = None
                for head in range(2):
                    mine = head_lanes(query, head)
                    chosen = jnp.where(mine, query, jnp.zeros_like(query))
                    chosen_grad = jnp.where(mine, grad, jnp.zeros_like(grad))
                    weights = window_weights(chosen, keys, allowed)
                    grad_weights = product(chosen_grad, gated, NT)
                    inner = jnp.sum(weights * grad_weights, axis=-1, keepdims=True)
                    grad_scores = (weights * (grad_weights - inner)).astype(bf16)
                    grad_queries.append(product(grad_scores, keys, NN))
                    more_keys = product(grad_scores, chosen, TN)
                    more_gated = product(weights.astype(bf16), chosen_grad, TN)
                    grad_keys = more_keys if grad_keys is None else grad_keys + more_keys
                    grad_gated = more_gated if grad_gated is None else grad_gated + more_gated
                merged = jnp.where(head_lanes(grad_queries[0], 0), grad_queries[0], grad_queries[1])
                out_ref[rows, lanes] = (merged * scaling).astype(bf16)
                keys_sum[local, lanes] += grad_keys
                gated_sum[local, lanes] += grad_gated
        out_ref[base : base + group, width : 2 * width] = (keys_sum[...] * scaling).astype(bf16)
        grad_gated = gated_sum[...]
        grad_mix = grad_gated * values * (sigmoid * (1.0 + mix * (1.0 - sigmoid)))
        grad_values = grad_gated * (mix * sigmoid) + grad_mix * conv[0:1]
        places = lax.broadcasted_iota(jnp.int32, values.shape, 0)
        own_seg = seg_of(places, ends)
        conv_sums[0] = conv_sums[0] + jnp.sum(grad_mix * shifted[0], axis=0, keepdims=True)
        for lag in range(1, CONV):
            same = (places < group - lag) & (seg_of(places + lag, ends) == own_seg)
            later = jnp.where(same, pltpu.roll(grad_mix, group - lag, 0), 0.0)
            grad_values = grad_values + later * conv[lag : lag + 1]
            conv_sums[lag] = conv_sums[lag] + jnp.sum(grad_mix * shifted[lag], axis=0, keepdims=True)
        out_ref[base : base + group, 2 * width :] = grad_values.astype(bf16)
    for lag in range(CONV):
        grad_conv_ref[lag : lag + 1, :] = conv_sums[lag]


def weight_grad_kernel(*refs):
    out_ref = refs[-1]
    at = 0
    for left_ref, right_ref in zip(refs[:-1:2], refs[1:-1:2]):
        width = right_ref.shape[1]
        out_ref[:, at : at + width] = product(left_ref[...], right_ref[...], TN, bf16)
        at += width


def weight_grad(*pairs, step=256):
    rows, d_model = pairs[0][0].shape
    width = sum(right.shape[1] for _, right in pairs)
    specs = []
    for left, right in pairs:
        specs.append(pl.BlockSpec((rows, step), lambda i: (0, i)))
        specs.append(pl.BlockSpec((rows, right.shape[1]), lambda i: (0, 0)))
    return pl.pallas_call(
        weight_grad_kernel,
        grid=(d_model // step,),
        out_shape=jax.ShapeDtypeStruct((d_model, width), bf16),
        in_specs=specs,
        out_specs=pl.BlockSpec((step, width), lambda i: (i, 0)),
        compiler_params=pltpu.CompilerParams(vmem_limit_bytes=40 * 1024 * 1024),
        cost_estimate=pl.CostEstimate(
            flops=2 * rows * d_model * width,
            bytes_accessed=2 * (rows * d_model * len(pairs) + (rows + d_model) * width),
            transcendentals=0,
        ),
        name="weight_grad",
    )(*[operand for pair in pairs for operand in pair])


def placed_kernel(each, total, counts, index_ref, *refs):
    n_parts = len(refs) - len(counts)
    outs = refs[n_parts:]
    for piece in range(n_parts):
        start = min(piece * each, total - each)
        shared = piece * each - start
        for k in range(n_parts):

            @pl.when((index_ref[0] ^ k) == piece)
            def _():
                at = 0
                for out, count in zip(outs, counts):
                    for i in range(count):
                        part = refs[k][:, at + shared : at + each].astype(f32)
                        at += each
                        out[i, :, start + shared : start + each] = part


def placed(parts, index, each, total, counts, steps):
    rows = parts[0].shape[0]
    block = rows // steps
    out_shape = [jax.ShapeDtypeStruct((count, rows, total), f32) for count in counts]
    out_specs = [pl.BlockSpec((count, block, total), lambda i: (0, i, 0)) for count in counts]
    width = parts[0].shape[1]
    return pl.pallas_call(
        functools.partial(placed_kernel, each, total, counts),
        grid=(steps,),
        out_shape=out_shape,
        in_specs=[SMEM] + [pl.BlockSpec((block, width), lambda i: (i, 0))] * len(parts),
        out_specs=out_specs,
        compiler_params=pltpu.CompilerParams(vmem_limit_bytes=40 * 1024 * 1024),
        cost_estimate=pl.CostEstimate(
            flops=0, bytes_accessed=rows * width * len(parts) * 6, transcendentals=0
        ),
        name="placed",
    )(index.reshape(1).astype(jnp.int32), *parts)


VMEM = pl.BlockSpec(memory_space=pltpu.VMEM)
SMEM = pl.BlockSpec(memory_space=pltpu.SMEM)


def attend_forward(lengths, qkv, conv):
    rows, width = qkv.shape[0], HEADS_EACH * HEAD
    return pl.pallas_call(
        attend_forward_kernel,
        out_shape=jax.ShapeDtypeStruct((rows, width), bf16),
        in_specs=[SMEM, VMEM, VMEM],
        out_specs=VMEM,
        scratch_shapes=[pltpu.VMEM((rows // BATCHES, width), bf16)],
        compiler_params=pltpu.CompilerParams(vmem_limit_bytes=32 * 1024 * 1024),
        name="attend_forward",
    )(lengths, qkv, conv)


def attend_backward(lengths, qkv, grad, conv):
    rows, width = qkv.shape[0], HEADS_EACH * HEAD
    group = rows // BATCHES
    return pl.pallas_call(
        attend_backward_kernel,
        out_shape=(
            jax.ShapeDtypeStruct((rows, 3 * width), bf16),
            jax.ShapeDtypeStruct((CONV, width), f32),
        ),
        in_specs=[SMEM, VMEM, VMEM, VMEM],
        out_specs=(VMEM, VMEM),
        scratch_shapes=[
            pltpu.VMEM((group, width), bf16),
            pltpu.VMEM((group, width), f32),
            pltpu.VMEM((group, width), f32),
        ],
        compiler_params=pltpu.CompilerParams(vmem_limit_bytes=32 * 1024 * 1024),
        name="attend_backward",
    )(lengths, qkv, grad, conv)


def part_of(total, each, index):
    start = jnp.minimum(index * each, total - each)
    return start, index * each - start


def joined(parts, total, each):
    pieces = []
    for index, part in enumerate(parts):
        start = min(index * each, total - each)
        pieces.append(part[:, index * each - start :])
    return jnp.concatenate(pieces, axis=1)


def per_device(
    tokens,
    cotangent,
    attn_in,
    attn_out,
    gate_up,
    down_proj,
    conv_weight,
    norm_gains,
    deal_order,
    lengths,
):
    sizes = tuple(lax.axis_size(axis) for axis in ("fsdp", "ctx", "tp"))
    n_fsdp, n_ctx, n_tp = sizes
    workers = n_fsdp * n_ctx
    f, c, t = (lax.axis_index(axis) for axis in ("fsdp", "ctx", "tp"))
    me = f * n_ctx + c
    tok_rows, d_model = tokens.shape[1:]
    d_own = attn_in.shape[1]
    heads_all = attn_in.shape[2]
    width = HEADS_EACH * HEAD
    ff_all = gate_up.shape[2]
    ff = -(-ff_all // (n_ctx * 128)) * 128
    from_each = tok_rows // n_fsdp
    half = from_each // n_tp
    group = n_ctx * tok_rows
    plane = BATCHES * group

    start, shared = part_of(heads_all, width, c)
    sliced = lax.dynamic_slice_in_dim(attn_in, start, width, 2)
    out_part = lax.dynamic_slice_in_dim(attn_out, start, width, 0)
    out_part = jnp.where(jnp.arange(width)[:, None] >= shared, out_part, jnp.zeros_like(out_part))
    attn_own = jnp.concatenate([sliced[0], sliced[1], sliced[2], out_part.T], axis=1)
    ff_start, ff_shared = part_of(ff_all, ff, c)
    sliced = lax.dynamic_slice_in_dim(gate_up, ff_start, ff, 2)
    down_part = lax.dynamic_slice_in_dim(down_proj, ff_start, ff, 0)
    down_part = jnp.where(jnp.arange(ff)[:, None] >= ff_shared, down_part, jnp.zeros_like(down_part))
    mlp_own = jnp.concatenate([sliced[0], sliced[1], down_part.T], axis=1)
    attn_w = lax.all_gather(attn_own, "fsdp", axis=0, tiled=True)
    mlp_w = lax.all_gather(after(mlp_own, attn_own), "fsdp", axis=0, tiled=True)
    gate_w, down_w = mlp_w[:, : 2 * ff], mlp_w[:, 2 * ff :]
    qkv_w, out_w = attn_w[:, : 3 * width], attn_w[:, 3 * width :]

    small = jnp.concatenate(
        [
            deal_order.reshape(-1).astype(f32),
            norm_gains.reshape(-1).astype(f32),
            conv_weight.reshape(-1).astype(f32),
        ]
    )
    small = after(small, attn_own)
    small = lax.all_to_all(
        jnp.broadcast_to(small[None], (workers,) + small.shape),
        ("fsdp", "ctx"),
        split_axis=0,
        concat_axis=0,
        tiled=True,
    )
    n_order, n_gain = deal_order.size, norm_gains.size
    orders = small[:, :n_order].astype(jnp.int32).reshape(workers, BATCHES, tok_rows)
    by_fsdp = small.reshape(n_fsdp, n_ctx, -1)[:, 0]
    gains = by_fsdp[:, n_order : n_order + n_gain].reshape(n_fsdp, 2, -1)
    gains = jnp.transpose(gains, (1, 0, 2)).reshape(2, 1, d_model)
    conv = by_fsdp[:, n_order + n_gain :].reshape(n_fsdp, CONV, -1)
    conv = jnp.transpose(conv, (1, 0, 2)).reshape(CONV, heads_all)
    conv = lax.dynamic_slice_in_dim(conv, start, width, 1)

    given = me * tok_rows + jnp.arange(tok_rows, dtype=jnp.int32)
    by_batch = jnp.transpose(orders, (1, 0, 2)).reshape(BATCHES, -1)
    planes = jnp.arange(workers * tok_rows, dtype=jnp.int32) // group
    to_plane = jnp.sum(
        jnp.where(by_batch[:, None, :] == given[None, :, None], planes[None, None, :], 0), axis=2
    )
    earlier = jnp.arange(tok_rows)[None, :] < jnp.arange(tok_rows)[:, None]
    slot = jnp.sum(
        ((to_plane[:, None, :] == to_plane[:, :, None]) & earlier[None]).astype(jnp.int32), axis=2
    )
    place = ((slot // half) * n_fsdp + (to_plane - f) % n_fsdp) * (BATCHES * half) + slot % half
    place = place + jnp.arange(BATCHES, dtype=jnp.int32)[:, None] * half
    place = place.reshape(-1)
    sent_rows = BATCHES * tok_rows // n_tp
    wire = t * sent_rows + jnp.arange(sent_rows, dtype=jnp.int32)
    choose = (place[None, :] == wire[:, None]).astype(bf16)
    both = jnp.concatenate([wire, (1 - t) * sent_rows + jnp.arange(sent_rows, dtype=jnp.int32)])
    undo = (place[:, None] == both[None, :]).astype(bf16)

    def to_planes(rows):
        picked = product(choose, rows.reshape(-1, d_model), NN, bf16)
        return z_exchange(jnp.split(picked, n_fsdp), sizes)

    def to_given(rows):
        blocks = jnp.split(rows, n_fsdp)
        home = jnp.concatenate(
            [blocks[0]] + [z_shifted(blocks[k], sizes, n_fsdp - k) for k in range(1, n_fsdp)]
        )
        pair = jnp.concatenate([home, flipped(home, sizes, 2)])
        return product(undo, pair, NN, bf16).reshape(BATCHES, tok_rows, d_model)

    own_x = to_planes(tokens).astype(f32)

    dealt = lax.dynamic_slice_in_dim(orders, f * n_ctx, n_ctx, 0)
    dealt = jnp.transpose(dealt, (1, 0, 2)).reshape(BATCHES, group)
    giver = dealt // tok_rows
    rank = jnp.sum(
        (
            (giver[:, None, :] == giver[:, :, None]) & (dealt[:, None, :] < dealt[:, :, None])
        ).astype(jnp.int32),
        axis=2,
    )
    core = rank // half
    away = (giver % n_ctx) ^ c
    swapped = jnp.where(core == 0, away, (away % 2) * 2 + away // 2)
    block = jnp.where(core == t, 0, n_ctx) + swapped
    arrival = block * (plane // (n_ctx * n_tp)) + (f - giver // n_ctx) % n_fsdp * (BATCHES * half)
    arrival = arrival + jnp.arange(BATCHES, dtype=jnp.int32)[:, None] * half + rank % half
    deal = (arrival.reshape(-1)[:, None] == jnp.arange(plane, dtype=jnp.int32)[None, :]).astype(bf16)

    first_scale = lax.rsqrt(jnp.mean(own_x * own_x, axis=-1, keepdims=True) + epsilon)
    hidden = plane_gather((own_x * first_scale * gains[0]).astype(bf16), sizes)
    own_lengths = lengths[:, 0]
    own_g = to_planes(after(cotangent, hidden))
    qkv = product(deal, product(hidden, qkv_w, NN, bf16), NN, bf16)
    grad_dealt = plane_gather(after(own_g, qkv), sizes)
    attended = product(deal, attend_forward(own_lengths, qkv, conv), TN, bf16)
    kept = plane // 2
    branch = plane_scatter(
        product(attended[:kept], out_w, NT),
        product(attended[kept:], out_w, NT, bf16),
        sizes,
    )
    resid = own_x + branch

    second_scale = lax.rsqrt(jnp.mean(resid * resid, axis=-1, keepdims=True) + epsilon)
    hidden_two = plane_gather((resid * second_scale * gains[1]).astype(bf16), sizes)
    grad_inner = product(grad_dealt, down_w, NN)
    gate_up_out = product(hidden_two, gate_w, NN)
    gate_act, upper = gate_up_out[:, :ff], gate_up_out[:, ff:]
    sigmoid = jax.nn.sigmoid(gate_act)
    silu = gate_act * sigmoid
    inner = (silu * upper).astype(bf16)
    grad_gate = grad_inner * upper * (sigmoid * (1.0 + gate_act * (1.0 - sigmoid)))
    grad_pair = jnp.concatenate([grad_gate, grad_inner * silu], axis=1).astype(bf16)
    grad_mlp_w = weight_grad((hidden_two, grad_pair), (grad_dealt, inner))
    grad_mlp = lax.psum_scatter(grad_mlp_w, "fsdp", scatter_dimension=0, tiled=True)
    grad_pair = after(grad_pair, grad_mlp_w)
    grad_two = plane_scatter(
        product(grad_pair[:kept], gate_w, NT),
        product(grad_pair[kept:], gate_w, NT, bf16),
        sizes,
    )
    lifted = plane_scatter(
        product(inner[:kept], down_w, NT),
        product(inner[kept:], down_w, NT, bf16),
        sizes,
    )
    normed = resid * second_scale
    scaled = grad_two * gains[1]
    grad_resid = own_g.astype(f32) + second_scale * (
        scaled - normed * jnp.mean(scaled * normed, axis=-1, keepdims=True)
    )

    grad_branch = plane_gather(
        after(grad_resid.astype(bf16), lifted), sizes
    )
    grad_attended = product(deal, product(grad_branch, out_w, NN, bf16), NN, bf16)
    grad_proj, grad_conv = attend_backward(own_lengths, qkv, grad_attended, conv)
    grad_proj = product(deal, grad_proj, TN, bf16)
    grad_attn_w = weight_grad((hidden, grad_proj), (grad_branch, attended))
    grad_attn = lax.psum_scatter(grad_attn_w, "fsdp", scatter_dimension=0, tiled=True)
    grad_proj = after(grad_proj, grad_attn_w)
    grad_hidden = plane_scatter(
        product(grad_proj[:kept], qkv_w, NT), product(grad_proj[kept:], qkv_w, NT, bf16), sizes
    )
    normed = own_x * first_scale
    scaled = grad_hidden * gains[0]
    grad_x = grad_resid + first_scale * (
        scaled - normed * jnp.mean(scaled * normed, axis=-1, keepdims=True)
    )
    input_grad = to_given(grad_x.astype(bf16))

    activations = to_given((resid + lifted).astype(bf16))

    if n_fsdp > 4:
        taps = lax.psum(grad_conv, "fsdp")
    else:
        taps = sum([z_shifted(grad_conv, sizes, k) for k in range(1, n_fsdp)], grad_conv)

    steps = 4 if d_own % 64 == 0 else 1
    grad_gate_up, grad_down = placed(
        ctx_shares(grad_mlp, sizes, t), c, ff, ff_all, (2, 1), steps
    )

    def gain_part(own, grad, each, skipped):
        columns = own.shape[1]
        counted = (jnp.arange(columns) % each) >= skipped
        terms = own.astype(f32) * grad[:, :columns].astype(f32)
        return jnp.sum(jnp.where(counted[None, :], terms, 0.0), axis=1)

    grad_attn, taps = after((grad_attn, taps), grad_down)
    sums = jnp.stack(
        [
            gain_part(attn_own[:, : 3 * width], grad_attn, width, shared),
            gain_part(mlp_own[:, : 2 * ff], grad_mlp, ff, ff_shared),
        ]
    )
    for step in (2, 0, 1):
        sums = sums + flipped(sums, sizes, step)
    grad_gains = sums / norm_gains.astype(f32)
    taps = ctx_shares(taps, sizes, t)
    taps = lax.switch(c, [lambda k=k: joined([taps[k ^ p] for p in range(n_ctx)], heads_all, width) for k in range(n_ctx)])
    grad_conv = lax.dynamic_slice_in_dim(taps, f * (heads_all // n_fsdp), heads_all // n_fsdp, 1)
    grad_attn_in, grad_attn_out = placed(
        ctx_shares(grad_attn, sizes, t), c, width, heads_all, (3, 1), steps
    )
    return (
        activations,
        input_grad,
        grad_attn_in,
        grad_attn_out[0].T,
        grad_gate_up,
        grad_down[0].T,
        grad_conv[None],
        grad_gains,
    )


def solution(mesh):
    return jax.shard_map(
        per_device,
        mesh=mesh,
        in_specs=(
            P(None, ("fsdp", "ctx"), None),
            P(None, ("fsdp", "ctx"), None),
            P(None, "fsdp", "tp"),
            P("tp", "fsdp"),
            P(None, "fsdp", "tp"),
            P("tp", "fsdp"),
            P("tp", None, "fsdp"),
            P(None, "fsdp"),
            P(None, ("fsdp", "ctx")),
            P(None, "fsdp", None),
        ),
        out_specs=(
            P(None, ("fsdp", "ctx"), None),
            P(None, ("fsdp", "ctx"), None),
            P(None, "fsdp", "tp"),
            P("tp", "fsdp"),
            P(None, "fsdp", "tp"),
            P("tp", "fsdp"),
            P("tp", None, "fsdp"),
            P(None, "fsdp"),
        ),
        check_vma=False,
    )
```

```python
import functools
import math

import jax
import jax.numpy as jnp
from jax import lax
from jax.experimental import pallas as pl
from jax.experimental.pallas import tpu as pltpu
from jax.sharding import PartitionSpec as P

HEAD = 64
WINDOW = 64
CONV = 3
BATCHES = 2
BLOCK = 128
HEADS_EACH = 4

epsilon = 1e-06
masked_score = -1e30
f32 = jnp.float32
bf16 = jnp.bfloat16


def flipped(value, sizes, step):
    n_fsdp, n_ctx, n_tp = sizes
    pairs = []
    for f in range(n_fsdp):
        for c in range(n_ctx):
            for t in range(n_tp):
                if step == 2:
                    other = (c, t ^ 1)
                else:
                    other = (c ^ (1 if t == step else 2), t)
                pairs.append(((f * n_ctx + c) * n_tp + t, (f * n_ctx + other[0]) * n_tp + other[1]))
    return lax.ppermute(value, ("fsdp", "ctx", "tp"), pairs)


def near_shares(own, sizes):
    return flipped(own, sizes, 0), flipped(own, sizes, 1)


def plane_gather(own, sizes, near=None):
    one, two = near or near_shares(own, sizes)
    three = flipped(one, sizes, 1)
    mine = [own, one, two, three]
    return jnp.concatenate(mine + [flipped(block, sizes, 2) for block in mine])


def plane_scatter(kept, sent, sizes):
    total = kept + flipped(sent.astype(bf16), sizes, 2).astype(f32)
    for step in (1, 0):
        half = total.shape[0] // 2
        total = total[:half] + flipped(total[half:].astype(bf16), sizes, step).astype(f32)
    return total


def after(value, *others):
    return lax.optimization_barrier((value,) + others)[0]


def stage(*values):
    return lax.optimization_barrier(values)


def added(part, got):
    half = part.shape[0] // 2
    return part[:half] + got[:half].astype(f32), (part[half:] + got[half:].astype(f32)).astype(bf16)


def z_shifted(value, sizes, steps):
    n = sizes[0]
    return lax.ppermute(value, "fsdp", [(i, (i + steps) % n) for i in range(n)])


def z_exchange(blocks, sizes):
    got = [blocks[0]] + [z_shifted(blocks[k], sizes, k) for k in range(1, sizes[0])]
    return jnp.concatenate(got)


def ctx_shares(own, sizes, core, near=None):
    one, two = near or near_shares(own, sizes)
    three = flipped(one, sizes, 1)
    return [own, jnp.where(core == 0, one, two), jnp.where(core == 0, two, one), three]


def product(left, right, dims, out_type=f32):
    return lax.dot_general(left, right, (dims, ((), ())), preferred_element_type=f32).astype(out_type)


NN = ((1,), (0,))
NT = ((1,), (1,))
TN = ((0,), (0,))


def seg_of(places, ends):
    return (places >= ends[0]).astype(jnp.int32) + (places >= ends[1]).astype(jnp.int32)


def conv_terms(values, conv, ends):
    rows = values.shape[0]
    places = lax.broadcasted_iota(jnp.int32, values.shape, 0)
    own_seg = seg_of(places, ends)
    shifted = [values]
    for lag in range(1, CONV):
        same = (places >= lag) & (seg_of(places - lag, ends) == own_seg)
        shifted.append(jnp.where(same, pltpu.roll(values, lag, 0), 0.0))
    mix = shifted[0] * conv[0:1]
    for lag in range(1, CONV):
        mix = mix + shifted[lag] * conv[lag : lag + 1]
    return shifted, mix


def block_mask(block, first, span, ends):
    query = block * BLOCK + lax.broadcasted_iota(jnp.int32, (BLOCK, span), 0)
    key = first * BLOCK + lax.broadcasted_iota(jnp.int32, (BLOCK, span), 1)
    return (seg_of(query, ends) == seg_of(key, ends)) & (key <= query) & (key > query - WINDOW)


def head_lanes(tile, head):
    lanes = lax.broadcasted_iota(jnp.int32, tile.shape, 1)
    return (lanes >= head * HEAD) & (lanes < (head + 1) * HEAD)


def window_weights(query, keys, allowed):
    scores = product(query, keys, NT) * (1.0 / math.sqrt(HEAD))
    scores = jnp.where(allowed, scores, masked_score)
    weights = jnp.exp(scores - jnp.max(scores, axis=-1, keepdims=True))
    return weights / jnp.sum(weights, axis=-1, keepdims=True)


def ends_of(lengths_ref, batch):
    first = lengths_ref[batch, 0]
    return (first, first + lengths_ref[batch, 1])


def attend_forward_kernel(lengths_ref, qkv_ref, conv_ref, out_ref, gated_ref):
    width = HEADS_EACH * HEAD
    group = qkv_ref.shape[0] // BATCHES
    conv = conv_ref[...]
    for batch in range(BATCHES):
        ends = ends_of(lengths_ref, batch)
        base = batch * group
        values = qkv_ref[base : base + group, 2 * width :].astype(f32)
        _, mix = conv_terms(values, conv, ends)
        gated_ref[...] = (values * (mix * jax.nn.sigmoid(mix))).astype(bf16)
        for block in range(group // BLOCK):
            first = max(block - 1, 0)
            span = (block + 1 - first) * BLOCK
            allowed = block_mask(block, first, span, ends)
            rows = slice(base + block * BLOCK, base + (block + 1) * BLOCK)
            for pair in range(width // 128):
                lanes = slice(pair * 128, (pair + 1) * 128)
                query = qkv_ref[rows, lanes]
                keys = qkv_ref[
                    base + first * BLOCK : base + first * BLOCK + span,
                    width + pair * 128 : width + (pair + 1) * 128,
                ]
                gated = gated_ref[first * BLOCK : first * BLOCK + span, lanes]
                blended = []
                for head in range(2):
                    chosen = jnp.where(head_lanes(query, head), query, jnp.zeros_like(query))
                    weights = window_weights(chosen, keys, allowed).astype(bf16)
                    blended.append(product(weights, gated, NN))
                merged = jnp.where(head_lanes(blended[0], 0), blended[0], blended[1])
                out_ref[rows, lanes] = merged.astype(bf16)


def attend_backward_kernel(
    lengths_ref, qkv_ref, grad_ref, conv_ref, out_ref, grad_conv_ref, gated_ref, keys_sum, gated_sum
):
    width = HEADS_EACH * HEAD
    group = qkv_ref.shape[0] // BATCHES
    conv = conv_ref[...]
    scaling = 1.0 / math.sqrt(HEAD)
    conv_sums = [jnp.zeros((1, width), f32) for _ in range(CONV)]
    for batch in range(BATCHES):
        ends = ends_of(lengths_ref, batch)
        base = batch * group
        values = qkv_ref[base : base + group, 2 * width :].astype(f32)
        shifted, mix = conv_terms(values, conv, ends)
        sigmoid = jax.nn.sigmoid(mix)
        gated_ref[...] = (values * (mix * sigmoid)).astype(bf16)
        keys_sum[...] = jnp.zeros_like(keys_sum)
        gated_sum[...] = jnp.zeros_like(gated_sum)
        for block in range(group // BLOCK):
            first = max(block - 1, 0)
            span = (block + 1 - first) * BLOCK
            allowed = block_mask(block, first, span, ends)
            rows = slice(base + block * BLOCK, base + (block + 1) * BLOCK)
            local = slice(first * BLOCK, first * BLOCK + span)
            for pair in range(width // 128):
                lanes = slice(pair * 128, (pair + 1) * 128)
                query = qkv_ref[rows, lanes]
                grad = grad_ref[rows, lanes]
                keys = qkv_ref[
                    base + first * BLOCK : base + first * BLOCK + span,
                    width + pair * 128 : width + (pair + 1) * 128,
                ]
                gated = gated_ref[local, lanes]
                grad_queries = []
                grad_keys = None
                grad_gated = None
                for head in range(2):
                    mine = head_lanes(query, head)
                    chosen = jnp.where(mine, query, jnp.zeros_like(query))
                    chosen_grad = jnp.where(mine, grad, jnp.zeros_like(grad))
                    weights = window_weights(chosen, keys, allowed)
                    grad_weights = product(chosen_grad, gated, NT)
                    inner = jnp.sum(weights * grad_weights, axis=-1, keepdims=True)
                    grad_scores = (weights * (grad_weights - inner)).astype(bf16)
                    grad_queries.append(product(grad_scores, keys, NN))
                    more_keys = product(grad_scores, chosen, TN)
                    more_gated = product(weights.astype(bf16), chosen_grad, TN)
                    grad_keys = more_keys if grad_keys is None else grad_keys + more_keys
                    grad_gated = more_gated if grad_gated is None else grad_gated + more_gated
                merged = jnp.where(head_lanes(grad_queries[0], 0), grad_queries[0], grad_queries[1])
                out_ref[rows, lanes] = (merged * scaling).astype(bf16)
                keys_sum[local, lanes] += grad_keys
                gated_sum[local, lanes] += grad_gated
        out_ref[base : base + group, width : 2 * width] = (keys_sum[...] * scaling).astype(bf16)
        grad_gated = gated_sum[...]
        grad_mix = grad_gated * values * (sigmoid * (1.0 + mix * (1.0 - sigmoid)))
        grad_values = grad_gated * (mix * sigmoid) + grad_mix * conv[0:1]
        places = lax.broadcasted_iota(jnp.int32, values.shape, 0)
        own_seg = seg_of(places, ends)
        conv_sums[0] = conv_sums[0] + jnp.sum(grad_mix * shifted[0], axis=0, keepdims=True)
        for lag in range(1, CONV):
            same = (places < group - lag) & (seg_of(places + lag, ends) == own_seg)
            later = jnp.where(same, pltpu.roll(grad_mix, group - lag, 0), 0.0)
            grad_values = grad_values + later * conv[lag : lag + 1]
            conv_sums[lag] = conv_sums[lag] + jnp.sum(grad_mix * shifted[lag], axis=0, keepdims=True)
        out_ref[base : base + group, 2 * width :] = grad_values.astype(bf16)
    for lag in range(CONV):
        grad_conv_ref[lag : lag + 1, :] = conv_sums[lag]


def weight_grad_kernel(turned, *refs):
    out_ref = refs[-1]
    at = 0
    for is_turned, left_ref, right_ref in zip(turned, refs[:-1:2], refs[1:-1:2]):
        width = right_ref.shape[1]
        dims = NN if is_turned else TN
        out_ref[:, at : at + width] = product(left_ref[...], right_ref[...], dims, bf16)
        at += width


def weight_grad(*pairs, step=256):
    rows = pairs[0][1].shape[0]
    turned = tuple(left.shape[1] == rows for left, _ in pairs)
    d_model = pairs[0][0].shape[0 if turned[0] else 1]
    width = sum(right.shape[1] for _, right in pairs)
    specs = []
    for is_turned, (left, right) in zip(turned, pairs):
        if is_turned:
            specs.append(pl.BlockSpec((step, rows), lambda i: (i, 0)))
        else:
            specs.append(pl.BlockSpec((rows, step), lambda i: (0, i)))
        specs.append(pl.BlockSpec((rows, right.shape[1]), lambda i: (0, 0)))
    return pl.pallas_call(
        functools.partial(weight_grad_kernel, turned),
        grid=(d_model // step,),
        out_shape=jax.ShapeDtypeStruct((d_model, width), bf16),
        in_specs=specs,
        out_specs=pl.BlockSpec((step, width), lambda i: (i, 0)),
        compiler_params=pltpu.CompilerParams(vmem_limit_bytes=40 * 1024 * 1024),
        cost_estimate=pl.CostEstimate(
            flops=2 * rows * d_model * width,
            bytes_accessed=2 * (rows * d_model * len(pairs) + (rows + d_model) * width),
            transcendentals=0,
        ),
        name="weight_grad",
    )(*[operand for pair in pairs for operand in pair])


def feed_forward_kernel(hidden_ref, grad_ref, weight_ref, inner_ref, pair_ref):
    ff = inner_ref.shape[1]
    both = product(hidden_ref[...], weight_ref[:, : 2 * ff], NN)
    grad_inner = product(grad_ref[...], weight_ref[:, 2 * ff :], NN)
    gate_act, upper = both[:, :ff], both[:, ff:]
    sigmoid = jax.nn.sigmoid(gate_act)
    silu = gate_act * sigmoid
    inner_ref[...] = (silu * upper).astype(bf16)
    grad_gate = grad_inner * upper * (sigmoid * (1.0 + gate_act * (1.0 - sigmoid)))
    pair_ref[:, :ff] = grad_gate.astype(bf16)
    pair_ref[:, ff:] = (grad_inner * silu).astype(bf16)


def feed_forward(hidden, grad, weight, step=256):
    rows, d_model = hidden.shape
    ff = weight.shape[1] // 3
    return pl.pallas_call(
        feed_forward_kernel,
        grid=(rows // step,),
        out_shape=(
            jax.ShapeDtypeStruct((rows, ff), bf16),
            jax.ShapeDtypeStruct((rows, 2 * ff), bf16),
        ),
        in_specs=[
            pl.BlockSpec((step, d_model), lambda i: (i, 0)),
            pl.BlockSpec((step, d_model), lambda i: (i, 0)),
            pl.BlockSpec((d_model, 3 * ff), lambda i: (0, 0)),
        ],
        out_specs=(
            pl.BlockSpec((step, ff), lambda i: (i, 0)),
            pl.BlockSpec((step, 2 * ff), lambda i: (i, 0)),
        ),
        compiler_params=pltpu.CompilerParams(vmem_limit_bytes=48 * 1024 * 1024),
        cost_estimate=pl.CostEstimate(
            flops=6 * rows * d_model * ff,
            bytes_accessed=2 * (2 * rows * d_model + 3 * (d_model + rows) * ff),
            transcendentals=rows * ff,
        ),
        name="feed_forward",
    )(hidden, grad, weight)


def placed_kernel(each, total, counts, index_ref, *refs):
    n_parts = len(refs) - len(counts)
    outs = refs[n_parts:]
    for piece in range(n_parts):
        start = min(piece * each, total - each)
        shared = piece * each - start
        for k in range(n_parts):

            @pl.when((index_ref[0] ^ k) == piece)
            def _():
                at = 0
                for out, count in zip(outs, counts):
                    for i in range(count):
                        part = refs[k][:, at + shared : at + each].astype(f32)
                        at += each
                        out[i, :, start + shared : start + each] = part


def placed(parts, index, each, total, counts, steps):
    rows = parts[0].shape[0]
    block = rows // steps
    out_shape = [jax.ShapeDtypeStruct((count, rows, total), f32) for count in counts]
    out_specs = [pl.BlockSpec((count, block, total), lambda i: (0, i, 0)) for count in counts]
    width = parts[0].shape[1]
    return pl.pallas_call(
        functools.partial(placed_kernel, each, total, counts),
        grid=(steps,),
        out_shape=out_shape,
        in_specs=[SMEM] + [pl.BlockSpec((block, width), lambda i: (i, 0))] * len(parts),
        out_specs=out_specs,
        compiler_params=pltpu.CompilerParams(vmem_limit_bytes=40 * 1024 * 1024),
        cost_estimate=pl.CostEstimate(
            flops=0, bytes_accessed=rows * width * len(parts) * 6, transcendentals=0
        ),
        name="placed",
    )(index.reshape(1).astype(jnp.int32), *parts)


def at_home_kernel(undo_ref, *refs):
    *blocks, first_ref, second_ref, rows = refs
    each = blocks[0].shape[0]
    for k, block in enumerate(blocks):
        rows[k * each : (k + 1) * each, :] = block[...]
    d_model = first_ref.shape[2]
    for batch in range(first_ref.shape[0]):
        undo = undo_ref[batch * first_ref.shape[1] : (batch + 1) * first_ref.shape[1], :]
        first_ref[batch] = product(undo, rows[:, :d_model], NN, bf16)
        second_ref[batch] = product(undo, rows[:, d_model:], NN, bf16)


def at_home(undo, blocks, batches, d_model):
    rows = undo.shape[0]
    out = jax.ShapeDtypeStruct((batches, rows // batches, d_model), bf16)
    return pl.pallas_call(
        at_home_kernel,
        out_shape=(out, out),
        in_specs=[VMEM] * (1 + len(blocks)),
        out_specs=(VMEM, VMEM),
        scratch_shapes=[pltpu.VMEM((rows, 2 * d_model), bf16)],
        compiler_params=pltpu.CompilerParams(vmem_limit_bytes=32 * 1024 * 1024),
        cost_estimate=pl.CostEstimate(flops=0, bytes_accessed=10_000_000, transcendentals=0),
        name="at_home",
    )(undo, *blocks)


VMEM = pl.BlockSpec(memory_space=pltpu.VMEM)
SMEM = pl.BlockSpec(memory_space=pltpu.SMEM)


def attend_forward(lengths, qkv, conv):
    rows, width = qkv.shape[0], HEADS_EACH * HEAD
    return pl.pallas_call(
        attend_forward_kernel,
        out_shape=jax.ShapeDtypeStruct((rows, width), bf16),
        in_specs=[SMEM, VMEM, VMEM],
        out_specs=VMEM,
        scratch_shapes=[pltpu.VMEM((rows // BATCHES, width), bf16)],
        compiler_params=pltpu.CompilerParams(vmem_limit_bytes=32 * 1024 * 1024),
        cost_estimate=pl.CostEstimate(flops=0, bytes_accessed=20_000_000, transcendentals=0),
        name="attend_forward",
    )(lengths, qkv, conv)


def attend_backward(lengths, qkv, grad, conv):
    rows, width = qkv.shape[0], HEADS_EACH * HEAD
    group = rows // BATCHES
    return pl.pallas_call(
        attend_backward_kernel,
        out_shape=(
            jax.ShapeDtypeStruct((rows, 3 * width), bf16),
            jax.ShapeDtypeStruct((CONV, width), f32),
        ),
        in_specs=[SMEM, VMEM, VMEM, VMEM],
        out_specs=(VMEM, VMEM),
        scratch_shapes=[
            pltpu.VMEM((group, width), bf16),
            pltpu.VMEM((group, width), f32),
            pltpu.VMEM((group, width), f32),
        ],
        compiler_params=pltpu.CompilerParams(vmem_limit_bytes=32 * 1024 * 1024),
        cost_estimate=pl.CostEstimate(flops=0, bytes_accessed=50_000_000, transcendentals=0),
        name="attend_backward",
    )(lengths, qkv, grad, conv)


def part_of(total, each, index):
    start = jnp.minimum(index * each, total - each)
    return start, index * each - start


def per_device(
    tokens,
    cotangent,
    attn_in,
    attn_out,
    gate_up,
    down_proj,
    conv_weight,
    norm_gains,
    deal_order,
    lengths,
):
    sizes = tuple(lax.axis_size(axis) for axis in ("fsdp", "ctx", "tp"))
    n_fsdp, n_ctx, n_tp = sizes
    workers = n_fsdp * n_ctx
    f, c, t = (lax.axis_index(axis) for axis in ("fsdp", "ctx", "tp"))
    me = f * n_ctx + c
    tok_rows, d_model = tokens.shape[1:]
    d_own = attn_in.shape[1]
    heads_all = attn_in.shape[2]
    width = HEADS_EACH * HEAD
    ff_all = gate_up.shape[2]
    ff = -(-ff_all // (n_ctx * 128)) * 128
    from_each = tok_rows // n_fsdp
    half = from_each // n_tp
    group = n_ctx * tok_rows
    plane = BATCHES * group

    start, shared = part_of(heads_all, width, c)
    sliced = lax.dynamic_slice_in_dim(attn_in, start, width, 2)
    out_part = lax.dynamic_slice_in_dim(attn_out, start, width, 0)
    out_part = jnp.where(jnp.arange(width)[:, None] >= shared, out_part, jnp.zeros_like(out_part))
    attn_own = jnp.concatenate([sliced[0], sliced[1], sliced[2], out_part.T], axis=1)
    ff_start, ff_shared = part_of(ff_all, ff, c)
    sliced = lax.dynamic_slice_in_dim(gate_up, ff_start, ff, 2)
    down_part = lax.dynamic_slice_in_dim(down_proj, ff_start, ff, 0)
    down_part = jnp.where(jnp.arange(ff)[:, None] >= ff_shared, down_part, jnp.zeros_like(down_part))
    mlp_own = jnp.concatenate([sliced[0], sliced[1], down_part.T], axis=1)
    attn_w = lax.all_gather(attn_own, "fsdp", axis=0, tiled=True)
    mlp_w = lax.all_gather(after(mlp_own, attn_own), "fsdp", axis=0, tiled=True)
    gate_w, down_w = mlp_w[:, : 2 * ff], mlp_w[:, 2 * ff :]
    qkv_w, out_w = attn_w[:, : 3 * width], attn_w[:, 3 * width :]

    small = jnp.concatenate(
        [
            deal_order.reshape(-1).astype(f32),
            norm_gains.reshape(-1).astype(f32),
            conv_weight.reshape(-1).astype(f32),
        ]
    )
    small = after(small, attn_own)
    small = lax.all_to_all(
        jnp.broadcast_to(small[None], (workers,) + small.shape),
        ("fsdp", "ctx"),
        split_axis=0,
        concat_axis=0,
        tiled=True,
    )
    n_order, n_gain = deal_order.size, norm_gains.size
    orders = small[:, :n_order].astype(jnp.int32).reshape(workers, BATCHES, tok_rows)
    by_fsdp = small.reshape(n_fsdp, n_ctx, -1)[:, 0]
    gains = by_fsdp[:, n_order : n_order + n_gain].reshape(n_fsdp, 2, -1)
    gains = jnp.transpose(gains, (1, 0, 2)).reshape(2, 1, d_model)
    conv = by_fsdp[:, n_order + n_gain :].reshape(n_fsdp, CONV, -1)
    conv = jnp.transpose(conv, (1, 0, 2)).reshape(CONV, heads_all)
    conv = lax.dynamic_slice_in_dim(conv, start, width, 1)

    given = me * tok_rows + jnp.arange(tok_rows, dtype=jnp.int32)
    by_batch = jnp.transpose(orders, (1, 0, 2)).reshape(BATCHES, -1)
    planes = jnp.arange(workers * tok_rows, dtype=jnp.int32) // group
    to_plane = jnp.sum(
        jnp.where(by_batch[:, None, :] == given[None, :, None], planes[None, None, :], 0), axis=2
    )
    earlier = jnp.arange(tok_rows)[None, :] < jnp.arange(tok_rows)[:, None]
    slot = jnp.sum(
        ((to_plane[:, None, :] == to_plane[:, :, None]) & earlier[None]).astype(jnp.int32), axis=2
    )
    place = ((slot // half) * n_fsdp + (to_plane - f) % n_fsdp) * (BATCHES * half) + slot % half
    place = place + jnp.arange(BATCHES, dtype=jnp.int32)[:, None] * half
    place = place.reshape(-1)
    sent_rows = BATCHES * tok_rows // n_tp
    wire = t * sent_rows + jnp.arange(sent_rows, dtype=jnp.int32)
    choose = (place[None, :] == wire[:, None]).astype(bf16)
    both = jnp.concatenate([wire, (1 - t) * sent_rows + jnp.arange(sent_rows, dtype=jnp.int32)])
    undo = (place[:, None] == both[None, :]).astype(bf16)

    def to_planes(rows):
        picked = product(choose, rows.reshape(-1, d_model), NN, bf16)
        return z_exchange(jnp.split(picked, n_fsdp), sizes)

    def to_home(rows):
        blocks = jnp.split(rows, n_fsdp)
        return [blocks[0]] + [z_shifted(blocks[k], sizes, n_fsdp - k) for k in range(1, n_fsdp)]

    own_x = to_planes(tokens).astype(f32)

    dealt = lax.dynamic_slice_in_dim(orders, f * n_ctx, n_ctx, 0)
    dealt = jnp.transpose(dealt, (1, 0, 2)).reshape(BATCHES, group)
    giver = dealt // tok_rows
    rank = jnp.sum(
        (
            (giver[:, None, :] == giver[:, :, None]) & (dealt[:, None, :] < dealt[:, :, None])
        ).astype(jnp.int32),
        axis=2,
    )
    core = rank // half
    away = (giver % n_ctx) ^ c
    swapped = jnp.where(core == 0, away, (away % 2) * 2 + away // 2)
    block = jnp.where(core == t, 0, n_ctx) + swapped
    arrival = block * (plane // (n_ctx * n_tp)) + (f - giver // n_ctx) % n_fsdp * (BATCHES * half)
    arrival = arrival + jnp.arange(BATCHES, dtype=jnp.int32)[:, None] * half + rank % half
    deal = (arrival.reshape(-1)[:, None] == jnp.arange(plane, dtype=jnp.int32)[None, :]).astype(bf16)

    first_scale = lax.rsqrt(jnp.mean(own_x * own_x, axis=-1, keepdims=True) + epsilon)
    hidden = plane_gather((own_x * first_scale * gains[0]).astype(bf16), sizes)
    own_lengths = lengths[:, 0]
    own_g = to_planes(after(cotangent, hidden))
    qkv = product(deal, product(hidden, qkv_w, NN, bf16), NN, bf16)
    grad_dealt = plane_gather(after(own_g, qkv), sizes)
    attended = product(deal, attend_forward(own_lengths, qkv, conv), TN, bf16)
    kept = plane // 2
    branch = plane_scatter(
        product(attended[:kept], out_w, NT),
        product(attended[kept:], out_w, NT, bf16),
        sizes,
    )
    resid = own_x + branch

    second_scale = lax.rsqrt(jnp.mean(resid * resid, axis=-1, keepdims=True) + epsilon)
    hidden_two = plane_gather((resid * second_scale * gains[1]).astype(bf16), sizes)
    hidden_two_turned, grad_dealt_turned = after((hidden_two.T, grad_dealt.T))
    inner, grad_pair = feed_forward(
        after(hidden_two, hidden_two_turned, grad_dealt_turned), grad_dealt, mlp_w
    )
    grad_mlp_w = weight_grad((hidden_two_turned, grad_pair), (grad_dealt_turned, inner))
    grad_mlp_w, grad_pair, inner = stage(grad_mlp_w, grad_pair, inner)
    grad_mlp = lax.psum_scatter(grad_mlp_w, "fsdp", scatter_dimension=0, tiled=True)

    sent = product(grad_pair[kept:], gate_w, NT, bf16)
    sent, grad_pair = stage(sent, grad_pair)

    got = flipped(sent, sizes, 2)
    part = product(grad_pair[:kept], gate_w, NT)
    got, part = stage(got, part)
    part, sent = added(part, got)
    part, sent, inner = stage(part, sent, inner)

    got = flipped(sent, sizes, 1)
    lift_sent = product(inner[kept:], down_w, NT, bf16)
    lift = product(inner[:kept], down_w, NT)
    got, part, lift_sent, lift = stage(got, part, lift_sent, lift)
    part, sent = added(part, got)
    part, sent, lift_sent, lift = stage(part, sent, lift_sent, lift)

    got = flipped(sent, sizes, 0)
    lift_got = flipped(lift_sent, sizes, 2)
    grad_two = part + got.astype(f32)
    normed = resid * second_scale
    scaled = grad_two * gains[1]
    grad_resid = own_g.astype(f32) + second_scale * (
        scaled - normed * jnp.mean(scaled * normed, axis=-1, keepdims=True)
    )
    grad_own = grad_resid.astype(bf16)
    lift, lift_sent = added(lift, lift_got)
    grad_own, lift, lift_sent = stage(grad_own, lift, lift_sent)

    near = near_shares(grad_own, sizes)
    grad_own, near = stage(grad_own, near)
    grad_branch = plane_gather(grad_own, sizes, near)
    grad_branch, lift_sent = stage(grad_branch, lift_sent)

    lift_got = flipped(lift_sent, sizes, 1)
    grad_attended = product(deal, product(grad_branch, out_w, NN, bf16), NN, bf16)
    grad_proj, grad_conv = attend_backward(own_lengths, qkv, grad_attended, conv)
    lift_got, lift, grad_proj = stage(lift_got, lift, grad_proj)
    lift, lift_sent = added(lift, lift_got)
    lift, lift_sent, grad_proj = stage(lift, lift_sent, grad_proj)

    lift_got = flipped(lift_sent, sizes, 0)
    grad_proj = product(deal, grad_proj, TN, bf16)
    sent = product(grad_proj[kept:], qkv_w, NT, bf16)
    lift_got, grad_proj, sent = stage(lift_got, grad_proj, sent)
    result = (resid + (lift + lift_got.astype(f32))).astype(bf16)

    got = flipped(sent, sizes, 2)
    part = product(grad_proj[:kept], qkv_w, NT)
    got, part = stage(got, part)
    part, sent = added(part, got)
    part, sent, grad_proj = stage(part, sent, grad_proj)

    got = flipped(sent, sizes, 1)
    grad_attn_w = weight_grad((hidden, grad_proj), (grad_branch, attended))
    got, part, grad_attn_w = stage(got, part, grad_attn_w)
    grad_attn = lax.psum_scatter(grad_attn_w, "fsdp", scatter_dimension=0, tiled=True)
    part, sent = added(part, got)

    grad_hidden = part + flipped(sent, sizes, 0).astype(f32)
    normed = own_x * first_scale
    scaled = grad_hidden * gains[0]
    grad_x = grad_resid + first_scale * (
        scaled - normed * jnp.mean(scaled * normed, axis=-1, keepdims=True)
    )
    grad_x = grad_x.astype(bf16)

    spread = lax.dynamic_update_slice(jnp.zeros((CONV, heads_all), f32), grad_conv, (0, start))
    taps = jnp.where(jnp.arange(heads_all)[None, :] >= start + shared, spread, 0.0)
    if n_fsdp > 4:
        taps = lax.psum(taps, "fsdp")
    else:
        taps = sum([z_shifted(taps, sizes, k) for k in range(1, n_fsdp)], taps)

    steps = 4 if d_own % 64 == 0 else 1

    def gain_part(own, grad, each, skipped):
        columns = own.shape[1]
        counted = (jnp.arange(columns) % each) >= skipped
        terms = own.astype(f32) * grad[:, :columns].astype(f32)
        return jnp.sum(jnp.where(counted[None, :], terms, 0.0), axis=1)

    mlp_shares = ctx_shares(after(grad_mlp, grad_x), sizes, t)
    gain_two = gain_part(mlp_own[:, : 2 * ff], grad_mlp, ff, ff_shared)
    rows_back = jnp.concatenate([result, grad_x], axis=1)
    grad_gate_up, grad_down = placed(mlp_shares, c, ff, ff_all, (2, 1), steps)
    grad_attn, rows_back, grad_gate_up, grad_down, gain_two, taps = stage(
        grad_attn, rows_back, grad_gate_up, grad_down, gain_two, taps
    )

    near = near_shares(grad_attn, sizes)
    home = to_home(rows_back)
    gain_one = gain_part(attn_own[:, : 3 * width], grad_attn, width, shared)
    gains_grad = jnp.stack([gain_one, gain_two])
    gains_grad = gains_grad + flipped(gains_grad, sizes, 2)
    near, gains_grad = stage(near, gains_grad)

    attn_shares = ctx_shares(grad_attn, sizes, t, near)
    small = jnp.concatenate([gains_grad.reshape(-1), taps.reshape(-1)])
    for step in (0, 1):
        small = small + flipped(small, sizes, step)
    activations, input_grad = at_home(
        undo, home + [flipped(block, sizes, 2) for block in home], BATCHES, d_model
    )
    grad_gains = small[: gains_grad.size].reshape(2, -1) / norm_gains.astype(f32)
    grad_conv = lax.dynamic_slice_in_dim(
        small[gains_grad.size :].reshape(CONV, heads_all),
        f * (heads_all // n_fsdp),
        heads_all // n_fsdp,
        1,
    )
    grad_attn_in, grad_attn_out = placed(
        attn_shares, c, width, heads_all, (3, 1), steps
    )
    return (
        activations,
        input_grad,
        grad_attn_in,
        grad_attn_out[0].T,
        grad_gate_up,
        grad_down[0].T,
        grad_conv[None],
        grad_gains,
    )


def solution(mesh):
    return jax.shard_map(
        per_device,
        mesh=mesh,
        in_specs=(
            P(None, ("fsdp", "ctx"), None),
            P(None, ("fsdp", "ctx"), None),
            P(None, "fsdp", "tp"),
            P("tp", "fsdp"),
            P(None, "fsdp", "tp"),
            P("tp", "fsdp"),
            P("tp", None, "fsdp"),
            P(None, "fsdp"),
            P(None, ("fsdp", "ctx")),
            P(None, "fsdp", None),
        ),
        out_specs=(
            P(None, ("fsdp", "ctx"), None),
            P(None, ("fsdp", "ctx"), None),
            P(None, "fsdp", "tp"),
            P("tp", "fsdp"),
            P(None, "fsdp", "tp"),
            P("tp", "fsdp"),
            P("tp", None, "fsdp"),
            P(None, "fsdp"),
        ),
        check_vma=False,
    )
```

```python
import functools
import math

import jax
import jax.numpy as jnp
from jax import lax
from jax.experimental import pallas as pl
from jax.experimental.pallas import tpu as pltpu
from jax.sharding import PartitionSpec as P

HEAD = 64
WINDOW = 64
CONV = 3
BATCHES = 2
BLOCK = 128
HEADS_EACH = 4

epsilon = 1e-06
masked_score = -1e30
f32 = jnp.float32
bf16 = jnp.bfloat16


def flipped(value, sizes, step):
    n_fsdp, n_ctx, n_tp = sizes
    pairs = []
    for f in range(n_fsdp):
        for c in range(n_ctx):
            for t in range(n_tp):
                if step == 2:
                    other = (c, t ^ 1)
                else:
                    other = (c ^ (1 if t == step else 2), t)
                pairs.append(((f * n_ctx + c) * n_tp + t, (f * n_ctx + other[0]) * n_tp + other[1]))
    return lax.ppermute(value, ("fsdp", "ctx", "tp"), pairs)


def near_shares(own, sizes):
    return flipped(own, sizes, 0), flipped(own, sizes, 1)


def plane_gather(own, sizes, near=None):
    one, two = near or near_shares(own, sizes)
    three = flipped(one, sizes, 1)
    mine = [own, one, two, three]
    return jnp.concatenate(mine + [flipped(block, sizes, 2) for block in mine])


def plane_scatter(kept, sent, sizes):
    total = kept + flipped(sent.astype(bf16), sizes, 2).astype(f32)
    for step in (1, 0):
        half = total.shape[0] // 2
        total = total[:half] + flipped(total[half:].astype(bf16), sizes, step).astype(f32)
    return total


def after(value, *others):
    return lax.optimization_barrier((value,) + others)[0]


def stage(*values):
    return lax.optimization_barrier(values)


def added(part, got):
    half = part.shape[0] // 2
    return part[:half] + got[:half].astype(f32), (part[half:] + got[half:].astype(f32)).astype(bf16)


def z_shifted(value, sizes, steps):
    n = sizes[0]
    return lax.ppermute(value, "fsdp", [(i, (i + steps) % n) for i in range(n)])


def packed(rest):
    return jnp.concatenate(jnp.split(rest, 128 // rest.shape[1]), axis=1)


def unpacked(full, width):
    return jnp.concatenate(jnp.split(full, full.shape[1] // width, axis=1))


def z_exchange(blocks, sizes):
    got = [blocks[0]] + [z_shifted(blocks[k], sizes, k) for k in range(1, sizes[0])]
    return jnp.concatenate(got)


def ctx_shares(own, sizes, core, near=None):
    one, two = near or near_shares(own, sizes)
    three = flipped(one, sizes, 1)
    return [own, jnp.where(core == 0, one, two), jnp.where(core == 0, two, one), three]


def product(left, right, dims, out_type=f32):
    return lax.dot_general(left, right, (dims, ((), ())), preferred_element_type=f32).astype(out_type)


NN = ((1,), (0,))
NT = ((1,), (1,))
TN = ((0,), (0,))


def seg_of(places, ends):
    return (places >= ends[0]).astype(jnp.int32) + (places >= ends[1]).astype(jnp.int32)


def conv_terms(values, conv, ends):
    rows = values.shape[0]
    places = lax.broadcasted_iota(jnp.int32, values.shape, 0)
    own_seg = seg_of(places, ends)
    shifted = [values]
    for lag in range(1, CONV):
        same = (places >= lag) & (seg_of(places - lag, ends) == own_seg)
        shifted.append(jnp.where(same, pltpu.roll(values, lag, 0), 0.0))
    mix = shifted[0] * conv[0:1]
    for lag in range(1, CONV):
        mix = mix + shifted[lag] * conv[lag : lag + 1]
    return shifted, mix


def block_mask(block, first, span, ends):
    query = block * BLOCK + lax.broadcasted_iota(jnp.int32, (BLOCK, span), 0)
    key = first * BLOCK + lax.broadcasted_iota(jnp.int32, (BLOCK, span), 1)
    return (seg_of(query, ends) == seg_of(key, ends)) & (key <= query) & (key > query - WINDOW)


def head_lanes(tile, head):
    lanes = lax.broadcasted_iota(jnp.int32, tile.shape, 1)
    return (lanes >= head * HEAD) & (lanes < (head + 1) * HEAD)


def window_weights(query, keys, allowed):
    scores = product(query, keys, NT) * (1.0 / math.sqrt(HEAD))
    scores = jnp.where(allowed, scores, masked_score)
    weights = jnp.exp(scores - jnp.max(scores, axis=-1, keepdims=True))
    return weights / jnp.sum(weights, axis=-1, keepdims=True)


def ends_of(lengths_ref, batch):
    first = lengths_ref[batch, 0]
    return (first, first + lengths_ref[batch, 1])


def attend_forward_kernel(lengths_ref, qkv_ref, conv_ref, out_ref, gated_ref):
    width = HEADS_EACH * HEAD
    group = qkv_ref.shape[0] // BATCHES
    conv = conv_ref[...]
    for batch in range(BATCHES):
        ends = ends_of(lengths_ref, batch)
        base = batch * group
        values = qkv_ref[base : base + group, 2 * width :].astype(f32)
        _, mix = conv_terms(values, conv, ends)
        gated_ref[...] = (values * (mix * jax.nn.sigmoid(mix))).astype(bf16)
        for block in range(group // BLOCK):
            first = max(block - 1, 0)
            span = (block + 1 - first) * BLOCK
            allowed = block_mask(block, first, span, ends)
            rows = slice(base + block * BLOCK, base + (block + 1) * BLOCK)
            for pair in range(width // 128):
                lanes = slice(pair * 128, (pair + 1) * 128)
                query = qkv_ref[rows, lanes]
                keys = qkv_ref[
                    base + first * BLOCK : base + first * BLOCK + span,
                    width + pair * 128 : width + (pair + 1) * 128,
                ]
                gated = gated_ref[first * BLOCK : first * BLOCK + span, lanes]
                blended = []
                for head in range(2):
                    chosen = jnp.where(head_lanes(query, head), query, jnp.zeros_like(query))
                    weights = window_weights(chosen, keys, allowed).astype(bf16)
                    blended.append(product(weights, gated, NN))
                merged = jnp.where(head_lanes(blended[0], 0), blended[0], blended[1])
                out_ref[rows, lanes] = merged.astype(bf16)


def attend_backward_kernel(
    lengths_ref, qkv_ref, grad_ref, conv_ref, out_ref, grad_conv_ref, gated_ref, keys_sum, gated_sum
):
    width = HEADS_EACH * HEAD
    group = qkv_ref.shape[0] // BATCHES
    conv = conv_ref[...]
    scaling = 1.0 / math.sqrt(HEAD)
    conv_sums = [jnp.zeros((1, width), f32) for _ in range(CONV)]
    for batch in range(BATCHES):
        ends = ends_of(lengths_ref, batch)
        base = batch * group
        values = qkv_ref[base : base + group, 2 * width :].astype(f32)
        shifted, mix = conv_terms(values, conv, ends)
        sigmoid = jax.nn.sigmoid(mix)
        gated_ref[...] = (values * (mix * sigmoid)).astype(bf16)
        keys_sum[...] = jnp.zeros_like(keys_sum)
        gated_sum[...] = jnp.zeros_like(gated_sum)
        for block in range(group // BLOCK):
            first = max(block - 1, 0)
            span = (block + 1 - first) * BLOCK
            allowed = block_mask(block, first, span, ends)
            rows = slice(base + block * BLOCK, base + (block + 1) * BLOCK)
            local = slice(first * BLOCK, first * BLOCK + span)
            for pair in range(width // 128):
                lanes = slice(pair * 128, (pair + 1) * 128)
                query = qkv_ref[rows, lanes]
                grad = grad_ref[rows, lanes]
                keys = qkv_ref[
                    base + first * BLOCK : base + first * BLOCK + span,
                    width + pair * 128 : width + (pair + 1) * 128,
                ]
                gated = gated_ref[local, lanes]
                grad_queries = []
                grad_keys = None
                grad_gated = None
                for head in range(2):
                    mine = head_lanes(query, head)
                    chosen = jnp.where(mine, query, jnp.zeros_like(query))
                    chosen_grad = jnp.where(mine, grad, jnp.zeros_like(grad))
                    weights = window_weights(chosen, keys, allowed)
                    grad_weights = product(chosen_grad, gated, NT)
                    inner = jnp.sum(weights * grad_weights, axis=-1, keepdims=True)
                    grad_scores = (weights * (grad_weights - inner)).astype(bf16)
                    grad_queries.append(product(grad_scores, keys, NN))
                    more_keys = product(grad_scores, chosen, TN)
                    more_gated = product(weights.astype(bf16), chosen_grad, TN)
                    grad_keys = more_keys if grad_keys is None else grad_keys + more_keys
                    grad_gated = more_gated if grad_gated is None else grad_gated + more_gated
                merged = jnp.where(head_lanes(grad_queries[0], 0), grad_queries[0], grad_queries[1])
                out_ref[rows, lanes] = (merged * scaling).astype(bf16)
                keys_sum[local, lanes] += grad_keys
                gated_sum[local, lanes] += grad_gated
        out_ref[base : base + group, width : 2 * width] = (keys_sum[...] * scaling).astype(bf16)
        grad_gated = gated_sum[...]
        grad_mix = grad_gated * values * (sigmoid * (1.0 + mix * (1.0 - sigmoid)))
        grad_values = grad_gated * (mix * sigmoid) + grad_mix * conv[0:1]
        places = lax.broadcasted_iota(jnp.int32, values.shape, 0)
        own_seg = seg_of(places, ends)
        conv_sums[0] = conv_sums[0] + jnp.sum(grad_mix * shifted[0], axis=0, keepdims=True)
        for lag in range(1, CONV):
            same = (places < group - lag) & (seg_of(places + lag, ends) == own_seg)
            later = jnp.where(same, pltpu.roll(grad_mix, group - lag, 0), 0.0)
            grad_values = grad_values + later * conv[lag : lag + 1]
            conv_sums[lag] = conv_sums[lag] + jnp.sum(grad_mix * shifted[lag], axis=0, keepdims=True)
        out_ref[base : base + group, 2 * width :] = grad_values.astype(bf16)
    for lag in range(CONV):
        grad_conv_ref[lag : lag + 1, :] = conv_sums[lag]


def weight_grad_kernel(*refs):
    out_ref = refs[-1]
    at = 0
    for left_ref, right_ref in zip(refs[:-1:2], refs[1:-1:2]):
        width = right_ref.shape[1]
        out_ref[:, at : at + width] = product(left_ref[...], right_ref[...], TN, bf16)
        at += width


def weight_grad(*pairs, step=256):
    rows, d_model = pairs[0][0].shape
    width = sum(right.shape[1] for _, right in pairs)
    specs = []
    for left, right in pairs:
        specs.append(pl.BlockSpec((rows, step), lambda i: (0, i)))
        specs.append(pl.BlockSpec((rows, right.shape[1]), lambda i: (0, 0)))
    return pl.pallas_call(
        weight_grad_kernel,
        grid=(d_model // step,),
        out_shape=jax.ShapeDtypeStruct((d_model, width), bf16),
        in_specs=specs,
        out_specs=pl.BlockSpec((step, width), lambda i: (i, 0)),
        compiler_params=pltpu.CompilerParams(vmem_limit_bytes=40 * 1024 * 1024),
        cost_estimate=pl.CostEstimate(
            flops=2 * rows * d_model * width,
            bytes_accessed=2 * (rows * d_model * len(pairs) + (rows + d_model) * width),
            transcendentals=0,
        ),
        name="weight_grad",
    )(*[operand for pair in pairs for operand in pair])


def mlp_grad_kernel(own_lanes, hidden_ref, grad_ref, pair_ref, inner_ref, out_ref, rest_ref):
    lead = out_ref.shape[1] - pair_ref.shape[1]
    pairs = product(hidden_ref[...], pair_ref[...], NN)
    down = product(grad_ref[...], inner_ref[...], NN)
    shared = down[:, lead : lead + 128]
    lanes = lax.broadcasted_iota(jnp.int32, shared.shape, 1)
    out_ref[:, :lead] = down[:, :lead].astype(bf16)
    out_ref[:, lead : lead + 128] = jnp.where(lanes < own_lanes, shared, pairs[:, :128]).astype(bf16)
    out_ref[:, lead + 128 :] = pairs[:, 128:].astype(bf16)
    rest_ref[...] = shared.astype(bf16)


def mlp_grad(hidden, grad, pair, inner, width, own_lanes, step=256):
    d_model, rows = hidden.shape
    return pl.pallas_call(
        functools.partial(mlp_grad_kernel, own_lanes),
        grid=(d_model // step,),
        out_shape=(
            jax.ShapeDtypeStruct((d_model, width), bf16),
            jax.ShapeDtypeStruct((d_model, 128), bf16),
        ),
        in_specs=[
            pl.BlockSpec((step, rows), lambda i: (i, 0)),
            pl.BlockSpec((step, rows), lambda i: (i, 0)),
            pl.BlockSpec(pair.shape, lambda i: (0, 0)),
            pl.BlockSpec(inner.shape, lambda i: (0, 0)),
        ],
        out_specs=(
            pl.BlockSpec((step, width), lambda i: (i, 0)),
            pl.BlockSpec((step, 128), lambda i: (i, 0)),
        ),
        compiler_params=pltpu.CompilerParams(vmem_limit_bytes=40 * 1024 * 1024),
        cost_estimate=pl.CostEstimate(
            flops=2 * rows * d_model * width,
            bytes_accessed=2 * (2 * rows * d_model + (rows + d_model) * width),
            transcendentals=0,
        ),
        name="mlp_grad",
    )(hidden, grad, pair, inner)


def feed_forward_kernel(ff, hidden_ref, grad_ref, weight_ref, rest_ref, inner_ref, pair_ref):
    own = weight_ref.shape[1] - 2 * ff
    first = own // 128 * 128
    lead = own - first
    both = product(hidden_ref[...], weight_ref[:, first:], NN)
    gate_act, upper = both[:, lead : lead + ff], both[:, lead + ff :]
    grad = grad_ref[...]
    grad_inner = jnp.concatenate(
        [product(grad, weight_ref[:, :own], NN), product(grad, rest_ref[...], NN)], axis=1
    )
    sigmoid = jax.nn.sigmoid(gate_act)
    silu = gate_act * sigmoid
    rows, spare = inner_ref.shape[0], inner_ref.shape[1] - ff
    inner_ref[...] = jnp.concatenate(
        [(silu * upper).astype(bf16), jnp.zeros((rows, spare), bf16)], axis=1
    )
    grad_gate = grad_inner * upper * (sigmoid * (1.0 + gate_act * (1.0 - sigmoid)))
    pair_ref[...] = jnp.concatenate(
        [
            jnp.zeros((rows, lead), bf16),
            grad_gate.astype(bf16),
            (grad_inner * silu).astype(bf16),
        ],
        axis=1,
    )


def feed_forward(hidden, grad, weight, rest, ff, step=256):
    rows, d_model = hidden.shape
    width = weight.shape[1]
    first = (width - 2 * ff) // 128 * 128
    padded = -(-ff // 128) * 128
    return pl.pallas_call(
        functools.partial(feed_forward_kernel, ff),
        grid=(rows // step,),
        out_shape=(
            jax.ShapeDtypeStruct((rows, padded), bf16),
            jax.ShapeDtypeStruct((rows, width - first), bf16),
        ),
        in_specs=[
            pl.BlockSpec((step, d_model), lambda i: (i, 0)),
            pl.BlockSpec((step, d_model), lambda i: (i, 0)),
            pl.BlockSpec((d_model, width), lambda i: (0, 0)),
            pl.BlockSpec(rest.shape, lambda i: (0, 0)),
        ],
        out_specs=(
            pl.BlockSpec((step, padded), lambda i: (i, 0)),
            pl.BlockSpec((step, width - first), lambda i: (i, 0)),
        ),
        compiler_params=pltpu.CompilerParams(vmem_limit_bytes=48 * 1024 * 1024),
        cost_estimate=pl.CostEstimate(
            flops=6 * rows * d_model * ff,
            bytes_accessed=2 * (2 * rows * d_model + 3 * (d_model + rows) * ff),
            transcendentals=rows * ff,
        ),
        name="feed_forward",
    )(hidden, grad, weight, rest)


def mlp_placed_kernel(ff, index_ref, *refs):
    mains, rests = refs[:4], refs[4:8]
    pair_ref, down_ref, columns = refs[8:]
    own = mains[0].shape[1] - 2 * ff
    for k in range(4):
        piece = index_ref[0] ^ k
        columns[piece, :, :own] = mains[k][:, :own].astype(f32)
        if rests[k].shape[1] == ff - own:
            columns[piece, :, own:ff] = rests[k][...].astype(f32)
        else:
            for step in range(rests[k].shape[1] // (ff - own)):

                @pl.when(pl.program_id(0) == step)
                def _():
                    at = step * (ff - own)
                    columns[piece, :, own:ff] = rests[k][:, at : at + ff - own].astype(f32)
        columns[piece, :, ff:] = mains[k][:, own:].astype(f32)
    for out, at in ((pair_ref.at[0], ff), (pair_ref.at[1], 2 * ff), (down_ref.at[0], 0)):
        out[...] = jnp.concatenate([columns[p, :, at : at + ff] for p in range(4)], axis=1)


def mlp_placed(mains, rests, index, ff, steps):
    rows, width = mains[0].shape
    block, total = rows // steps, 4 * ff
    if steps == 1:
        rests = [unpacked(rest, ff - (width - 2 * ff)) for rest in rests]
    return pl.pallas_call(
        functools.partial(mlp_placed_kernel, ff),
        grid=(steps,),
        out_shape=[
            jax.ShapeDtypeStruct((2, rows, total), f32),
            jax.ShapeDtypeStruct((1, rows, total), f32),
        ],
        in_specs=[SMEM]
        + [pl.BlockSpec((block, width), lambda i: (i, 0))] * 4
        + [pl.BlockSpec(rests[0].shape, lambda i: (0, 0))] * 4,
        out_specs=[
            pl.BlockSpec((2, block, total), lambda i: (0, i, 0)),
            pl.BlockSpec((1, block, total), lambda i: (0, i, 0)),
        ],
        scratch_shapes=[pltpu.VMEM((4, block, 3 * ff), f32)],
        compiler_params=pltpu.CompilerParams(vmem_limit_bytes=40 * 1024 * 1024),
        cost_estimate=pl.CostEstimate(
            flops=0, bytes_accessed=20 * rows * total, transcendentals=0
        ),
        name="mlp_placed",
    )(index.reshape(1).astype(jnp.int32), *mains, *rests)


def placed_kernel(each, total, counts, index_ref, *refs):
    n_parts = len(refs) - len(counts)
    outs = refs[n_parts:]
    for piece in range(total // each + (total % each > 0)):
        start = min(piece * each, total - each)
        shared = piece * each - start
        for k in range(n_parts):

            @pl.when((index_ref[0] ^ k) == piece)
            def _():
                at = 0
                for out, count in zip(outs, counts):
                    for i in range(count):
                        part = refs[k][:, at + shared : at + each].astype(f32)
                        at += each
                        out[i, :, start + shared : start + each] = part


def placed(parts, index, each, total, counts, steps):
    rows = parts[0].shape[0]
    block = rows // steps
    out_shape = [jax.ShapeDtypeStruct((count, rows, total), f32) for count in counts]
    out_specs = [pl.BlockSpec((count, block, total), lambda i: (0, i, 0)) for count in counts]
    width = parts[0].shape[1]
    return pl.pallas_call(
        functools.partial(placed_kernel, each, total, counts),
        grid=(steps,),
        out_shape=out_shape,
        in_specs=[SMEM] + [pl.BlockSpec((block, width), lambda i: (i, 0))] * len(parts),
        out_specs=out_specs,
        compiler_params=pltpu.CompilerParams(vmem_limit_bytes=40 * 1024 * 1024),
        cost_estimate=pl.CostEstimate(
            flops=0, bytes_accessed=rows * width * len(parts) * 6, transcendentals=0
        ),
        name="placed",
    )(index.reshape(1).astype(jnp.int32), *parts)


def last_placed_kernel(count, place_ref, *refs):
    *parts, _, _, first_ref, second_ref = refs
    for i in range(count):
        first_ref[i] = parts[i][...].astype(f32)
    second_ref[0] = parts[count][...].astype(f32)


def last_placed(part, index, each, total, first, second):
    rows, count = part.shape[0], first.shape[0]
    tiles, last = each // 128, total // 128 - 1

    def source(i):
        shift = tiles * (last // tiles + 1) - 1 - last
        return lambda j, ref: (
            0,
            i * tiles + jnp.where(ref[0] == last // tiles, jnp.minimum(j + shift, tiles - 1), j),
        )

    def target(j, ref):
        return (0, 0, jnp.minimum(ref[0] * tiles + j, last))

    out_specs = [pl.BlockSpec((n, rows, 128), target) for n in (count, 1)]
    return pl.pallas_call(
        functools.partial(last_placed_kernel, count),
        grid_spec=pltpu.PrefetchScalarGridSpec(
            num_scalar_prefetch=1,
            grid=(tiles,),
            in_specs=[pl.BlockSpec((rows, 128), source(i)) for i in range(count + 1)]
            + [pl.BlockSpec(memory_space=pl.ANY)] * 2,
            out_specs=out_specs,
        ),
        out_shape=[jax.ShapeDtypeStruct(first.shape, f32), jax.ShapeDtypeStruct(second.shape, f32)],
        input_output_aliases={count + 2: 0, count + 3: 1},
        name="last_placed",
    )(index.reshape(1).astype(jnp.int32), *[part] * (count + 1), first, second)


def at_home_kernel(undo_ref, *refs):
    *blocks, first_ref, second_ref, rows = refs
    each = blocks[0].shape[0]
    for k, block in enumerate(blocks):
        rows[k * each : (k + 1) * each, :] = block[...]
    d_model = first_ref.shape[2]
    for batch in range(first_ref.shape[0]):
        undo = undo_ref[batch * first_ref.shape[1] : (batch + 1) * first_ref.shape[1], :]
        first_ref[batch] = product(undo, rows[:, :d_model], NN, bf16)
        second_ref[batch] = product(undo, rows[:, d_model:], NN, bf16)


def at_home(undo, blocks, batches, d_model):
    rows = undo.shape[0]
    out = jax.ShapeDtypeStruct((batches, rows // batches, d_model), bf16)
    return pl.pallas_call(
        at_home_kernel,
        out_shape=(out, out),
        in_specs=[VMEM] * (1 + len(blocks)),
        out_specs=(VMEM, VMEM),
        scratch_shapes=[pltpu.VMEM((rows, 2 * d_model), bf16)],
        compiler_params=pltpu.CompilerParams(vmem_limit_bytes=32 * 1024 * 1024),
        cost_estimate=pl.CostEstimate(flops=0, bytes_accessed=10_000_000, transcendentals=0),
        name="at_home",
    )(undo, *blocks)


VMEM = pl.BlockSpec(memory_space=pltpu.VMEM)
SMEM = pl.BlockSpec(memory_space=pltpu.SMEM)


def attend_forward(lengths, qkv, conv):
    rows, width = qkv.shape[0], HEADS_EACH * HEAD
    return pl.pallas_call(
        attend_forward_kernel,
        out_shape=jax.ShapeDtypeStruct((rows, width), bf16),
        in_specs=[SMEM, VMEM, VMEM],
        out_specs=VMEM,
        scratch_shapes=[pltpu.VMEM((rows // BATCHES, width), bf16)],
        compiler_params=pltpu.CompilerParams(vmem_limit_bytes=32 * 1024 * 1024),
        cost_estimate=pl.CostEstimate(flops=0, bytes_accessed=20_000_000, transcendentals=0),
        name="attend_forward",
    )(lengths, qkv, conv)


def attend_backward(lengths, qkv, grad, conv):
    rows, width = qkv.shape[0], HEADS_EACH * HEAD
    group = rows // BATCHES
    return pl.pallas_call(
        attend_backward_kernel,
        out_shape=(
            jax.ShapeDtypeStruct((rows, 3 * width), bf16),
            jax.ShapeDtypeStruct((CONV, width), f32),
        ),
        in_specs=[SMEM, VMEM, VMEM, VMEM],
        out_specs=(VMEM, VMEM),
        scratch_shapes=[
            pltpu.VMEM((group, width), bf16),
            pltpu.VMEM((group, width), f32),
            pltpu.VMEM((group, width), f32),
        ],
        compiler_params=pltpu.CompilerParams(vmem_limit_bytes=32 * 1024 * 1024),
        cost_estimate=pl.CostEstimate(flops=0, bytes_accessed=50_000_000, transcendentals=0),
        name="attend_backward",
    )(lengths, qkv, grad, conv)


def part_of(total, each, index):
    start = jnp.minimum(index * each, total - each)
    return start, index * each - start


def per_device(
    tokens,
    cotangent,
    attn_in,
    attn_out,
    gate_up,
    down_proj,
    conv_weight,
    norm_gains,
    deal_order,
    lengths,
):
    sizes = tuple(lax.axis_size(axis) for axis in ("fsdp", "ctx", "tp"))
    n_fsdp, n_ctx, n_tp = sizes
    workers = n_fsdp * n_ctx
    f, c, t = (lax.axis_index(axis) for axis in ("fsdp", "ctx", "tp"))
    me = f * n_ctx + c
    tok_rows, d_model = tokens.shape[1:]
    d_own = attn_in.shape[1]
    heads_all = attn_in.shape[2]
    width = HEADS_EACH * HEAD
    ff_all = gate_up.shape[2]
    ff = ff_all // n_ctx
    from_each = tok_rows // n_fsdp
    half = from_each // n_tp
    group = n_ctx * tok_rows
    plane = BATCHES * group

    start, shared = part_of(heads_all, width, c)
    sliced = lax.dynamic_slice_in_dim(attn_in, start, width, 2)
    out_part = lax.dynamic_slice_in_dim(attn_out, start, width, 0)
    out_part = jnp.where(jnp.arange(width)[:, None] >= shared, out_part, jnp.zeros_like(out_part))
    attn_own = jnp.concatenate([sliced[0], sliced[1], sliced[2], out_part.T], axis=1)
    own_down = 3 * ff // 128 * 128 - 2 * ff
    sliced = lax.dynamic_slice_in_dim(gate_up, c * ff, ff, 2)
    down_own = lax.dynamic_slice_in_dim(down_proj, c * ff, ff, 0).T
    mlp_own = jnp.concatenate([down_own[:, :own_down], sliced[0], sliced[1]], axis=1)
    rest_own = down_own[:, own_down:]
    rest_width = ff - own_down
    attn_w = lax.all_gather(attn_own, "fsdp", axis=0, tiled=True)
    mlp_w = lax.all_gather(after(mlp_own, attn_own), "fsdp", axis=0, tiled=True)
    down_w, pair_w = mlp_w[:, :own_down], mlp_w[:, own_down // 128 * 128 :]
    qkv_w, out_w = attn_w[:, : 3 * width], attn_w[:, 3 * width :]

    small = jnp.concatenate(
        [
            deal_order.reshape(-1).astype(f32),
            norm_gains.reshape(-1).astype(f32),
            conv_weight.reshape(-1).astype(f32),
        ]
    )
    small = after(small, attn_own)
    small = lax.all_to_all(
        jnp.broadcast_to(small[None], (workers,) + small.shape),
        ("fsdp", "ctx"),
        split_axis=0,
        concat_axis=0,
        tiled=True,
    )
    n_order, n_gain = deal_order.size, norm_gains.size
    orders = small[:, :n_order].astype(jnp.int32).reshape(workers, BATCHES, tok_rows)
    by_fsdp = small.reshape(n_fsdp, n_ctx, -1)[:, 0]
    gains = by_fsdp[:, n_order : n_order + n_gain].reshape(n_fsdp, 2, -1)
    gains = jnp.transpose(gains, (1, 0, 2)).reshape(2, 1, d_model)
    conv = by_fsdp[:, n_order + n_gain :].reshape(n_fsdp, CONV, -1)
    conv = jnp.transpose(conv, (1, 0, 2)).reshape(CONV, heads_all)
    conv = lax.dynamic_slice_in_dim(conv, start, width, 1)

    given = me * tok_rows + jnp.arange(tok_rows, dtype=jnp.int32)
    by_batch = jnp.transpose(orders, (1, 0, 2)).reshape(BATCHES, -1)
    planes = jnp.arange(workers * tok_rows, dtype=jnp.int32) // group
    to_plane = jnp.sum(
        jnp.where(by_batch[:, None, :] == given[None, :, None], planes[None, None, :], 0), axis=2
    )
    earlier = jnp.arange(tok_rows)[None, :] < jnp.arange(tok_rows)[:, None]
    slot = jnp.sum(
        ((to_plane[:, None, :] == to_plane[:, :, None]) & earlier[None]).astype(jnp.int32), axis=2
    )
    place = ((slot // half) * n_fsdp + (to_plane - f) % n_fsdp) * (BATCHES * half) + slot % half
    place = place + jnp.arange(BATCHES, dtype=jnp.int32)[:, None] * half
    place = place.reshape(-1)
    sent_rows = BATCHES * tok_rows // n_tp
    wire = t * sent_rows + jnp.arange(sent_rows, dtype=jnp.int32)
    choose = (place[None, :] == wire[:, None]).astype(bf16)
    both = jnp.concatenate([wire, (1 - t) * sent_rows + jnp.arange(sent_rows, dtype=jnp.int32)])
    undo = (place[:, None] == both[None, :]).astype(bf16)

    def to_planes(rows):
        picked = product(choose, rows.reshape(-1, d_model), NN, bf16)
        return z_exchange(jnp.split(picked, n_fsdp), sizes)

    def to_home(rows):
        blocks = jnp.split(rows, n_fsdp)
        return [blocks[0]] + [z_shifted(blocks[k], sizes, n_fsdp - k) for k in range(1, n_fsdp)]

    own_x = to_planes(tokens).astype(f32)

    dealt = lax.dynamic_slice_in_dim(orders, f * n_ctx, n_ctx, 0)
    dealt = jnp.transpose(dealt, (1, 0, 2)).reshape(BATCHES, group)
    giver = dealt // tok_rows
    rank = jnp.sum(
        (
            (giver[:, None, :] == giver[:, :, None]) & (dealt[:, None, :] < dealt[:, :, None])
        ).astype(jnp.int32),
        axis=2,
    )
    core = rank // half
    away = (giver % n_ctx) ^ c
    swapped = jnp.where(core == 0, away, (away % 2) * 2 + away // 2)
    block = jnp.where(core == t, 0, n_ctx) + swapped
    arrival = block * (plane // (n_ctx * n_tp)) + (f - giver // n_ctx) % n_fsdp * (BATCHES * half)
    arrival = arrival + jnp.arange(BATCHES, dtype=jnp.int32)[:, None] * half + rank % half
    deal = (arrival.reshape(-1)[:, None] == jnp.arange(plane, dtype=jnp.int32)[None, :]).astype(bf16)

    first_scale = lax.rsqrt(jnp.mean(own_x * own_x, axis=-1, keepdims=True) + epsilon)
    hidden = plane_gather((own_x * first_scale * gains[0]).astype(bf16), sizes)
    own_lengths = lengths[:, 0]
    hidden, given_g, rest_own = stage(hidden, cotangent, packed(rest_own))
    own_g = to_planes(given_g)
    if n_fsdp > 4:
        rests = lax.all_gather(rest_own, "fsdp")
        rest_w = jnp.concatenate([unpacked(rests[k], rest_width) for k in range(n_fsdp)])
    else:
        rest_w = jnp.zeros((d_model, rest_width), bf16)
        for k in range(n_fsdp):
            part = unpacked(z_shifted(rest_own, sizes, k) if k else rest_own, rest_width)
            rest_w = lax.dynamic_update_slice_in_dim(rest_w, part, (f - k) % n_fsdp * d_own, 0)
    qkv = product(deal, product(hidden, qkv_w, NN, bf16), NN, bf16)
    grad_dealt = plane_gather(after(own_g, qkv), sizes)
    attended = product(deal, attend_forward(own_lengths, qkv, conv), TN, bf16)
    kept = plane // 2
    branch = plane_scatter(
        product(attended[:kept], out_w, NT),
        product(attended[kept:], out_w, NT, bf16),
        sizes,
    )
    resid = own_x + branch

    second_scale = lax.rsqrt(jnp.mean(resid * resid, axis=-1, keepdims=True) + epsilon)
    hidden_two = plane_gather((resid * second_scale * gains[1]).astype(bf16), sizes)
    hidden_two_turned, grad_dealt_turned = after((hidden_two.T, grad_dealt.T))
    inner, grad_pair = feed_forward(
        after(hidden_two, hidden_two_turned, grad_dealt_turned), grad_dealt, mlp_w, rest_w, ff
    )
    grad_mlp_w, grad_rest_w = mlp_grad(
        hidden_two_turned, grad_dealt_turned, grad_pair, inner, mlp_w.shape[1], own_down % 128
    )
    grad_mlp_w, grad_rest_w, grad_pair, inner = stage(grad_mlp_w, grad_rest_w, grad_pair, inner)
    grad_mlp = lax.psum_scatter(grad_mlp_w, "fsdp", scatter_dimension=0, tiled=True)
    grad_rest_w = grad_rest_w[:, own_down % 128 :][:, :rest_width]
    rests = [
        packed(lax.dynamic_slice_in_dim(grad_rest_w, (f + k) % n_fsdp * d_own, d_own, 0))
        for k in range(n_fsdp)
    ]

    sent = product(grad_pair[kept:], pair_w, NT, bf16)
    sent, grad_pair = stage(sent, grad_pair)

    got = flipped(sent, sizes, 2)
    part = product(grad_pair[:kept], pair_w, NT)
    got, part = stage(got, part)
    part, sent = added(part, got)
    part, sent, inner = stage(part, sent, inner)

    got = flipped(sent, sizes, 1)
    lift = product(inner[:, :own_down], down_w, NT) + product(inner[:, own_down:ff], rest_w, NT)
    lift, lift_sent = lift[:kept], lift[kept:].astype(bf16)
    got, part, lift_sent, lift = stage(got, part, lift_sent, lift)
    part, sent = added(part, got)
    part, sent, lift_sent, lift = stage(part, sent, lift_sent, lift)

    got = flipped(sent, sizes, 0)
    lift_got = flipped(lift_sent, sizes, 2)
    grad_two = part + got.astype(f32)
    normed = resid * second_scale
    scaled = grad_two * gains[1]
    grad_resid = own_g.astype(f32) + second_scale * (
        scaled - normed * jnp.mean(scaled * normed, axis=-1, keepdims=True)
    )
    grad_own = grad_resid.astype(bf16)
    lift, lift_sent = added(lift, lift_got)
    grad_own, lift, lift_sent = stage(grad_own, lift, lift_sent)

    near = near_shares(grad_own, sizes)
    grad_own, near = stage(grad_own, near)
    grad_branch = plane_gather(grad_own, sizes, near)
    grad_branch, lift_sent = stage(grad_branch, lift_sent)

    lift_got = flipped(lift_sent, sizes, 1)
    grad_attended = product(deal, product(grad_branch, out_w, NN, bf16), NN, bf16)
    grad_proj, grad_conv = attend_backward(own_lengths, qkv, grad_attended, conv)
    lift_got, lift, grad_proj = stage(lift_got, lift, grad_proj)
    lift, lift_sent = added(lift, lift_got)
    lift, lift_sent, grad_proj = stage(lift, lift_sent, grad_proj)

    lift_got = flipped(lift_sent, sizes, 0)
    grad_proj = product(deal, grad_proj, TN, bf16)
    sent = product(grad_proj[kept:], qkv_w, NT, bf16)
    lift_got, grad_proj, sent = stage(lift_got, grad_proj, sent)
    result = (resid + (lift + lift_got.astype(f32))).astype(bf16)

    got = flipped(sent, sizes, 2)
    part = product(grad_proj[:kept], qkv_w, NT)
    got, part = stage(got, part)
    part, sent = added(part, got)
    part, sent, grad_proj = stage(part, sent, grad_proj)

    got = flipped(sent, sizes, 1)
    grad_attn_w = weight_grad((hidden, grad_proj), (grad_branch, attended))
    got, part, grad_attn_w = stage(got, part, grad_attn_w)
    grad_attn = lax.psum_scatter(grad_attn_w, "fsdp", scatter_dimension=0, tiled=True)
    part, sent = added(part, got)

    got_last = flipped(sent, sizes, 0)
    grad_hidden = part + got_last.astype(f32)
    normed = own_x * first_scale
    scaled = grad_hidden * gains[0]
    grad_x = grad_resid + first_scale * (
        scaled - normed * jnp.mean(scaled * normed, axis=-1, keepdims=True)
    )
    grad_x = grad_x.astype(bf16)

    taps = jnp.concatenate(jnp.split(grad_conv, width // 128, axis=1)).astype(bf16)
    taps, grad_mlp, _, *rests = stage(taps, grad_mlp, got_last, *rests)
    little = [jnp.concatenate([rest, taps]) for rest in rests]
    little = sum(
        [z_shifted(little[k], sizes, k).astype(f32) for k in range(1, n_fsdp)], little[0].astype(f32)
    ).astype(bf16)

    steps = 128 // rest_width if d_own * rest_width % (128 * 16) == 0 else 1

    def gain_part(own, grad, each, skipped):
        columns = own.shape[1]
        counted = (jnp.arange(columns) % each) >= skipped
        terms = own.astype(f32) * grad[:, :columns].astype(f32)
        return jnp.sum(jnp.where(counted[None, :], terms, 0.0), axis=1)

    mlp_shares = ctx_shares(grad_mlp, sizes, t)
    little_shares = ctx_shares(little, sizes, t)
    rest_rows = d_own * rest_width // 128
    rest_shares = [share[:rest_rows] for share in little_shares]
    taps = [share[rest_rows:].astype(f32) for share in little_shares]
    taps = [jnp.concatenate(jnp.split(tap, width // 128), axis=1) for tap in taps]
    first_shared = n_ctx * width - heads_all
    taps = jnp.stack(taps)
    taps = [lax.dynamic_index_in_dim(taps, c ^ k, 0, False) for k in range(n_ctx)]
    taps = jnp.concatenate(taps[:-1] + [taps[-1][:, first_shared:]], axis=1)
    grad_conv = lax.dynamic_slice_in_dim(taps, f * (heads_all // n_fsdp), heads_all // n_fsdp, 1)
    gain_two = gain_part(mlp_own[:, own_down:], grad_mlp[:, own_down:], ff, 0)
    rows_back = jnp.concatenate([result, grad_x], axis=1)
    grad_attn, rows_back, gain_two, grad_conv, rest_shares = stage(
        grad_attn, rows_back, gain_two, grad_conv, rest_shares
    )

    near = near_shares(grad_attn, sizes)
    home = to_home(rows_back)
    gain_one = gain_part(attn_own[:, : 3 * width], grad_attn, width, shared)
    gains_grad = jnp.stack([gain_one, gain_two])
    gains_grad = gains_grad + flipped(gains_grad, sizes, 2)
    grad_gate_up, grad_down = mlp_placed(mlp_shares, rest_shares, c, ff, steps)
    near, gains_grad, grad_gate_up, grad_down = stage(near, gains_grad, grad_gate_up, grad_down)

    attn_shares = ctx_shares(grad_attn, sizes, t, near)
    grad_attn_in, grad_attn_out = placed(attn_shares[:3], c, width, heads_all, (3, 1), steps)
    for step in (0, 1):
        gains_grad = gains_grad + flipped(gains_grad, sizes, step)
    activations, input_grad = at_home(
        undo, home + [flipped(block, sizes, 2) for block in home], BATCHES, d_model
    )
    grad_gains = gains_grad / norm_gains.astype(f32)
    grad_attn_in, grad_attn_out = last_placed(
        attn_shares[3], c ^ 3, width, heads_all, grad_attn_in, grad_attn_out
    )
    return (
        activations,
        input_grad,
        grad_attn_in,
        grad_attn_out[0].T,
        grad_gate_up,
        grad_down[0].T,
        grad_conv[None],
        grad_gains,
    )


def solution(mesh):
    return jax.shard_map(
        per_device,
        mesh=mesh,
        in_specs=(
            P(None, ("fsdp", "ctx"), None),
            P(None, ("fsdp", "ctx"), None),
            P(None, "fsdp", "tp"),
            P("tp", "fsdp"),
            P(None, "fsdp", "tp"),
            P("tp", "fsdp"),
            P("tp", None, "fsdp"),
            P(None, "fsdp"),
            P(None, ("fsdp", "ctx")),
            P(None, "fsdp", None),
        ),
        out_specs=(
            P(None, ("fsdp", "ctx"), None),
            P(None, ("fsdp", "ctx"), None),
            P(None, "fsdp", "tp"),
            P("tp", "fsdp"),
            P(None, "fsdp", "tp"),
            P("tp", "fsdp"),
            P("tp", None, "fsdp"),
            P(None, "fsdp"),
        ),
        check_vma=False,
    )
```

```python
import functools
import math

import jax
import jax.numpy as jnp
from jax import lax
from jax.experimental import pallas as pl
from jax.experimental.pallas import tpu as pltpu
from jax.sharding import PartitionSpec as P

HEAD = 64
WINDOW = 64
CONV = 3
BATCHES = 2
BLOCK = 128
HEADS_EACH = 4

epsilon = 1e-06
masked_score = -1e30
f32 = jnp.float32
bf16 = jnp.bfloat16


def flipped(value, sizes, step):
    n_fsdp, n_ctx, n_tp = sizes
    pairs = []
    for f in range(n_fsdp):
        for c in range(n_ctx):
            for t in range(n_tp):
                if step == 2:
                    other = (c, t ^ 1)
                else:
                    other = (c ^ (1 if t == step else 2), t)
                pairs.append(((f * n_ctx + c) * n_tp + t, (f * n_ctx + other[0]) * n_tp + other[1]))
    return lax.ppermute(value, ("fsdp", "ctx", "tp"), pairs)


def near_shares(own, sizes):
    return flipped(own, sizes, 0), flipped(own, sizes, 1)


def plane_gather(own, sizes, near=None):
    one, two = near or near_shares(own, sizes)
    three = flipped(one, sizes, 1)
    mine = [own, one, two, three]
    return jnp.concatenate(mine + [flipped(block, sizes, 2) for block in mine])


def plane_scatter(kept, sent, sizes):
    total = kept + flipped(sent.astype(bf16), sizes, 2).astype(f32)
    for step in (1, 0):
        half = total.shape[0] // 2
        total = total[:half] + flipped(total[half:].astype(bf16), sizes, step).astype(f32)
    return total


def after(value, *others):
    return lax.optimization_barrier((value,) + others)[0]


def stage(*values):
    return lax.optimization_barrier(values)


def added(part, got):
    half = part.shape[0] // 2
    return part[:half] + got[:half].astype(f32), (part[half:] + got[half:].astype(f32)).astype(bf16)


def z_shifted(value, sizes, steps):
    n = sizes[0]
    return lax.ppermute(value, "fsdp", [(i, (i + steps) % n) for i in range(n)])


def packed(rest):
    return jnp.concatenate(jnp.split(rest, 128 // rest.shape[1]), axis=1)


def unpacked(full, width):
    return jnp.concatenate(jnp.split(full, full.shape[1] // width, axis=1))


def z_exchange(blocks, sizes):
    got = [blocks[0]] + [z_shifted(blocks[k], sizes, k) for k in range(1, sizes[0])]
    return jnp.concatenate(got)


def ctx_shares(own, sizes, core, near=None):
    one, two = near or near_shares(own, sizes)
    three = flipped(one, sizes, 1)
    return [own, jnp.where(core == 0, one, two), jnp.where(core == 0, two, one), three]


def product(left, right, dims, out_type=f32):
    return lax.dot_general(left, right, (dims, ((), ())), preferred_element_type=f32).astype(out_type)


NN = ((1,), (0,))
NT = ((1,), (1,))
TN = ((0,), (0,))


def seg_of(places, ends):
    return (places >= ends[0]).astype(jnp.int32) + (places >= ends[1]).astype(jnp.int32)


def conv_terms(values, conv, ends):
    rows = values.shape[0]
    places = lax.broadcasted_iota(jnp.int32, values.shape, 0)
    own_seg = seg_of(places, ends)
    shifted = [values]
    for lag in range(1, CONV):
        same = (places >= lag) & (seg_of(places - lag, ends) == own_seg)
        shifted.append(jnp.where(same, pltpu.roll(values, lag, 0), 0.0))
    mix = shifted[0] * conv[0:1]
    for lag in range(1, CONV):
        mix = mix + shifted[lag] * conv[lag : lag + 1]
    return shifted, mix


def block_mask(block, first, span, ends):
    query = block * BLOCK + lax.broadcasted_iota(jnp.int32, (BLOCK, span), 0)
    key = first * BLOCK + lax.broadcasted_iota(jnp.int32, (BLOCK, span), 1)
    return (seg_of(query, ends) == seg_of(key, ends)) & (key <= query) & (key > query - WINDOW)


def head_lanes(tile, head):
    lanes = lax.broadcasted_iota(jnp.int32, tile.shape, 1)
    return (lanes >= head * HEAD) & (lanes < (head + 1) * HEAD)


def window_weights(query, keys, allowed):
    scores = product(query, keys, NT) * (1.0 / math.sqrt(HEAD))
    scores = jnp.where(allowed, scores, masked_score)
    weights = jnp.exp(scores - jnp.max(scores, axis=-1, keepdims=True))
    return weights / jnp.sum(weights, axis=-1, keepdims=True)


def ends_of(lengths_ref, batch):
    first = lengths_ref[batch, 0]
    return (first, first + lengths_ref[batch, 1])


def attend_forward_kernel(lengths_ref, qkv_ref, conv_ref, out_ref, gated_ref):
    width = HEADS_EACH * HEAD
    group = qkv_ref.shape[0] // BATCHES
    conv = conv_ref[...]
    for batch in range(BATCHES):
        ends = ends_of(lengths_ref, batch)
        base = batch * group
        values = qkv_ref[base : base + group, 2 * width :].astype(f32)
        _, mix = conv_terms(values, conv, ends)
        gated_ref[...] = (values * (mix * jax.nn.sigmoid(mix))).astype(bf16)
        for block in range(group // BLOCK):
            first = max(block - 1, 0)
            span = (block + 1 - first) * BLOCK
            allowed = block_mask(block, first, span, ends)
            rows = slice(base + block * BLOCK, base + (block + 1) * BLOCK)
            for pair in range(width // 128):
                lanes = slice(pair * 128, (pair + 1) * 128)
                query = qkv_ref[rows, lanes]
                keys = qkv_ref[
                    base + first * BLOCK : base + first * BLOCK + span,
                    width + pair * 128 : width + (pair + 1) * 128,
                ]
                gated = gated_ref[first * BLOCK : first * BLOCK + span, lanes]
                blended = []
                for head in range(2):
                    chosen = jnp.where(head_lanes(query, head), query, jnp.zeros_like(query))
                    weights = window_weights(chosen, keys, allowed).astype(bf16)
                    blended.append(product(weights, gated, NN))
                merged = jnp.where(head_lanes(blended[0], 0), blended[0], blended[1])
                out_ref[rows, lanes] = merged.astype(bf16)


def attend_backward_kernel(
    lengths_ref, qkv_ref, grad_ref, conv_ref, out_ref, grad_conv_ref, gated_ref, keys_sum, gated_sum
):
    width = HEADS_EACH * HEAD
    group = qkv_ref.shape[0] // BATCHES
    conv = conv_ref[...]
    scaling = 1.0 / math.sqrt(HEAD)
    conv_sums = [jnp.zeros((1, width), f32) for _ in range(CONV)]
    for batch in range(BATCHES):
        ends = ends_of(lengths_ref, batch)
        base = batch * group
        values = qkv_ref[base : base + group, 2 * width :].astype(f32)
        shifted, mix = conv_terms(values, conv, ends)
        sigmoid = jax.nn.sigmoid(mix)
        gated_ref[...] = (values * (mix * sigmoid)).astype(bf16)
        keys_sum[...] = jnp.zeros_like(keys_sum)
        gated_sum[...] = jnp.zeros_like(gated_sum)
        for block in range(group // BLOCK):
            first = max(block - 1, 0)
            span = (block + 1 - first) * BLOCK
            allowed = block_mask(block, first, span, ends)
            rows = slice(base + block * BLOCK, base + (block + 1) * BLOCK)
            local = slice(first * BLOCK, first * BLOCK + span)
            for pair in range(width // 128):
                lanes = slice(pair * 128, (pair + 1) * 128)
                query = qkv_ref[rows, lanes]
                grad = grad_ref[rows, lanes]
                keys = qkv_ref[
                    base + first * BLOCK : base + first * BLOCK + span,
                    width + pair * 128 : width + (pair + 1) * 128,
                ]
                gated = gated_ref[local, lanes]
                grad_queries = []
                grad_keys = None
                grad_gated = None
                for head in range(2):
                    mine = head_lanes(query, head)
                    chosen = jnp.where(mine, query, jnp.zeros_like(query))
                    chosen_grad = jnp.where(mine, grad, jnp.zeros_like(grad))
                    weights = window_weights(chosen, keys, allowed)
                    grad_weights = product(chosen_grad, gated, NT)
                    inner = jnp.sum(weights * grad_weights, axis=-1, keepdims=True)
                    grad_scores = (weights * (grad_weights - inner)).astype(bf16)
                    grad_queries.append(product(grad_scores, keys, NN))
                    more_keys = product(grad_scores, chosen, TN)
                    more_gated = product(weights.astype(bf16), chosen_grad, TN)
                    grad_keys = more_keys if grad_keys is None else grad_keys + more_keys
                    grad_gated = more_gated if grad_gated is None else grad_gated + more_gated
                merged = jnp.where(head_lanes(grad_queries[0], 0), grad_queries[0], grad_queries[1])
                out_ref[rows, lanes] = (merged * scaling).astype(bf16)
                keys_sum[local, lanes] += grad_keys
                gated_sum[local, lanes] += grad_gated
        out_ref[base : base + group, width : 2 * width] = (keys_sum[...] * scaling).astype(bf16)
        grad_gated = gated_sum[...]
        grad_mix = grad_gated * values * (sigmoid * (1.0 + mix * (1.0 - sigmoid)))
        grad_values = grad_gated * (mix * sigmoid) + grad_mix * conv[0:1]
        places = lax.broadcasted_iota(jnp.int32, values.shape, 0)
        own_seg = seg_of(places, ends)
        conv_sums[0] = conv_sums[0] + jnp.sum(grad_mix * shifted[0], axis=0, keepdims=True)
        for lag in range(1, CONV):
            same = (places < group - lag) & (seg_of(places + lag, ends) == own_seg)
            later = jnp.where(same, pltpu.roll(grad_mix, group - lag, 0), 0.0)
            grad_values = grad_values + later * conv[lag : lag + 1]
            conv_sums[lag] = conv_sums[lag] + jnp.sum(grad_mix * shifted[lag], axis=0, keepdims=True)
        out_ref[base : base + group, 2 * width :] = grad_values.astype(bf16)
    for lag in range(CONV):
        grad_conv_ref[lag : lag + 1, :] = conv_sums[lag]


def weight_grad_kernel(*refs):
    out_ref = refs[-1]
    at = 0
    for left_ref, right_ref in zip(refs[:-1:2], refs[1:-1:2]):
        width = right_ref.shape[1]
        out_ref[:, at : at + width] = product(left_ref[...], right_ref[...], TN, bf16)
        at += width


def weight_grad(*pairs, step=256):
    rows, d_model = pairs[0][0].shape
    width = sum(right.shape[1] for _, right in pairs)
    specs = []
    for left, right in pairs:
        specs.append(pl.BlockSpec((rows, step), lambda i: (0, i)))
        specs.append(pl.BlockSpec((rows, right.shape[1]), lambda i: (0, 0)))
    return pl.pallas_call(
        weight_grad_kernel,
        grid=(d_model // step,),
        out_shape=jax.ShapeDtypeStruct((d_model, width), bf16),
        in_specs=specs,
        out_specs=pl.BlockSpec((step, width), lambda i: (i, 0)),
        compiler_params=pltpu.CompilerParams(vmem_limit_bytes=40 * 1024 * 1024),
        cost_estimate=pl.CostEstimate(
            flops=2 * rows * d_model * width,
            bytes_accessed=2 * (rows * d_model * len(pairs) + (rows + d_model) * width),
            transcendentals=0,
        ),
        name="weight_grad",
    )(*[operand for pair in pairs for operand in pair])


def mlp_grad_kernel(own_lanes, hidden_ref, grad_ref, pair_ref, inner_ref, out_ref, rest_ref):
    lead = out_ref.shape[1] - pair_ref.shape[1]
    pairs = product(hidden_ref[...], pair_ref[...], NN)
    down = product(grad_ref[...], inner_ref[...], NN)
    shared = down[:, lead : lead + 128]
    lanes = lax.broadcasted_iota(jnp.int32, shared.shape, 1)
    out_ref[:, :lead] = down[:, :lead].astype(bf16)
    out_ref[:, lead : lead + 128] = jnp.where(lanes < own_lanes, shared, pairs[:, :128]).astype(bf16)
    out_ref[:, lead + 128 :] = pairs[:, 128:].astype(bf16)
    rest_ref[...] = shared.astype(bf16)


def mlp_grad(hidden, grad, pair, inner, width, own_lanes, step=448):
    d_model, rows = hidden.shape
    return pl.pallas_call(
        functools.partial(mlp_grad_kernel, own_lanes),
        grid=(d_model // step,),
        out_shape=(
            jax.ShapeDtypeStruct((d_model, width), bf16),
            jax.ShapeDtypeStruct((d_model, 128), bf16),
        ),
        in_specs=[
            pl.BlockSpec((step, rows), lambda i: (i, 0)),
            pl.BlockSpec((step, rows), lambda i: (i, 0)),
            pl.BlockSpec(pair.shape, lambda i: (0, 0)),
            pl.BlockSpec(inner.shape, lambda i: (0, 0)),
        ],
        out_specs=(
            pl.BlockSpec((step, width), lambda i: (i, 0)),
            pl.BlockSpec((step, 128), lambda i: (i, 0)),
        ),
        compiler_params=pltpu.CompilerParams(vmem_limit_bytes=40 * 1024 * 1024),
        cost_estimate=pl.CostEstimate(
            flops=2 * rows * d_model * width,
            bytes_accessed=2 * (2 * rows * d_model + (rows + d_model) * width),
            transcendentals=0,
        ),
        name="mlp_grad",
    )(hidden, grad, pair, inner)


def feed_forward_kernel(ff, hidden_ref, grad_ref, weight_ref, rest_ref, inner_ref, pair_ref):
    own = weight_ref.shape[1] - 2 * ff
    first = own // 128 * 128
    lead = own - first
    both = product(hidden_ref[...], weight_ref[:, first:], NN)
    gate_act, upper = both[:, lead : lead + ff], both[:, lead + ff :]
    grad = grad_ref[...]
    shared = weight_ref[:, first : first + 128]
    lanes = lax.broadcasted_iota(jnp.int32, shared.shape, 1)
    shared = jnp.where(lanes < lead, shared, rest_ref[...])
    grad_inner = jnp.concatenate(
        [
            product(grad, weight_ref[:, :first], NN),
            product(grad, shared, NN)[:, : ff - first],
        ],
        axis=1,
    )
    sigmoid = jax.nn.sigmoid(gate_act)
    silu = gate_act * sigmoid
    rows, spare = inner_ref.shape[0], inner_ref.shape[1] - ff
    inner_ref[...] = jnp.concatenate(
        [(silu * upper).astype(bf16), jnp.zeros((rows, spare), bf16)], axis=1
    )
    grad_gate = grad_inner * upper * (sigmoid * (1.0 + gate_act * (1.0 - sigmoid)))
    pair_ref[...] = jnp.concatenate(
        [
            jnp.zeros((rows, lead), bf16),
            grad_gate.astype(bf16),
            (grad_inner * silu).astype(bf16),
        ],
        axis=1,
    )


def feed_forward(hidden, grad, weight, rest, ff, step=256):
    rows, d_model = hidden.shape
    width = weight.shape[1]
    first = (width - 2 * ff) // 128 * 128
    padded = -(-ff // 128) * 128
    return pl.pallas_call(
        functools.partial(feed_forward_kernel, ff),
        grid=(rows // step,),
        out_shape=(
            jax.ShapeDtypeStruct((rows, padded), bf16),
            jax.ShapeDtypeStruct((rows, width - first), bf16),
        ),
        in_specs=[
            pl.BlockSpec((step, d_model), lambda i: (i, 0)),
            pl.BlockSpec((step, d_model), lambda i: (i, 0)),
            pl.BlockSpec((d_model, width), lambda i: (0, 0)),
            pl.BlockSpec(rest.shape, lambda i: (0, 0)),
        ],
        out_specs=(
            pl.BlockSpec((step, padded), lambda i: (i, 0)),
            pl.BlockSpec((step, width - first), lambda i: (i, 0)),
        ),
        compiler_params=pltpu.CompilerParams(vmem_limit_bytes=48 * 1024 * 1024),
        cost_estimate=pl.CostEstimate(
            flops=6 * rows * d_model * ff,
            bytes_accessed=2 * (2 * rows * d_model + 3 * (d_model + rows) * ff),
            transcendentals=rows * ff,
        ),
        name="feed_forward",
    )(hidden, grad, weight, rest)


def mlp_placed_kernel(ff, index_ref, *refs):
    mains, rests = refs[:4], refs[4:8]
    pair_ref, down_ref, columns = refs[8:]
    own = mains[0].shape[1] - 2 * ff
    for k in range(4):
        piece = index_ref[0] ^ k
        columns[piece, :, :own] = mains[k][:, :own].astype(f32)
        if rests[k].shape[1] == ff - own:
            columns[piece, :, own:ff] = rests[k][...].astype(f32)
        else:
            for step in range(rests[k].shape[1] // (ff - own)):

                @pl.when(pl.program_id(0) == step)
                def _():
                    at = step * (ff - own)
                    columns[piece, :, own:ff] = rests[k][:, at : at + ff - own].astype(f32)
        columns[piece, :, ff:] = mains[k][:, own:].astype(f32)
    for out, at in ((pair_ref.at[0], ff), (pair_ref.at[1], 2 * ff), (down_ref.at[0], 0)):
        out[...] = jnp.concatenate([columns[p, :, at : at + ff] for p in range(4)], axis=1)


def mlp_placed(mains, rests, index, ff, steps):
    rows, width = mains[0].shape
    block, total = rows // steps, 4 * ff
    if steps == 1:
        rests = [unpacked(rest, ff - (width - 2 * ff)) for rest in rests]
    return pl.pallas_call(
        functools.partial(mlp_placed_kernel, ff),
        grid=(steps,),
        out_shape=[
            jax.ShapeDtypeStruct((2, rows, total), f32),
            jax.ShapeDtypeStruct((1, rows, total), f32),
        ],
        in_specs=[SMEM]
        + [pl.BlockSpec((block, width), lambda i: (i, 0))] * 4
        + [pl.BlockSpec(rests[0].shape, lambda i: (0, 0))] * 4,
        out_specs=[
            pl.BlockSpec((2, block, total), lambda i: (0, i, 0)),
            pl.BlockSpec((1, block, total), lambda i: (0, i, 0)),
        ],
        scratch_shapes=[pltpu.VMEM((4, block, 3 * ff), f32)],
        compiler_params=pltpu.CompilerParams(vmem_limit_bytes=40 * 1024 * 1024),
        cost_estimate=pl.CostEstimate(
            flops=0, bytes_accessed=20 * rows * total, transcendentals=0
        ),
        name="mlp_placed",
    )(index.reshape(1).astype(jnp.int32), *mains, *rests)


def placed_kernel(each, total, counts, index_ref, *refs):
    n_parts = len(refs) - len(counts)
    outs = refs[n_parts:]
    for piece in range(total // each + (total % each > 0)):
        start = min(piece * each, total - each)
        shared = piece * each - start
        for k in range(n_parts):

            @pl.when((index_ref[0] ^ k) == piece)
            def _():
                at = 0
                for out, count in zip(outs, counts):
                    for i in range(count):
                        part = refs[k][:, at + shared : at + each].astype(f32)
                        at += each
                        out[i, :, start + shared : start + each] = part


def placed(parts, index, each, total, counts, steps):
    rows = parts[0].shape[0]
    block = rows // steps
    out_shape = [jax.ShapeDtypeStruct((count, rows, total), f32) for count in counts]
    out_specs = [pl.BlockSpec((count, block, total), lambda i: (0, i, 0)) for count in counts]
    width = parts[0].shape[1]
    return pl.pallas_call(
        functools.partial(placed_kernel, each, total, counts),
        grid=(steps,),
        out_shape=out_shape,
        in_specs=[SMEM] + [pl.BlockSpec((block, width), lambda i: (i, 0))] * len(parts),
        out_specs=out_specs,
        compiler_params=pltpu.CompilerParams(vmem_limit_bytes=40 * 1024 * 1024),
        cost_estimate=pl.CostEstimate(
            flops=0, bytes_accessed=rows * width * len(parts) * 6, transcendentals=0
        ),
        name="placed",
    )(index.reshape(1).astype(jnp.int32), *parts)


def last_placed_kernel(count, place_ref, *refs):
    *parts, _, _, first_ref, second_ref = refs
    for i in range(count):
        first_ref[i] = parts[i][...].astype(f32)
    second_ref[0] = parts[count][...].astype(f32)


def last_placed(part, index, each, total, first, second):
    rows, count = part.shape[0], first.shape[0]
    tiles, last = each // 128, total // 128 - 1

    def source(i):
        shift = tiles * (last // tiles + 1) - 1 - last
        return lambda j, ref: (
            0,
            i * tiles + jnp.where(ref[0] == last // tiles, jnp.minimum(j + shift, tiles - 1), j),
        )

    def target(j, ref):
        return (0, 0, jnp.minimum(ref[0] * tiles + j, last))

    out_specs = [pl.BlockSpec((n, rows, 128), target) for n in (count, 1)]
    return pl.pallas_call(
        functools.partial(last_placed_kernel, count),
        grid_spec=pltpu.PrefetchScalarGridSpec(
            num_scalar_prefetch=1,
            grid=(tiles,),
            in_specs=[pl.BlockSpec((rows, 128), source(i)) for i in range(count + 1)]
            + [pl.BlockSpec(memory_space=pl.ANY)] * 2,
            out_specs=out_specs,
        ),
        out_shape=[jax.ShapeDtypeStruct(first.shape, f32), jax.ShapeDtypeStruct(second.shape, f32)],
        input_output_aliases={count + 2: 0, count + 3: 1},
        name="last_placed",
    )(index.reshape(1).astype(jnp.int32), *[part] * (count + 1), first, second)


def at_home_kernel(undo_ref, *refs):
    *blocks, first_ref, second_ref, rows = refs
    each = blocks[0].shape[0]
    for k, block in enumerate(blocks):
        rows[k * each : (k + 1) * each, :] = block[...]
    d_model = first_ref.shape[2]
    for batch in range(first_ref.shape[0]):
        undo = undo_ref[batch * first_ref.shape[1] : (batch + 1) * first_ref.shape[1], :]
        first_ref[batch] = product(undo, rows[:, :d_model], NN, bf16)
        second_ref[batch] = product(undo, rows[:, d_model:], NN, bf16)


def at_home(undo, blocks, batches, d_model):
    rows = undo.shape[0]
    out = jax.ShapeDtypeStruct((batches, rows // batches, d_model), bf16)
    return pl.pallas_call(
        at_home_kernel,
        out_shape=(out, out),
        in_specs=[VMEM] * (1 + len(blocks)),
        out_specs=(VMEM, VMEM),
        scratch_shapes=[pltpu.VMEM((rows, 2 * d_model), bf16)],
        compiler_params=pltpu.CompilerParams(vmem_limit_bytes=32 * 1024 * 1024),
        cost_estimate=pl.CostEstimate(flops=0, bytes_accessed=10_000_000, transcendentals=0),
        name="at_home",
    )(undo, *blocks)


VMEM = pl.BlockSpec(memory_space=pltpu.VMEM)
SMEM = pl.BlockSpec(memory_space=pltpu.SMEM)


def attend_forward(lengths, qkv, conv):
    rows, width = qkv.shape[0], HEADS_EACH * HEAD
    return pl.pallas_call(
        attend_forward_kernel,
        out_shape=jax.ShapeDtypeStruct((rows, width), bf16),
        in_specs=[SMEM, VMEM, VMEM],
        out_specs=VMEM,
        scratch_shapes=[pltpu.VMEM((rows // BATCHES, width), bf16)],
        compiler_params=pltpu.CompilerParams(vmem_limit_bytes=32 * 1024 * 1024),
        cost_estimate=pl.CostEstimate(flops=0, bytes_accessed=20_000_000, transcendentals=0),
        name="attend_forward",
    )(lengths, qkv, conv)


def attend_backward(lengths, qkv, grad, conv):
    rows, width = qkv.shape[0], HEADS_EACH * HEAD
    group = rows // BATCHES
    return pl.pallas_call(
        attend_backward_kernel,
        out_shape=(
            jax.ShapeDtypeStruct((rows, 3 * width), bf16),
            jax.ShapeDtypeStruct((CONV, width), f32),
        ),
        in_specs=[SMEM, VMEM, VMEM, VMEM],
        out_specs=(VMEM, VMEM),
        scratch_shapes=[
            pltpu.VMEM((group, width), bf16),
            pltpu.VMEM((group, width), f32),
            pltpu.VMEM((group, width), f32),
        ],
        compiler_params=pltpu.CompilerParams(vmem_limit_bytes=32 * 1024 * 1024),
        cost_estimate=pl.CostEstimate(flops=0, bytes_accessed=50_000_000, transcendentals=0),
        name="attend_backward",
    )(lengths, qkv, grad, conv)


def part_of(total, each, index):
    start = jnp.minimum(index * each, total - each)
    return start, index * each - start


def per_device(
    tokens,
    cotangent,
    attn_in,
    attn_out,
    gate_up,
    down_proj,
    conv_weight,
    norm_gains,
    deal_order,
    lengths,
):
    sizes = tuple(lax.axis_size(axis) for axis in ("fsdp", "ctx", "tp"))
    n_fsdp, n_ctx, n_tp = sizes
    workers = n_fsdp * n_ctx
    f, c, t = (lax.axis_index(axis) for axis in ("fsdp", "ctx", "tp"))
    me = f * n_ctx + c
    tok_rows, d_model = tokens.shape[1:]
    d_own = attn_in.shape[1]
    heads_all = attn_in.shape[2]
    width = HEADS_EACH * HEAD
    ff_all = gate_up.shape[2]
    ff = ff_all // n_ctx
    from_each = tok_rows // n_fsdp
    half = from_each // n_tp
    group = n_ctx * tok_rows
    plane = BATCHES * group

    start, shared = part_of(heads_all, width, c)
    sliced = lax.dynamic_slice_in_dim(attn_in, start, width, 2)
    out_part = lax.dynamic_slice_in_dim(attn_out, start, width, 0)
    out_part = jnp.where(jnp.arange(width)[:, None] >= shared, out_part, jnp.zeros_like(out_part))
    attn_own = jnp.concatenate([sliced[0], sliced[1], sliced[2], out_part.T], axis=1)
    own_down = 3 * ff // 128 * 128 - 2 * ff
    sliced = lax.dynamic_slice_in_dim(gate_up, c * ff, ff, 2)
    down_own = lax.dynamic_slice_in_dim(down_proj, c * ff, ff, 0).T
    mlp_own = jnp.concatenate([down_own[:, :own_down], sliced[0], sliced[1]], axis=1)
    rest_own = down_own[:, own_down:]
    rest_width = ff - own_down
    attn_w = lax.all_gather(attn_own, "fsdp", axis=0, tiled=True)
    mlp_w = lax.all_gather(after(mlp_own, attn_own), "fsdp", axis=0, tiled=True)
    down_w, pair_w = mlp_w[:, :own_down], mlp_w[:, own_down // 128 * 128 :]
    qkv_w, out_w = attn_w[:, : 3 * width], attn_w[:, 3 * width :]

    small = jnp.concatenate(
        [
            deal_order.reshape(-1).astype(f32),
            norm_gains.reshape(-1).astype(f32),
            conv_weight.reshape(-1).astype(f32),
        ]
    )
    small = after(small, attn_own)
    small = lax.all_to_all(
        jnp.broadcast_to(small[None], (workers,) + small.shape),
        ("fsdp", "ctx"),
        split_axis=0,
        concat_axis=0,
        tiled=True,
    )
    n_order, n_gain = deal_order.size, norm_gains.size
    orders = small[:, :n_order].astype(jnp.int32).reshape(workers, BATCHES, tok_rows)
    by_fsdp = small.reshape(n_fsdp, n_ctx, -1)[:, 0]
    gains = by_fsdp[:, n_order : n_order + n_gain].reshape(n_fsdp, 2, -1)
    gains = jnp.transpose(gains, (1, 0, 2)).reshape(2, 1, d_model)
    conv = by_fsdp[:, n_order + n_gain :].reshape(n_fsdp, CONV, -1)
    conv = jnp.transpose(conv, (1, 0, 2)).reshape(CONV, heads_all)
    conv = lax.dynamic_slice_in_dim(conv, start, width, 1)

    given = me * tok_rows + jnp.arange(tok_rows, dtype=jnp.int32)
    by_batch = jnp.transpose(orders, (1, 0, 2)).reshape(BATCHES, -1)
    planes = jnp.arange(workers * tok_rows, dtype=jnp.int32) // group
    to_plane = jnp.sum(
        jnp.where(by_batch[:, None, :] == given[None, :, None], planes[None, None, :], 0), axis=2
    )
    earlier = jnp.arange(tok_rows)[None, :] < jnp.arange(tok_rows)[:, None]
    slot = jnp.sum(
        ((to_plane[:, None, :] == to_plane[:, :, None]) & earlier[None]).astype(jnp.int32), axis=2
    )
    place = ((slot // half) * n_fsdp + (to_plane - f) % n_fsdp) * (BATCHES * half) + slot % half
    place = place + jnp.arange(BATCHES, dtype=jnp.int32)[:, None] * half
    place = place.reshape(-1)
    sent_rows = BATCHES * tok_rows // n_tp
    wire = t * sent_rows + jnp.arange(sent_rows, dtype=jnp.int32)
    choose = (place[None, :] == wire[:, None]).astype(bf16)
    both = jnp.concatenate([wire, (1 - t) * sent_rows + jnp.arange(sent_rows, dtype=jnp.int32)])
    undo = (place[:, None] == both[None, :]).astype(bf16)

    def to_planes(rows):
        picked = product(choose, rows.reshape(-1, d_model), NN, bf16)
        return z_exchange(jnp.split(picked, n_fsdp), sizes)

    def to_home(rows):
        blocks = jnp.split(rows, n_fsdp)
        return [blocks[0]] + [z_shifted(blocks[k], sizes, n_fsdp - k) for k in range(1, n_fsdp)]

    own_x = to_planes(tokens).astype(f32)

    dealt = lax.dynamic_slice_in_dim(orders, f * n_ctx, n_ctx, 0)
    dealt = jnp.transpose(dealt, (1, 0, 2)).reshape(BATCHES, group)
    giver = dealt // tok_rows
    rank = jnp.sum(
        (
            (giver[:, None, :] == giver[:, :, None]) & (dealt[:, None, :] < dealt[:, :, None])
        ).astype(jnp.int32),
        axis=2,
    )
    core = rank // half
    away = (giver % n_ctx) ^ c
    swapped = jnp.where(core == 0, away, (away % 2) * 2 + away // 2)
    block = jnp.where(core == t, 0, n_ctx) + swapped
    arrival = block * (plane // (n_ctx * n_tp)) + (f - giver // n_ctx) % n_fsdp * (BATCHES * half)
    arrival = arrival + jnp.arange(BATCHES, dtype=jnp.int32)[:, None] * half + rank % half
    deal = (arrival.reshape(-1)[:, None] == jnp.arange(plane, dtype=jnp.int32)[None, :]).astype(bf16)

    first_scale = lax.rsqrt(jnp.mean(own_x * own_x, axis=-1, keepdims=True) + epsilon)
    hidden = plane_gather((own_x * first_scale * gains[0]).astype(bf16), sizes)
    own_lengths = lengths[:, 0]
    hidden, given_g, rest_own = stage(hidden, cotangent, packed(rest_own))
    own_g = to_planes(given_g)
    if n_fsdp > 4:
        rests = lax.all_gather(rest_own, "fsdp")
        rest_w = jnp.concatenate([unpacked(rests[k], rest_width) for k in range(n_fsdp)])
    else:
        rest_w = jnp.zeros((d_model, rest_width), bf16)
        for k in range(n_fsdp):
            part = unpacked(z_shifted(rest_own, sizes, k) if k else rest_own, rest_width)
            rest_w = lax.dynamic_update_slice_in_dim(rest_w, part, (f - k) % n_fsdp * d_own, 0)
    qkv = product(deal, product(hidden, qkv_w, NN, bf16), NN, bf16)
    grad_dealt = plane_gather(after(own_g, qkv), sizes)
    attended = product(deal, attend_forward(own_lengths, qkv, conv), TN, bf16)
    kept = plane // 2
    branch = plane_scatter(
        product(attended[:kept], out_w, NT),
        product(attended[kept:], out_w, NT, bf16),
        sizes,
    )
    resid = own_x + branch

    second_scale = lax.rsqrt(jnp.mean(resid * resid, axis=-1, keepdims=True) + epsilon)
    hidden_two = plane_gather((resid * second_scale * gains[1]).astype(bf16), sizes)
    rest_tile = jnp.pad(rest_w, ((0, 0), (own_down % 128, 128 - own_down % 128 - rest_width)))
    hidden_two_turned, grad_dealt_turned, rest_tile = after(
        (hidden_two.T, grad_dealt.T, rest_tile)
    )
    inner, grad_pair = feed_forward(
        after(hidden_two, hidden_two_turned, grad_dealt_turned), grad_dealt, mlp_w, rest_tile, ff
    )
    grad_mlp_w, grad_rest_w = mlp_grad(
        hidden_two_turned, grad_dealt_turned, grad_pair, inner, mlp_w.shape[1], own_down % 128
    )
    grad_mlp_w, grad_rest_w, grad_pair, inner = stage(grad_mlp_w, grad_rest_w, grad_pair, inner)
    grad_mlp = lax.psum_scatter(grad_mlp_w, "fsdp", scatter_dimension=0, tiled=True)
    grad_rest_w = grad_rest_w[:, own_down % 128 :][:, :rest_width]
    rests = [
        packed(lax.dynamic_slice_in_dim(grad_rest_w, (f + k) % n_fsdp * d_own, d_own, 0))
        for k in range(n_fsdp)
    ]

    sent = product(grad_pair[kept:], pair_w, NT, bf16)
    sent, grad_pair = stage(sent, grad_pair)

    got = flipped(sent, sizes, 2)
    part = product(grad_pair[:kept], pair_w, NT)
    got, part = stage(got, part)
    part, sent = added(part, got)
    part, sent, inner = stage(part, sent, inner)

    got = flipped(sent, sizes, 1)
    lift = product(inner[:, :own_down], down_w, NT) + product(inner[:, own_down:ff], rest_w, NT)
    lift, lift_sent = lift[:kept], lift[kept:].astype(bf16)
    got, part, lift_sent, lift = stage(got, part, lift_sent, lift)
    part, sent = added(part, got)
    part, sent, lift_sent, lift = stage(part, sent, lift_sent, lift)

    got = flipped(sent, sizes, 0)
    lift_got = flipped(lift_sent, sizes, 2)
    grad_two = part + got.astype(f32)
    normed = resid * second_scale
    scaled = grad_two * gains[1]
    grad_resid = own_g.astype(f32) + second_scale * (
        scaled - normed * jnp.mean(scaled * normed, axis=-1, keepdims=True)
    )
    grad_own = grad_resid.astype(bf16)
    grad_own, lift, lift_got = stage(grad_own, lift, lift_got)

    near = near_shares(grad_own, sizes)
    lift, lift_sent = added(lift, lift_got)
    grad_own, near, lift, lift_sent = stage(grad_own, near, lift, lift_sent)
    grad_branch = plane_gather(grad_own, sizes, near)
    grad_branch, lift_sent = stage(grad_branch, lift_sent)

    lift_got = flipped(lift_sent, sizes, 1)
    grad_attended = product(deal, product(grad_branch, out_w, NN, bf16), NN, bf16)
    grad_proj, grad_conv = attend_backward(own_lengths, qkv, grad_attended, conv)
    lift_got, lift, grad_proj = stage(lift_got, lift, grad_proj)

    grad_proj = product(deal, grad_proj, TN, bf16)
    sent = product(grad_proj[kept:], qkv_w, NT, bf16)
    lift_got, lift, grad_proj, sent = stage(lift_got, lift, grad_proj, sent)

    got = flipped(sent, sizes, 2)
    part = product(grad_proj[:kept], qkv_w, NT)
    lift, lift_sent = added(lift, lift_got)
    got, part, lift, lift_sent = stage(got, part, lift, lift_sent)
    lift_got = flipped(lift_sent, sizes, 0)
    part, sent = added(part, got)
    part, sent, grad_proj = stage(part, sent, grad_proj)

    got = flipped(sent, sizes, 1)
    grad_attn_w = weight_grad((hidden, grad_proj), (grad_branch, attended))
    got, part, grad_attn_w, lift_got = stage(got, part, grad_attn_w, lift_got)
    result = (resid + (lift + lift_got.astype(f32))).astype(bf16)
    grad_attn = lax.psum_scatter(grad_attn_w, "fsdp", scatter_dimension=0, tiled=True)
    part, sent = added(part, got)

    taps = jnp.concatenate(jnp.split(grad_conv, width // 128, axis=1)).astype(bf16)
    grad_mlp, sent, taps, *rests = stage(grad_mlp, sent, taps, *rests)
    got_last = flipped(sent, sizes, 0)
    mlp_near = near_shares(grad_mlp, sizes)
    little = [jnp.concatenate([rest, taps]) for rest in rests]
    little = sum(
        [z_shifted(little[k], sizes, k).astype(f32) for k in range(1, n_fsdp)], little[0].astype(f32)
    ).astype(bf16)
    mlp_near, got_last, little = stage(mlp_near, got_last, little)

    grad_hidden = part + got_last.astype(f32)
    normed = own_x * first_scale
    scaled = grad_hidden * gains[0]
    grad_x = grad_resid + first_scale * (
        scaled - normed * jnp.mean(scaled * normed, axis=-1, keepdims=True)
    )
    grad_x = grad_x.astype(bf16)

    steps = 128 // rest_width if d_own * rest_width % (128 * 16) == 0 else 1

    def gain_part(own, grad, each, skipped):
        columns = own.shape[1]
        counted = (jnp.arange(columns) % each) >= skipped
        terms = own.astype(f32) * grad[:, :columns].astype(f32)
        return jnp.sum(jnp.where(counted[None, :], terms, 0.0), axis=1)

    mlp_shares = ctx_shares(grad_mlp, sizes, t, mlp_near)
    little_shares = ctx_shares(little, sizes, t)
    rest_rows = d_own * rest_width // 128
    rest_shares = [share[:rest_rows] for share in little_shares]
    taps = [share[rest_rows:].astype(f32) for share in little_shares]
    taps = [jnp.concatenate(jnp.split(tap, width // 128), axis=1) for tap in taps]
    first_shared = n_ctx * width - heads_all
    taps = jnp.stack(taps)
    taps = [lax.dynamic_index_in_dim(taps, c ^ k, 0, False) for k in range(n_ctx)]
    taps = jnp.concatenate(taps[:-1] + [taps[-1][:, first_shared:]], axis=1)
    grad_conv = lax.dynamic_slice_in_dim(taps, f * (heads_all // n_fsdp), heads_all // n_fsdp, 1)
    gain_two = gain_part(mlp_own[:, own_down:], grad_mlp[:, own_down:], ff, 0)
    rows_back = jnp.concatenate([result, grad_x], axis=1)
    grad_attn, rows_back, gain_two, grad_conv, rest_shares = stage(
        grad_attn, rows_back, gain_two, grad_conv, rest_shares
    )

    near = near_shares(grad_attn, sizes)
    home = to_home(rows_back)
    gain_one = gain_part(attn_own[:, : 3 * width], grad_attn, width, shared)
    gains_grad = jnp.stack([gain_one, gain_two])
    gains_grad = gains_grad + flipped(gains_grad, sizes, 2)
    grad_gate_up, grad_down = mlp_placed(mlp_shares, rest_shares, c, ff, steps)
    near, gains_grad, grad_gate_up, grad_down = stage(near, gains_grad, grad_gate_up, grad_down)

    attn_shares = ctx_shares(grad_attn, sizes, t, near)
    grad_attn_in, grad_attn_out = placed(attn_shares[:3], c, width, heads_all, (3, 1), steps)
    for step in (0, 1):
        gains_grad = gains_grad + flipped(gains_grad, sizes, step)
    activations, input_grad = at_home(
        undo, home + [flipped(block, sizes, 2) for block in home], BATCHES, d_model
    )
    grad_gains = gains_grad / norm_gains.astype(f32)
    grad_attn_in, grad_attn_out = last_placed(
        attn_shares[3], c ^ 3, width, heads_all, grad_attn_in, grad_attn_out
    )
    return (
        activations,
        input_grad,
        grad_attn_in,
        grad_attn_out[0].T,
        grad_gate_up,
        grad_down[0].T,
        grad_conv[None],
        grad_gains,
    )


def solution(mesh):
    return jax.shard_map(
        per_device,
        mesh=mesh,
        in_specs=(
            P(None, ("fsdp", "ctx"), None),
            P(None, ("fsdp", "ctx"), None),
            P(None, "fsdp", "tp"),
            P("tp", "fsdp"),
            P(None, "fsdp", "tp"),
            P("tp", "fsdp"),
            P("tp", None, "fsdp"),
            P(None, "fsdp"),
            P(None, ("fsdp", "ctx")),
            P(None, "fsdp", None),
        ),
        out_specs=(
            P(None, ("fsdp", "ctx"), None),
            P(None, ("fsdp", "ctx"), None),
            P(None, "fsdp", "tp"),
            P("tp", "fsdp"),
            P(None, "fsdp", "tp"),
            P("tp", "fsdp"),
            P("tp", None, "fsdp"),
            P(None, "fsdp"),
        ),
        check_vma=False,
    )
```

```python
import functools
import math

import jax
import jax.numpy as jnp
from jax import lax
from jax.experimental import pallas as pl
from jax.experimental.pallas import tpu as pltpu
from jax.sharding import PartitionSpec as P

HEAD = 64
WINDOW = 64
CONV = 3
BATCHES = 2
BLOCK = 128
HEADS_EACH = 4

epsilon = 1e-06
masked_score = -1e30
f32 = jnp.float32
bf16 = jnp.bfloat16


def flipped(value, sizes, step):
    n_fsdp, n_ctx, n_tp = sizes
    pairs = []
    for f in range(n_fsdp):
        for c in range(n_ctx):
            for t in range(n_tp):
                if step == 2:
                    other = (c, t ^ 1)
                else:
                    other = (c ^ (1 if t == step else 2), t)
                pairs.append(((f * n_ctx + c) * n_tp + t, (f * n_ctx + other[0]) * n_tp + other[1]))
    return lax.ppermute(value, ("fsdp", "ctx", "tp"), pairs)


def near_shares(own, sizes):
    return flipped(own, sizes, 0), flipped(own, sizes, 1)


def plane_gather(own, sizes, near=None):
    one, two = near or near_shares(own, sizes)
    three = flipped(one, sizes, 1)
    mine = [own, one, two, three]
    return jnp.concatenate(mine + [flipped(block, sizes, 2) for block in mine])


def plane_scatter(kept, sent, sizes):
    total = kept + flipped(sent.astype(bf16), sizes, 2).astype(f32)
    for step in (1, 0):
        half = total.shape[0] // 2
        total = total[:half] + flipped(total[half:].astype(bf16), sizes, step).astype(f32)
    return total


def after(value, *others):
    return lax.optimization_barrier((value,) + others)[0]


def stage(*values):
    return lax.optimization_barrier(values)


def added(part, got):
    half = part.shape[0] // 2
    return part[:half] + got[:half].astype(f32), (part[half:] + got[half:].astype(f32)).astype(bf16)


def z_shifted(value, sizes, steps):
    n = sizes[0]
    return lax.ppermute(value, "fsdp", [(i, (i + steps) % n) for i in range(n)])


def packed(rest):
    return jnp.concatenate(jnp.split(rest, 128 // rest.shape[1]), axis=1)


def unpacked(full, width):
    return jnp.concatenate(jnp.split(full, full.shape[1] // width, axis=1))


def z_exchange(blocks, sizes):
    got = [blocks[0]] + [z_shifted(blocks[k], sizes, k) for k in range(1, sizes[0])]
    return jnp.concatenate(got)


def ctx_shares(own, sizes, core, near=None):
    one, two = near or near_shares(own, sizes)
    three = flipped(one, sizes, 1)
    return [own, jnp.where(core == 0, one, two), jnp.where(core == 0, two, one), three]


def product(left, right, dims, out_type=f32):
    return lax.dot_general(left, right, (dims, ((), ())), preferred_element_type=f32).astype(out_type)


NN = ((1,), (0,))
NT = ((1,), (1,))
TN = ((0,), (0,))


def seg_of(places, ends):
    return (places >= ends[0]).astype(jnp.int32) + (places >= ends[1]).astype(jnp.int32)


def conv_terms(values, conv, ends):
    rows = values.shape[0]
    places = lax.broadcasted_iota(jnp.int32, values.shape, 0)
    own_seg = seg_of(places, ends)
    shifted = [values]
    for lag in range(1, CONV):
        same = (places >= lag) & (seg_of(places - lag, ends) == own_seg)
        shifted.append(jnp.where(same, pltpu.roll(values, lag, 0), 0.0))
    mix = shifted[0] * conv[0:1]
    for lag in range(1, CONV):
        mix = mix + shifted[lag] * conv[lag : lag + 1]
    return shifted, mix


def block_mask(block, first, span, ends):
    query = block * BLOCK + lax.broadcasted_iota(jnp.int32, (BLOCK, span), 0)
    key = first * BLOCK + lax.broadcasted_iota(jnp.int32, (BLOCK, span), 1)
    return (seg_of(query, ends) == seg_of(key, ends)) & (key <= query) & (key > query - WINDOW)


def head_lanes(tile, head):
    lanes = lax.broadcasted_iota(jnp.int32, tile.shape, 1)
    return (lanes >= head * HEAD) & (lanes < (head + 1) * HEAD)


def window_weights(query, keys, allowed):
    scores = product(query, keys, NT) * (1.0 / math.sqrt(HEAD))
    scores = jnp.where(allowed, scores, masked_score)
    weights = jnp.exp(scores - jnp.max(scores, axis=-1, keepdims=True))
    return weights / jnp.sum(weights, axis=-1, keepdims=True)


def ends_of(lengths_ref, batch):
    first = lengths_ref[batch, 0]
    return (first, first + lengths_ref[batch, 1])


def attend_forward_kernel(lengths_ref, qkv_ref, conv_ref, out_ref, gated_ref):
    width = HEADS_EACH * HEAD
    group = qkv_ref.shape[0] // BATCHES
    conv = conv_ref[...]
    for batch in range(BATCHES):
        ends = ends_of(lengths_ref, batch)
        base = batch * group
        values = qkv_ref[base : base + group, 2 * width :].astype(f32)
        _, mix = conv_terms(values, conv, ends)
        gated_ref[...] = (values * (mix * jax.nn.sigmoid(mix))).astype(bf16)
        for block in range(group // BLOCK):
            first = max(block - 1, 0)
            span = (block + 1 - first) * BLOCK
            allowed = block_mask(block, first, span, ends)
            rows = slice(base + block * BLOCK, base + (block + 1) * BLOCK)
            for pair in range(width // 128):
                lanes = slice(pair * 128, (pair + 1) * 128)
                query = qkv_ref[rows, lanes]
                keys = qkv_ref[
                    base + first * BLOCK : base + first * BLOCK + span,
                    width + pair * 128 : width + (pair + 1) * 128,
                ]
                gated = gated_ref[first * BLOCK : first * BLOCK + span, lanes]
                blended = []
                for head in range(2):
                    chosen = jnp.where(head_lanes(query, head), query, jnp.zeros_like(query))
                    weights = window_weights(chosen, keys, allowed).astype(bf16)
                    blended.append(product(weights, gated, NN))
                merged = jnp.where(head_lanes(blended[0], 0), blended[0], blended[1])
                out_ref[rows, lanes] = merged.astype(bf16)


def attend_backward_kernel(
    lengths_ref, qkv_ref, grad_ref, conv_ref, out_ref, grad_conv_ref, gated_ref, keys_sum, gated_sum
):
    width = HEADS_EACH * HEAD
    group = qkv_ref.shape[0] // BATCHES
    conv = conv_ref[...]
    scaling = 1.0 / math.sqrt(HEAD)
    conv_sums = [jnp.zeros((1, width), f32) for _ in range(CONV)]
    for batch in range(BATCHES):
        ends = ends_of(lengths_ref, batch)
        base = batch * group
        values = qkv_ref[base : base + group, 2 * width :].astype(f32)
        shifted, mix = conv_terms(values, conv, ends)
        sigmoid = jax.nn.sigmoid(mix)
        gated_ref[...] = (values * (mix * sigmoid)).astype(bf16)
        keys_sum[...] = jnp.zeros_like(keys_sum)
        gated_sum[...] = jnp.zeros_like(gated_sum)
        for block in range(group // BLOCK):
            first = max(block - 1, 0)
            span = (block + 1 - first) * BLOCK
            allowed = block_mask(block, first, span, ends)
            rows = slice(base + block * BLOCK, base + (block + 1) * BLOCK)
            local = slice(first * BLOCK, first * BLOCK + span)
            for pair in range(width // 128):
                lanes = slice(pair * 128, (pair + 1) * 128)
                query = qkv_ref[rows, lanes]
                grad = grad_ref[rows, lanes]
                keys = qkv_ref[
                    base + first * BLOCK : base + first * BLOCK + span,
                    width + pair * 128 : width + (pair + 1) * 128,
                ]
                gated = gated_ref[local, lanes]
                grad_queries = []
                grad_keys = None
                grad_gated = None
                for head in range(2):
                    mine = head_lanes(query, head)
                    chosen = jnp.where(mine, query, jnp.zeros_like(query))
                    chosen_grad = jnp.where(mine, grad, jnp.zeros_like(grad))
                    weights = window_weights(chosen, keys, allowed)
                    grad_weights = product(chosen_grad, gated, NT)
                    inner = jnp.sum(weights * grad_weights, axis=-1, keepdims=True)
                    grad_scores = (weights * (grad_weights - inner)).astype(bf16)
                    grad_queries.append(product(grad_scores, keys, NN))
                    more_keys = product(grad_scores, chosen, TN)
                    more_gated = product(weights.astype(bf16), chosen_grad, TN)
                    grad_keys = more_keys if grad_keys is None else grad_keys + more_keys
                    grad_gated = more_gated if grad_gated is None else grad_gated + more_gated
                merged = jnp.where(head_lanes(grad_queries[0], 0), grad_queries[0], grad_queries[1])
                out_ref[rows, lanes] = (merged * scaling).astype(bf16)
                keys_sum[local, lanes] += grad_keys
                gated_sum[local, lanes] += grad_gated
        out_ref[base : base + group, width : 2 * width] = (keys_sum[...] * scaling).astype(bf16)
        grad_gated = gated_sum[...]
        grad_mix = grad_gated * values * (sigmoid * (1.0 + mix * (1.0 - sigmoid)))
        grad_values = grad_gated * (mix * sigmoid) + grad_mix * conv[0:1]
        places = lax.broadcasted_iota(jnp.int32, values.shape, 0)
        own_seg = seg_of(places, ends)
        conv_sums[0] = conv_sums[0] + jnp.sum(grad_mix * shifted[0], axis=0, keepdims=True)
        for lag in range(1, CONV):
            same = (places < group - lag) & (seg_of(places + lag, ends) == own_seg)
            later = jnp.where(same, pltpu.roll(grad_mix, group - lag, 0), 0.0)
            grad_values = grad_values + later * conv[lag : lag + 1]
            conv_sums[lag] = conv_sums[lag] + jnp.sum(grad_mix * shifted[lag], axis=0, keepdims=True)
        out_ref[base : base + group, 2 * width :] = grad_values.astype(bf16)
    for lag in range(CONV):
        grad_conv_ref[lag : lag + 1, :] = conv_sums[lag]


def weight_grad_kernel(*refs):
    out_ref = refs[-1]
    at = 0
    for left_ref, right_ref in zip(refs[:-1:2], refs[1:-1:2]):
        width = right_ref.shape[1]
        out_ref[:, at : at + width] = product(left_ref[...], right_ref[...], TN, bf16)
        at += width


def weight_grad(*pairs, step=256):
    rows, d_model = pairs[0][0].shape
    width = sum(right.shape[1] for _, right in pairs)
    specs = []
    for left, right in pairs:
        specs.append(pl.BlockSpec((rows, step), lambda i: (0, i)))
        specs.append(pl.BlockSpec((rows, right.shape[1]), lambda i: (0, 0)))
    return pl.pallas_call(
        weight_grad_kernel,
        grid=(d_model // step,),
        out_shape=jax.ShapeDtypeStruct((d_model, width), bf16),
        in_specs=specs,
        out_specs=pl.BlockSpec((step, width), lambda i: (i, 0)),
        compiler_params=pltpu.CompilerParams(vmem_limit_bytes=40 * 1024 * 1024),
        cost_estimate=pl.CostEstimate(
            flops=2 * rows * d_model * width,
            bytes_accessed=2 * (rows * d_model * len(pairs) + (rows + d_model) * width),
            transcendentals=0,
        ),
        name="weight_grad",
    )(*[operand for pair in pairs for operand in pair])


def mlp_grad_kernel(own_lanes, hidden_ref, grad_ref, pair_ref, inner_ref, out_ref, rest_ref):
    lead = out_ref.shape[1] - pair_ref.shape[1]
    pairs = product(hidden_ref[...], pair_ref[...], NN)
    down = product(grad_ref[...], inner_ref[...], NN)
    shared = down[:, lead : lead + 128]
    lanes = lax.broadcasted_iota(jnp.int32, shared.shape, 1)
    out_ref[:, :lead] = down[:, :lead].astype(bf16)
    out_ref[:, lead : lead + 128] = jnp.where(lanes < own_lanes, shared, pairs[:, :128]).astype(bf16)
    out_ref[:, lead + 128 :] = pairs[:, 128:].astype(bf16)
    rest_ref[...] = shared.astype(bf16)


def mlp_grad(hidden, grad, pair, inner, width, own_lanes, step=448):
    d_model, rows = hidden.shape
    return pl.pallas_call(
        functools.partial(mlp_grad_kernel, own_lanes),
        grid=(d_model // step,),
        out_shape=(
            jax.ShapeDtypeStruct((d_model, width), bf16),
            jax.ShapeDtypeStruct((d_model, 128), bf16),
        ),
        in_specs=[
            pl.BlockSpec((step, rows), lambda i: (i, 0)),
            pl.BlockSpec((step, rows), lambda i: (i, 0)),
            pl.BlockSpec(pair.shape, lambda i: (0, 0)),
            pl.BlockSpec(inner.shape, lambda i: (0, 0)),
        ],
        out_specs=(
            pl.BlockSpec((step, width), lambda i: (i, 0)),
            pl.BlockSpec((step, 128), lambda i: (i, 0)),
        ),
        compiler_params=pltpu.CompilerParams(vmem_limit_bytes=40 * 1024 * 1024),
        cost_estimate=pl.CostEstimate(
            flops=2 * rows * d_model * width,
            bytes_accessed=2 * (2 * rows * d_model + (rows + d_model) * width),
            transcendentals=0,
        ),
        name="mlp_grad",
    )(hidden, grad, pair, inner)


def feed_forward_kernel(ff, hidden_ref, grad_ref, weight_ref, rest_ref, inner_ref, pair_ref):
    own = weight_ref.shape[1] - 2 * ff
    first = own // 128 * 128
    lead = own - first
    both = product(hidden_ref[...], weight_ref[:, first:], NN)
    gate_act, upper = both[:, lead : lead + ff], both[:, lead + ff :]
    grad = grad_ref[...]
    shared = weight_ref[:, first : first + 128]
    lanes = lax.broadcasted_iota(jnp.int32, shared.shape, 1)
    shared = jnp.where(lanes < lead, shared, rest_ref[...])
    grad_inner = jnp.concatenate(
        [
            product(grad, weight_ref[:, :first], NN),
            product(grad, shared, NN)[:, : ff - first],
        ],
        axis=1,
    )
    sigmoid = jax.nn.sigmoid(gate_act)
    silu = gate_act * sigmoid
    rows, spare = inner_ref.shape[0], inner_ref.shape[1] - ff
    inner_ref[...] = jnp.concatenate(
        [(silu * upper).astype(bf16), jnp.zeros((rows, spare), bf16)], axis=1
    )
    grad_gate = grad_inner * upper * (sigmoid * (1.0 + gate_act * (1.0 - sigmoid)))
    pair_ref[...] = jnp.concatenate(
        [
            jnp.zeros((rows, lead), bf16),
            grad_gate.astype(bf16),
            (grad_inner * silu).astype(bf16),
        ],
        axis=1,
    )


def feed_forward(hidden, grad, weight, rest, ff, step=256):
    rows, d_model = hidden.shape
    width = weight.shape[1]
    first = (width - 2 * ff) // 128 * 128
    padded = -(-ff // 128) * 128
    return pl.pallas_call(
        functools.partial(feed_forward_kernel, ff),
        grid=(rows // step,),
        out_shape=(
            jax.ShapeDtypeStruct((rows, padded), bf16),
            jax.ShapeDtypeStruct((rows, width - first), bf16),
        ),
        in_specs=[
            pl.BlockSpec((step, d_model), lambda i: (i, 0)),
            pl.BlockSpec((step, d_model), lambda i: (i, 0)),
            pl.BlockSpec((d_model, width), lambda i: (0, 0)),
            pl.BlockSpec(rest.shape, lambda i: (0, 0)),
        ],
        out_specs=(
            pl.BlockSpec((step, padded), lambda i: (i, 0)),
            pl.BlockSpec((step, width - first), lambda i: (i, 0)),
        ),
        compiler_params=pltpu.CompilerParams(vmem_limit_bytes=48 * 1024 * 1024),
        cost_estimate=pl.CostEstimate(
            flops=6 * rows * d_model * ff,
            bytes_accessed=2 * (2 * rows * d_model + 3 * (d_model + rows) * ff),
            transcendentals=rows * ff,
        ),
        name="feed_forward",
    )(hidden, grad, weight, rest)


def mlp_placed_kernel(ff, index_ref, *refs):
    mains, rests = refs[:4], refs[4:8]
    pair_ref, down_ref, columns = refs[8:]
    own = mains[0].shape[1] - 2 * ff
    for k in range(4):
        piece = index_ref[0] ^ k
        columns[piece, :, :own] = mains[k][:, :own].astype(f32)
        if rests[k].shape[1] == ff - own:
            columns[piece, :, own:ff] = rests[k][...].astype(f32)
        else:
            for step in range(rests[k].shape[1] // (ff - own)):

                @pl.when(pl.program_id(0) == step)
                def _():
                    at = step * (ff - own)
                    columns[piece, :, own:ff] = rests[k][:, at : at + ff - own].astype(f32)
        columns[piece, :, ff:] = mains[k][:, own:].astype(f32)
    for out, at in ((pair_ref.at[0], ff), (pair_ref.at[1], 2 * ff), (down_ref.at[0], 0)):
        out[...] = jnp.concatenate([columns[p, :, at : at + ff] for p in range(4)], axis=1)


def mlp_placed(mains, rests, index, ff, steps):
    rows, width = mains[0].shape
    block, total = rows // steps, 4 * ff
    if steps == 1:
        rests = [unpacked(rest, ff - (width - 2 * ff)) for rest in rests]
    return pl.pallas_call(
        functools.partial(mlp_placed_kernel, ff),
        grid=(steps,),
        out_shape=[
            jax.ShapeDtypeStruct((2, rows, total), f32),
            jax.ShapeDtypeStruct((1, rows, total), f32),
        ],
        in_specs=[SMEM]
        + [pl.BlockSpec((block, width), lambda i: (i, 0))] * 4
        + [pl.BlockSpec(rests[0].shape, lambda i: (0, 0))] * 4,
        out_specs=[
            pl.BlockSpec((2, block, total), lambda i: (0, i, 0)),
            pl.BlockSpec((1, block, total), lambda i: (0, i, 0)),
        ],
        scratch_shapes=[pltpu.VMEM((4, block, 3 * ff), f32)],
        compiler_params=pltpu.CompilerParams(vmem_limit_bytes=40 * 1024 * 1024),
        cost_estimate=pl.CostEstimate(
            flops=0, bytes_accessed=20 * rows * total, transcendentals=0
        ),
        name="mlp_placed",
    )(index.reshape(1).astype(jnp.int32), *mains, *rests)


def placed_kernel(each, total, counts, index_ref, *refs):
    n_parts = len(refs) - len(counts)
    outs = refs[n_parts:]
    for piece in range(total // each + (total % each > 0)):
        start = min(piece * each, total - each)
        shared = piece * each - start
        for k in range(n_parts):

            @pl.when((index_ref[0] ^ k) == piece)
            def _():
                at = 0
                for out, count in zip(outs, counts):
                    for i in range(count):
                        part = refs[k][:, at + shared : at + each].astype(f32)
                        at += each
                        out[i, :, start + shared : start + each] = part


def placed(parts, index, each, total, counts, steps):
    rows = parts[0].shape[0]
    block = rows // steps
    out_shape = [jax.ShapeDtypeStruct((count, rows, total), f32) for count in counts]
    out_specs = [pl.BlockSpec((count, block, total), lambda i: (0, i, 0)) for count in counts]
    width = parts[0].shape[1]
    return pl.pallas_call(
        functools.partial(placed_kernel, each, total, counts),
        grid=(steps,),
        out_shape=out_shape,
        in_specs=[SMEM] + [pl.BlockSpec((block, width), lambda i: (i, 0))] * len(parts),
        out_specs=out_specs,
        compiler_params=pltpu.CompilerParams(vmem_limit_bytes=40 * 1024 * 1024),
        cost_estimate=pl.CostEstimate(
            flops=0, bytes_accessed=rows * width * len(parts) * 6, transcendentals=0
        ),
        name="placed",
    )(index.reshape(1).astype(jnp.int32), *parts)


def last_placed_kernel(count, place_ref, *refs):
    *parts, _, _, first_ref, second_ref = refs
    for i in range(count):
        first_ref[i] = parts[i][...].astype(f32)
    second_ref[0] = parts[count][...].astype(f32)


def last_placed(part, index, each, total, first, second):
    rows, count = part.shape[0], first.shape[0]
    tiles, last = each // 128, total // 128 - 1

    def source(i):
        shift = tiles * (last // tiles + 1) - 1 - last
        return lambda j, ref: (
            0,
            i * tiles + jnp.where(ref[0] == last // tiles, jnp.minimum(j + shift, tiles - 1), j),
        )

    def target(j, ref):
        return (0, 0, jnp.minimum(ref[0] * tiles + j, last))

    out_specs = [pl.BlockSpec((n, rows, 128), target) for n in (count, 1)]
    return pl.pallas_call(
        functools.partial(last_placed_kernel, count),
        grid_spec=pltpu.PrefetchScalarGridSpec(
            num_scalar_prefetch=1,
            grid=(tiles,),
            in_specs=[pl.BlockSpec((rows, 128), source(i)) for i in range(count + 1)]
            + [pl.BlockSpec(memory_space=pl.ANY)] * 2,
            out_specs=out_specs,
        ),
        out_shape=[jax.ShapeDtypeStruct(first.shape, f32), jax.ShapeDtypeStruct(second.shape, f32)],
        input_output_aliases={count + 2: 0, count + 3: 1},
        name="last_placed",
    )(index.reshape(1).astype(jnp.int32), *[part] * (count + 1), first, second)


def at_home_kernel(undo_ref, *refs):
    *blocks, first_ref, second_ref, rows = refs
    each = blocks[0].shape[0]
    for k, block in enumerate(blocks):
        rows[k * each : (k + 1) * each, :] = block[...]
    d_model = first_ref.shape[2]
    for batch in range(first_ref.shape[0]):
        undo = undo_ref[batch * first_ref.shape[1] : (batch + 1) * first_ref.shape[1], :]
        first_ref[batch] = product(undo, rows[:, :d_model], NN, bf16)
        second_ref[batch] = product(undo, rows[:, d_model:], NN, bf16)


def at_home(undo, blocks, batches, d_model):
    rows = undo.shape[0]
    out = jax.ShapeDtypeStruct((batches, rows // batches, d_model), bf16)
    return pl.pallas_call(
        at_home_kernel,
        out_shape=(out, out),
        in_specs=[VMEM] * (1 + len(blocks)),
        out_specs=(VMEM, VMEM),
        scratch_shapes=[pltpu.VMEM((rows, 2 * d_model), bf16)],
        compiler_params=pltpu.CompilerParams(vmem_limit_bytes=32 * 1024 * 1024),
        cost_estimate=pl.CostEstimate(flops=0, bytes_accessed=10_000_000, transcendentals=0),
        name="at_home",
    )(undo, *blocks)


VMEM = pl.BlockSpec(memory_space=pltpu.VMEM)
SMEM = pl.BlockSpec(memory_space=pltpu.SMEM)


def attend_forward(lengths, qkv, conv):
    rows, width = qkv.shape[0], HEADS_EACH * HEAD
    return pl.pallas_call(
        attend_forward_kernel,
        out_shape=jax.ShapeDtypeStruct((rows, width), bf16),
        in_specs=[SMEM, VMEM, VMEM],
        out_specs=VMEM,
        scratch_shapes=[pltpu.VMEM((rows // BATCHES, width), bf16)],
        compiler_params=pltpu.CompilerParams(vmem_limit_bytes=32 * 1024 * 1024),
        cost_estimate=pl.CostEstimate(flops=0, bytes_accessed=20_000_000, transcendentals=0),
        name="attend_forward",
    )(lengths, qkv, conv)


def attend_backward(lengths, qkv, grad, conv):
    rows, width = qkv.shape[0], HEADS_EACH * HEAD
    group = rows // BATCHES
    return pl.pallas_call(
        attend_backward_kernel,
        out_shape=(
            jax.ShapeDtypeStruct((rows, 3 * width), bf16),
            jax.ShapeDtypeStruct((CONV, width), f32),
        ),
        in_specs=[SMEM, VMEM, VMEM, VMEM],
        out_specs=(VMEM, VMEM),
        scratch_shapes=[
            pltpu.VMEM((group, width), bf16),
            pltpu.VMEM((group, width), f32),
            pltpu.VMEM((group, width), f32),
        ],
        compiler_params=pltpu.CompilerParams(vmem_limit_bytes=32 * 1024 * 1024),
        cost_estimate=pl.CostEstimate(flops=0, bytes_accessed=50_000_000, transcendentals=0),
        name="attend_backward",
    )(lengths, qkv, grad, conv)


def attn_packed_kernel(tile_ref, in_ref, out_ref, packed_ref):
    count = in_ref.shape[0]
    tiles = packed_ref.shape[1] // (count + 1) // 128
    for step in range(tiles):

        @pl.when(pl.program_id(0) == step)
        def _():
            for i in range(count):
                at = (i * tiles + step) * 128
                packed_ref[:, at : at + 128] = in_ref[i]
            at = (count * tiles + step) * 128
            packed_ref[:, at : at + 128] = out_ref[...]


def attn_packed(first, attn_in, attn_out, width):
    count, rows, _ = attn_in.shape
    return pl.pallas_call(
        attn_packed_kernel,
        grid_spec=pltpu.PrefetchScalarGridSpec(
            num_scalar_prefetch=1,
            grid=(width // 128,),
            in_specs=[
                pl.BlockSpec((count, rows, 128), lambda j, ref: (0, 0, ref[0] + j)),
                pl.BlockSpec((rows, 128), lambda j, ref: (0, ref[0] + j)),
            ],
            out_specs=pl.BlockSpec((rows, (count + 1) * width), lambda j, ref: (0, 0)),
        ),
        out_shape=jax.ShapeDtypeStruct((rows, (count + 1) * width), bf16),
        name="attn_packed",
    )(first.reshape(1).astype(jnp.int32), attn_in, attn_out)


def part_of(total, each, index):
    start = jnp.minimum(index * each, total - each)
    return start, index * each - start


def per_device(
    tokens,
    cotangent,
    attn_in,
    attn_out,
    gate_up,
    down_proj,
    conv_weight,
    norm_gains,
    deal_order,
    lengths,
):
    sizes = tuple(lax.axis_size(axis) for axis in ("fsdp", "ctx", "tp"))
    n_fsdp, n_ctx, n_tp = sizes
    workers = n_fsdp * n_ctx
    f, c, t = (lax.axis_index(axis) for axis in ("fsdp", "ctx", "tp"))
    me = f * n_ctx + c
    tok_rows, d_model = tokens.shape[1:]
    d_own = attn_in.shape[1]
    heads_all = attn_in.shape[2]
    width = HEADS_EACH * HEAD
    ff_all = gate_up.shape[2]
    ff = ff_all // n_ctx
    from_each = tok_rows // n_fsdp
    half = from_each // n_tp
    group = n_ctx * tok_rows
    plane = BATCHES * group

    start, shared = part_of(heads_all, width, c)
    attn_own = attn_packed(start // 128, attn_in, attn_out.T, width)
    own_down = 3 * ff // 128 * 128 - 2 * ff
    sliced = lax.dynamic_slice_in_dim(gate_up, c * ff, ff, 2)
    down_own = lax.dynamic_slice_in_dim(down_proj, c * ff, ff, 0).T
    mlp_own = jnp.concatenate([down_own[:, :own_down], sliced[0], sliced[1]], axis=1)
    rest_own = down_own[:, own_down:]
    rest_width = ff - own_down
    attn_w = lax.all_gather(attn_own, "fsdp", axis=0, tiled=True)
    mlp_w = lax.all_gather(after(mlp_own, attn_own), "fsdp", axis=0, tiled=True)
    down_w, pair_w = mlp_w[:, :own_down], mlp_w[:, own_down // 128 * 128 :]
    qkv_w, out_w = attn_w[:, : 3 * width], attn_w[:, 3 * width :]

    small = jnp.concatenate(
        [
            deal_order.reshape(-1).astype(f32),
            norm_gains.reshape(-1).astype(f32),
            conv_weight.reshape(-1).astype(f32),
        ]
    )
    small = after(small, attn_own)
    small = lax.all_to_all(
        jnp.broadcast_to(small[None], (workers,) + small.shape),
        ("fsdp", "ctx"),
        split_axis=0,
        concat_axis=0,
        tiled=True,
    )
    n_order, n_gain = deal_order.size, norm_gains.size
    orders = small[:, :n_order].astype(jnp.int32).reshape(workers, BATCHES, tok_rows)
    by_fsdp = small.reshape(n_fsdp, n_ctx, -1)[:, 0]
    gains = by_fsdp[:, n_order : n_order + n_gain].reshape(n_fsdp, 2, -1)
    gains = jnp.transpose(gains, (1, 0, 2)).reshape(2, 1, d_model)
    conv = by_fsdp[:, n_order + n_gain :].reshape(n_fsdp, CONV, -1)
    conv = jnp.transpose(conv, (1, 0, 2)).reshape(CONV, heads_all)
    conv = lax.dynamic_slice_in_dim(conv, start, width, 1)

    given = me * tok_rows + jnp.arange(tok_rows, dtype=jnp.int32)
    by_batch = jnp.transpose(orders, (1, 0, 2)).reshape(BATCHES, -1)
    planes = jnp.arange(workers * tok_rows, dtype=jnp.int32) // group
    to_plane = jnp.sum(
        jnp.where(by_batch[:, None, :] == given[None, :, None], planes[None, None, :], 0), axis=2
    )
    earlier = jnp.arange(tok_rows)[None, :] < jnp.arange(tok_rows)[:, None]
    slot = jnp.sum(
        ((to_plane[:, None, :] == to_plane[:, :, None]) & earlier[None]).astype(jnp.int32), axis=2
    )
    place = ((slot // half) * n_fsdp + (to_plane - f) % n_fsdp) * (BATCHES * half) + slot % half
    place = place + jnp.arange(BATCHES, dtype=jnp.int32)[:, None] * half
    place = place.reshape(-1)
    sent_rows = BATCHES * tok_rows // n_tp
    wire = t * sent_rows + jnp.arange(sent_rows, dtype=jnp.int32)
    choose = (place[None, :] == wire[:, None]).astype(bf16)
    both = jnp.concatenate([wire, (1 - t) * sent_rows + jnp.arange(sent_rows, dtype=jnp.int32)])
    undo = (place[:, None] == both[None, :]).astype(bf16)

    def to_planes(rows):
        picked = product(choose, rows.reshape(-1, d_model), NN, bf16)
        return z_exchange(jnp.split(picked, n_fsdp), sizes)

    def to_home(rows):
        blocks = jnp.split(rows, n_fsdp)
        return [blocks[0]] + [z_shifted(blocks[k], sizes, n_fsdp - k) for k in range(1, n_fsdp)]

    own_x = to_planes(tokens).astype(f32)

    dealt = lax.dynamic_slice_in_dim(orders, f * n_ctx, n_ctx, 0)
    dealt = jnp.transpose(dealt, (1, 0, 2)).reshape(BATCHES, group)
    giver = dealt // tok_rows
    rank = jnp.sum(
        (
            (giver[:, None, :] == giver[:, :, None]) & (dealt[:, None, :] < dealt[:, :, None])
        ).astype(jnp.int32),
        axis=2,
    )
    core = rank // half
    away = (giver % n_ctx) ^ c
    swapped = jnp.where(core == 0, away, (away % 2) * 2 + away // 2)
    block = jnp.where(core == t, 0, n_ctx) + swapped
    arrival = block * (plane // (n_ctx * n_tp)) + (f - giver // n_ctx) % n_fsdp * (BATCHES * half)
    arrival = arrival + jnp.arange(BATCHES, dtype=jnp.int32)[:, None] * half + rank % half
    deal = (arrival.reshape(-1)[:, None] == jnp.arange(plane, dtype=jnp.int32)[None, :]).astype(bf16)

    first_scale = lax.rsqrt(jnp.mean(own_x * own_x, axis=-1, keepdims=True) + epsilon)
    hidden = plane_gather((own_x * first_scale * gains[0]).astype(bf16), sizes)
    own_lengths = lengths[:, 0]
    hidden, given_g, rest_own = stage(hidden, cotangent, packed(rest_own))
    own_g = to_planes(given_g)
    if n_fsdp > 4:
        rests = lax.all_gather(rest_own, "fsdp")
        rest_w = jnp.concatenate([unpacked(rests[k], rest_width) for k in range(n_fsdp)])
    else:
        rest_w = jnp.zeros((d_model, rest_width), bf16)
        for k in range(n_fsdp):
            part = unpacked(z_shifted(rest_own, sizes, k) if k else rest_own, rest_width)
            rest_w = lax.dynamic_update_slice_in_dim(rest_w, part, (f - k) % n_fsdp * d_own, 0)
    qkv = product(deal, product(hidden, qkv_w, NN, bf16), NN, bf16)
    counted = jnp.arange(width)[None, :] >= shared
    attended = attend_forward(own_lengths, qkv, conv)
    attended, own_g = stage(attended, own_g)
    grad_dealt = plane_gather(own_g, sizes)
    attended = jnp.where(counted, product(deal, attended, TN, bf16), jnp.zeros((), bf16))
    kept = plane // 2
    branch = plane_scatter(
        product(attended[:kept], out_w, NT),
        product(attended[kept:], out_w, NT, bf16),
        sizes,
    )
    resid = own_x + branch

    second_scale = lax.rsqrt(jnp.mean(resid * resid, axis=-1, keepdims=True) + epsilon)
    hidden_two = plane_gather((resid * second_scale * gains[1]).astype(bf16), sizes)
    rest_tile = jnp.pad(rest_w, ((0, 0), (own_down % 128, 128 - own_down % 128 - rest_width)))
    hidden_two_turned, grad_dealt_turned, rest_tile = after(
        (hidden_two.T, grad_dealt.T, rest_tile)
    )
    inner, grad_pair = feed_forward(
        after(hidden_two, hidden_two_turned, grad_dealt_turned), grad_dealt, mlp_w, rest_tile, ff
    )
    grad_mlp_w, grad_rest_w = mlp_grad(
        hidden_two_turned, grad_dealt_turned, grad_pair, inner, mlp_w.shape[1], own_down % 128
    )
    grad_mlp_w, grad_rest_w, grad_pair, inner = stage(grad_mlp_w, grad_rest_w, grad_pair, inner)
    grad_mlp = lax.psum_scatter(grad_mlp_w, "fsdp", scatter_dimension=0, tiled=True)
    grad_rest_w = grad_rest_w[:, own_down % 128 :][:, :rest_width]
    rests = [
        packed(lax.dynamic_slice_in_dim(grad_rest_w, (f + k) % n_fsdp * d_own, d_own, 0))
        for k in range(n_fsdp)
    ]

    sent = product(grad_pair[kept:], pair_w, NT, bf16)
    sent, grad_pair = stage(sent, grad_pair)

    got = flipped(sent, sizes, 2)
    part = product(grad_pair[:kept], pair_w, NT)
    got, part = stage(got, part)
    part, sent = added(part, got)
    part, sent, inner = stage(part, sent, inner)

    got = flipped(sent, sizes, 1)
    lift = product(inner[:, :own_down], down_w, NT) + product(inner[:, own_down:ff], rest_w, NT)
    lift, lift_sent = lift[:kept], lift[kept:].astype(bf16)
    got, part, lift_sent, lift = stage(got, part, lift_sent, lift)
    part, sent = added(part, got)
    part, sent, lift_sent, lift = stage(part, sent, lift_sent, lift)

    got = flipped(sent, sizes, 0)
    lift_got = flipped(lift_sent, sizes, 2)
    grad_two = part + got.astype(f32)
    normed = resid * second_scale
    scaled = grad_two * gains[1]
    grad_resid = own_g.astype(f32) + second_scale * (
        scaled - normed * jnp.mean(scaled * normed, axis=-1, keepdims=True)
    )
    grad_own = grad_resid.astype(bf16)
    grad_own, lift, lift_got = stage(grad_own, lift, lift_got)

    near = near_shares(grad_own, sizes)
    lift, lift_sent = added(lift, lift_got)
    grad_own, near, lift, lift_sent = stage(grad_own, near, lift, lift_sent)
    grad_branch = plane_gather(grad_own, sizes, near)
    grad_branch, lift_sent = stage(grad_branch, lift_sent)

    lift_got = flipped(lift_sent, sizes, 1)
    grad_attended = product(deal, product(grad_branch, out_w, NN, bf16), NN, bf16)
    grad_attended = jnp.where(counted, grad_attended, jnp.zeros((), bf16))
    grad_proj, grad_conv = attend_backward(own_lengths, qkv, grad_attended, conv)
    lift_got, lift, grad_proj = stage(lift_got, lift, grad_proj)

    grad_proj = product(deal, grad_proj, TN, bf16)
    sent = product(grad_proj[kept:], qkv_w, NT, bf16)
    lift_got, lift, grad_proj, sent = stage(lift_got, lift, grad_proj, sent)

    got = flipped(sent, sizes, 2)
    part = product(grad_proj[:kept], qkv_w, NT)
    lift, lift_sent = added(lift, lift_got)
    got, part, lift, lift_sent = stage(got, part, lift, lift_sent)
    lift_got = flipped(lift_sent, sizes, 0)
    part, sent = added(part, got)
    part, sent, grad_proj = stage(part, sent, grad_proj)

    got = flipped(sent, sizes, 1)
    grad_attn_w = weight_grad((hidden, grad_proj), (grad_branch, attended))
    got, part, grad_attn_w, lift_got = stage(got, part, grad_attn_w, lift_got)
    result = (resid + (lift + lift_got.astype(f32))).astype(bf16)
    grad_attn = lax.psum_scatter(grad_attn_w, "fsdp", scatter_dimension=0, tiled=True)
    part, sent = added(part, got)

    taps = jnp.concatenate(jnp.split(grad_conv, width // 128, axis=1)).astype(bf16)
    grad_mlp, sent, taps, *rests = stage(grad_mlp, sent, taps, *rests)
    got_last = flipped(sent, sizes, 0)
    mlp_near = near_shares(grad_mlp, sizes)
    little = [jnp.concatenate([rest, taps]) for rest in rests]
    little = sum(
        [z_shifted(little[k], sizes, k).astype(f32) for k in range(1, n_fsdp)], little[0].astype(f32)
    ).astype(bf16)
    mlp_near, got_last, little = stage(mlp_near, got_last, little)

    grad_hidden = part + got_last.astype(f32)
    normed = own_x * first_scale
    scaled = grad_hidden * gains[0]
    grad_x = grad_resid + first_scale * (
        scaled - normed * jnp.mean(scaled * normed, axis=-1, keepdims=True)
    )
    grad_x = grad_x.astype(bf16)

    steps = 128 // rest_width if d_own * rest_width % (128 * 16) == 0 else 1

    def gain_part(own, grad, each, skipped):
        columns = own.shape[1]
        counted = (jnp.arange(columns) % each) >= skipped
        terms = own.astype(f32) * grad[:, :columns].astype(f32)
        return jnp.sum(jnp.where(counted[None, :], terms, 0.0), axis=1)

    mlp_shares = ctx_shares(grad_mlp, sizes, t, mlp_near)
    little_shares = ctx_shares(little, sizes, t)
    rest_rows = d_own * rest_width // 128
    rest_shares = [share[:rest_rows] for share in little_shares]
    taps = [share[rest_rows:].astype(f32) for share in little_shares]
    taps = [jnp.concatenate(jnp.split(tap, width // 128), axis=1) for tap in taps]
    first_shared = n_ctx * width - heads_all
    taps = jnp.stack(taps)
    taps = [lax.dynamic_index_in_dim(taps, c ^ k, 0, False) for k in range(n_ctx)]
    taps = jnp.concatenate(taps[:-1] + [taps[-1][:, first_shared:]], axis=1)
    grad_conv = lax.dynamic_slice_in_dim(taps, f * (heads_all // n_fsdp), heads_all // n_fsdp, 1)
    gain_two = gain_part(mlp_own[:, own_down:], grad_mlp[:, own_down:], ff, 0)
    rows_back = jnp.concatenate([result, grad_x], axis=1)
    grad_attn, rows_back, gain_two, grad_conv, rest_shares = stage(
        grad_attn, rows_back, gain_two, grad_conv, rest_shares
    )

    near = near_shares(grad_attn, sizes)
    home = to_home(rows_back)
    gain_one = gain_part(attn_own[:, : 3 * width], grad_attn, width, shared)
    gains_grad = jnp.stack([gain_one, gain_two])
    gains_grad = gains_grad + flipped(gains_grad, sizes, 2)
    grad_gate_up, grad_down = mlp_placed(mlp_shares, rest_shares, c, ff, steps)
    near, gains_grad, grad_gate_up, grad_down = stage(near, gains_grad, grad_gate_up, grad_down)

    attn_shares = ctx_shares(grad_attn, sizes, t, near)
    grad_attn_in, grad_attn_out = placed(attn_shares[:3], c, width, heads_all, (3, 1), steps)
    for step in (0, 1):
        gains_grad = gains_grad + flipped(gains_grad, sizes, step)
    activations, input_grad = at_home(
        undo, home + [flipped(block, sizes, 2) for block in home], BATCHES, d_model
    )
    grad_gains = gains_grad / norm_gains.astype(f32)
    grad_attn_in, grad_attn_out = last_placed(
        attn_shares[3], c ^ 3, width, heads_all, grad_attn_in, grad_attn_out
    )
    return (
        activations,
        input_grad,
        grad_attn_in,
        grad_attn_out[0].T,
        grad_gate_up,
        grad_down[0].T,
        grad_conv[None],
        grad_gains,
    )


def solution(mesh):
    return jax.shard_map(
        per_device,
        mesh=mesh,
        in_specs=(
            P(None, ("fsdp", "ctx"), None),
            P(None, ("fsdp", "ctx"), None),
            P(None, "fsdp", "tp"),
            P("tp", "fsdp"),
            P(None, "fsdp", "tp"),
            P("tp", "fsdp"),
            P("tp", None, "fsdp"),
            P(None, "fsdp"),
            P(None, ("fsdp", "ctx")),
            P(None, "fsdp", None),
        ),
        out_specs=(
            P(None, ("fsdp", "ctx"), None),
            P(None, ("fsdp", "ctx"), None),
            P(None, "fsdp", "tp"),
            P("tp", "fsdp"),
            P(None, "fsdp", "tp"),
            P("tp", "fsdp"),
            P("tp", None, "fsdp"),
            P(None, "fsdp"),
        ),
        check_vma=False,
    )
```
